256 devices in a mesh: owner: 64 (over x, z, core), group: 4 (over y).
Axes of the slice: x: 4, y: 4, z: 8, core: 2. Of those that a mesh axis runs over, the one named last changes fastest.
Arguments:
- table: float32 [524288, 128], P(('owner', 'group')), may hold values from -0.6 to 0.6
- accum: float32 [524288], P(('owner', 'group')), may hold values from 0.0001 to 0.01
- requests: int32 [3, 64, 4, 64, 4], P(None, 'owner', 'group'), may hold values from 0 to 2047
- members: int32 [3, 32768, 26, 4], P(None, ('owner', 'group')), may hold values from 0 to 255
- labels: int32 [3, 32768], P(None, ('owner', 'group')), may hold values from 0 to 1
- down_proj: bfloat16 [3328, 256], replicated, may hold values from -0.109375 to 0.109375
- up_proj: bfloat16 [256, 3328], replicated, may hold values from -0.375 to 0.375
- cross_bias: float32 [3328], replicated, may hold values from -3 to 3
- out_weight: bfloat16 [3328], replicated, may hold values from -0.109375 to 0.109375
Outputs:
- table_new: float32 [524288, 128], P(('owner', 'group'))
- accum_new: float32 [524288], P(('owner', 'group'))
- grad_down: float32 [3328, 256], P(('owner', 'group'))
- grad_up: float32 [256, 3328], P(None, ('owner', 'group'))
- grad_bias: float32 [3328], P(('owner', 'group'))
- grad_out: float32 [3328], P(('owner', 'group'))
The draws below stay inside these ranges and needn't reach their ends.
All inputs are finite; a program needn't handle non-finite values.
Results may differ from the reference program's by a relative error of at most 0.008.
Values may be sent and summed in bfloat16 or wider, within the bound.
A program may use at most 128 MiB of HBM per device.

```python
import math
import jax
import jax.numpy as jnp
from jax import lax

E = 128
NB = 26
RANK = 256
BAGLEN = 4
STEPS = 3
ROWS_DEV = 2048
SLOTS = 4
TOK_DEV = 128
D_IN = 3328
FETCH = 256
TOKENS = 32768
TABLE_ROWS = 524288
N_OWNER = 64
N_GROUP = 4


def with_ends(values, rng, low, high):
    dims = values.shape
    spot = [jax.random.randint(jax.random.fold_in(rng, axis), (), 0, dims[axis]) for axis in range(len(dims))]
    values = values.at[tuple(spot)].set(low)
    longest = dims.index(max(dims))
    spot[longest] = (spot[longest] + 1) % dims[longest]
    return values.at[tuple(spot)].set(high)


def shard_levels(stream_key, dims, split, low, high):
    def one(dim, shards_of):
        steps = jax.random.uniform(jax.random.fold_in(jax.random.fold_in(stream_key, 6), dim), (shards_of,), jnp.float32, low / len(split), high / len(split))
        return jnp.repeat(jnp.exp(steps), dims[dim] // shards_of).reshape((-1,) + (1,) * (len(dims) - dim - 1))

    level = one(*split[0])
    for cut in split[1:]:
        level = level * one(*cut)
    return level


def gaussian(own_key, extent, width, reach, pieces=(), kind=jnp.bfloat16):
    entries = jax.random.normal(own_key, extent, jnp.float32) * width
    if len(pieces) > 0:
        entries = shard_levels(own_key, extent, pieces, -0.22, 0.18) * entries
    return jnp.clip(entries, min=-reach, max=reach).astype(kind)


def setup_inputs(seed: int = 0) -> dict:
    splits = jax.random.split(jax.random.key(seed), 10)
    return {
        "table": gaussian(splits[0], (TABLE_ROWS, E), 0.1, 0.6, ((0, 256),), jnp.float32),
        "accum": jnp.clip(jnp.exp(math.log(0.01) - 4.6051702 * jax.random.uniform(splits[1], (TABLE_ROWS,), jnp.float32) ** shard_levels(splits[1], (TABLE_ROWS,), ((0, 256),), -0.2, 0.2)), 0.0001, 0.01),
        "requests": with_ends(jax.random.randint(splits[2], (STEPS, N_OWNER, N_GROUP, N_OWNER, SLOTS), 0, ROWS_DEV), jax.random.fold_in(splits[2], 1), 0, ROWS_DEV - 1).astype(jnp.int32),
        "members": with_ends(jax.random.randint(splits[3], (STEPS, TOKENS, NB, BAGLEN), 0, FETCH), jax.random.fold_in(splits[3], 1), 0, FETCH - 1).astype(jnp.int32),
        "labels": with_ends(jax.random.randint(splits[4], (STEPS, TOKENS), 0, 2), jax.random.fold_in(splits[4], 1), 0, 1).astype(jnp.int32),
        "down_proj": gaussian(splits[5], (D_IN, RANK), D_IN ** -0.5, 0.109375),
        "up_proj": gaussian(splits[6], (RANK, D_IN), RANK ** -0.5, 0.375),
        "cross_bias": gaussian(splits[7], (D_IN,), 0.5, 3.0, (), jnp.float32),
        "out_weight": gaussian(splits[8], (D_IN,), D_IN ** -0.5, 0.109375),
    }


learn_rate = 0.05

def reference(table, accum, requests, members, labels, down_proj, up_proj, cross_bias, out_weight):
    devices = N_OWNER * N_GROUP
    tokens = TOK_DEV * devices
    dst = jnp.arange(N_OWNER, dtype=jnp.int32)[None, None, :, None]
    grp = jnp.arange(N_GROUP, dtype=jnp.int32)[None, :, None, None]
    grad_down = jnp.zeros((D_IN, RANK), jnp.float32)
    grad_up = jnp.zeros((RANK, D_IN), jnp.float32)
    grad_bias = jnp.zeros((D_IN,), jnp.float32)
    grad_out = jnp.zeros((D_IN,), jnp.float32)
    for step in range(STEPS):
        tab4 = table.reshape(N_OWNER, N_GROUP, ROWS_DEV, E)
        req = requests[step]
        fetched = tab4[dst, grp, req].astype(jnp.bfloat16).reshape(devices, FETCH, E)
        mem = members[step].reshape(devices, TOK_DEV, NB, BAGLEN)

        def pool_one(pair):
            rows, idx = pair
            return lax.optimization_barrier(jnp.sum(rows[idx].astype(jnp.float32), axis=2))
        pooled = lax.map(pool_one, (fetched, mem))
        x0 = pooled.reshape(tokens, D_IN).astype(jnp.bfloat16)
        low = jnp.dot(x0, down_proj, preferred_element_type=jnp.float32).astype(jnp.bfloat16)
        gate = jnp.dot(low, up_proj, preferred_element_type=jnp.float32) + cross_bias
        x0f = x0.astype(jnp.float32)
        x1 = (x0f * gate + x0f).astype(jnp.bfloat16)
        logit = jnp.dot(x1, out_weight, preferred_element_type=jnp.float32)
        dlogit = jax.nn.sigmoid(logit) - labels[step].astype(jnp.float32)
        dx1 = dlogit[:, None] * out_weight.astype(jnp.float32)[None, :]
        dgate = (dx1 * x0f).astype(jnp.bfloat16)
        dlow = jnp.dot(dgate, up_proj.T, preferred_element_type=jnp.float32).astype(jnp.bfloat16)
        dx0 = dx1 * (gate + 1.0) + jnp.dot(dlow, down_proj.T, preferred_element_type=jnp.float32)
        dpooled = dx0.astype(jnp.bfloat16).reshape(devices, TOK_DEV * NB, E)

        def spread_one(pair):
            grads, idx = pair
            idx = idx.reshape(TOK_DEV * NB, BAGLEN)
            total = jnp.zeros((FETCH, E), jnp.float32)
            for member in range(BAGLEN):
                total = total + jax.ops.segment_sum(grads.astype(jnp.float32), idx[:, member], FETCH)
            return total
        gfetch = lax.map(spread_one, (dpooled, mem))
        ids = ((dst * N_GROUP + grp) * ROWS_DEV + req).astype(jnp.int32)
        row_grad = jax.ops.segment_sum(gfetch.reshape(-1, E), ids.reshape(-1), TABLE_ROWS)
        accum = accum + lax.optimization_barrier(jnp.mean(row_grad * row_grad, axis=1))
        table = table - learn_rate * row_grad / jnp.sqrt(accum)[:, None]
        grad_down = grad_down + jnp.dot(x0.T, dlow, preferred_element_type=jnp.float32)
        grad_up = grad_up + jnp.dot(low.T, dgate, preferred_element_type=jnp.float32)
        grad_bias = grad_bias + lax.optimization_barrier(jnp.sum(dgate.astype(jnp.float32), axis=0))
        grad_out = grad_out + lax.optimization_barrier(jnp.sum(x1.astype(jnp.float32) * dlogit[:, None], axis=0))
    scale = 1.0 / (STEPS * tokens)
    return (table, accum, grad_down * scale, grad_up * scale, grad_bias * scale, grad_out * scale)
```

```python
import functools

import jax
import jax.numpy as jnp
from jax import lax
from jax.experimental import pallas as pl
from jax.experimental.pallas import tpu as pltpu
from jax.sharding import PartitionSpec as P

NX, NY, NZ, NC = 4, 4, 8, 2
NXC = NX * NC
NB = 26
BAGLEN = 4
STEPS = 3
E = 128
TOK = 128
RANK = 256
D_IN = NB * E
ROWS = 2048
SLOTS = 4
FETCH = NZ * NXC * SLOTS
SLAB = 32
CH = 256
NCH = D_IN // CH
XROWS = D_IN // NX
HALF = XROWS // NC
PART = HALF // 2
BLOCK = XROWS // NZ
SHARE = 13
WIN = 24

learn_rate = 0.05
F32 = jnp.float32
BF16 = jnp.bfloat16


def nn(a, b):
    return jnp.dot(a, b, preferred_element_type=F32)


def nt(a, b):
    return lax.dot_general(a, b, (((1,), (1,)), ((), ())), preferred_element_type=F32)


def iota(shape, dim):
    return lax.broadcasted_iota(jnp.int32, shape, dim)


def onehot(mask):
    return jnp.where(mask, 1.0, 0.0).astype(BF16)


def al(value, step):
    return pl.multiple_of(value, step)


def remote(src, dst, send, recv, dev):
    copy = pltpu.make_async_remote_copy(
        src_ref=src, dst_ref=dst, send_sem=send, recv_sem=recv,
        device_id=dev, device_id_type=pl.DeviceIdType.MESH,
    )
    copy.start()
    return copy


def wait_all(copies):
    for copy in copies:
        copy.wait()


def kernel(
    table_in, accum_in, reqs, mem, labels, down, up, bias, outw,
    table, accum_out, gdu_out, bo_out,
    rq, wcol, wrow, s1, r1, s2, r2, g0, g1, g2, g3,
    down_t, up_t, bias_b, out_b, acc_b, posq,
    counts, x0s, dgs, lows, dlows, gates, x1s, bo3,
    gs, rc, ss, rx1, ry1, rx2, ry2, aa, bb, ff, rz, tt, fw,
    bo, boc, box, boy, boz,
    q1s, q1r, q2s, q2r, f1s, f1r, f2s, f2r, b1s, b1r, b2s, b2r,
    cs, cr, xs, xr, ys, yr, x2s, x2r, y2s, y2r, zs, zr, fs, fr,
    bcs, bcr, bxs, bxr, bys, byr, bzs, bzr,
):
    owner = lax.axis_index("owner")
    y = lax.axis_index("group")
    c = owner % NC
    z = (owner // NC) % NZ
    x = owner // (NC * NZ)
    xc = x * NC + c

    def dev(px, pz, pc, py):
        return ((px * NZ + pz) * NC + pc, py)

    def zpeer(k):
        pz = (z + k) % NZ
        return pz, dev(x, pz, c, y)

    def xcpeer(k):
        pxc = (xc + k) % NXC
        return pxc, dev(pxc // NC, z, pxc % NC, y)

    def xpeer(k):
        px = (x + k) % NX
        return px, dev(px, z, c, y)

    def ypeer(k):
        py = (y + k) % NY
        return py, dev(x, z, c, py)

    partner = dev(x, z, 1 - c, y)

    barrier = pltpu.get_barrier_semaphore()
    greet = [zpeer(k)[1] for k in range(1, NZ)] + [xcpeer(k)[1] for k in range(1, NXC)]
    greet += [ypeer(k)[1] for k in range(1, NY)]
    greet += [dev(x, z, 1 - c, (y + k) % NY) for k in range(1, NY)]
    for peer in greet:
        pl.semaphore_signal(barrier, inc=1, device_id=peer, device_id_type=pl.DeviceIdType.MESH)
    pl.semaphore_wait(barrier, len(greet))

    rq[xc, z] = reqs[...]
    copies = []
    for k in range(1, NZ):
        copies.append(remote(rq.at[xc, z], rq.at[xc, z], q1s.at[k], q1r.at[k], zpeer(k)[1]))

    eye = onehot(iota((CH, CH), 0) == iota((CH, CH), 1))

    def weights(i, carry):
        at = al(i * CH, CH)
        down_t[:, pl.ds(at, CH)] = nt(eye, down[pl.ds(at, CH), :]).astype(BF16)
        up_t[pl.ds(at, CH), :] = nt(eye, up[:, pl.ds(at, CH)]).astype(BF16)
        return carry

    wait_all(copies)
    copies = []
    for k in range(1, NXC):
        copies.append(remote(rq.at[xc], rq.at[xc], q2s.at[k], q2r.at[k], xcpeer(k)[1]))
    lax.fori_loop(0, NCH, weights, 0)

    def columns(i, carry):
        at = al(i * E, E)
        bias_b[pl.ds(at, E), :] = jnp.broadcast_to(bias[pl.ds(i, 1), :], (E, E)).T
        out_b[pl.ds(at, E), :] = jnp.broadcast_to(outw[pl.ds(i, 1), :], (E, E)).T
        return carry

    lax.fori_loop(0, NB, columns, 0)

    def acc_columns(i, carry):
        at = al(i * E, E)
        acc_b[pl.ds(at, E), :] = jnp.broadcast_to(accum_in[pl.ds(i, 1), :], (E, E)).T
        return carry

    lax.fori_loop(0, ROWS // E, acc_columns, 0)
    table[...] = table_in[...]
    bo3[...] = jnp.zeros_like(bo3)

    qi = iota((FETCH, E), 0)
    qb = qi // SLOTS
    q_xc = qb // NZ
    q_z = qb % NZ
    posq[...] = (((q_xc // NC) * NZ + q_z) * NC + q_xc % NC) * SLOTS + qi % SLOTS

    pi = iota((FETCH, FETCH), 0)
    pb = pi // SLOTS
    perm = onehot(((pb % 8) * 8 + pb // 8) * SLOTS + pi % SLOTS == iota((FETCH, FETCH), 1))

    wait_all(copies)

    allreq = rq[...].reshape(NXC * NZ * 8, E)
    req_hi = (allreq // 64).astype(F32).astype(BF16)
    req_lo = (allreq % 64).astype(F32).astype(BF16)
    si = iota((FETCH, NXC * NZ * 8), 0)
    sb = si // SLOTS
    s_z = sb // NXC
    s_xc = sb % NXC
    s_row = (s_xc * NZ + s_z) * 8 + (si % SLOTS) // 2
    s_col = iota((FETCH, NXC * NZ * 8), 1)
    li = iota((FETCH, E), 0) % SLOTS
    lane_mask = iota((FETCH, E), 1) == (li % 2) * 64 + owner
    ones8 = jnp.ones((16, E), BF16)
    for t in range(STEPS):
        sel = onehot(s_row + 2 * t == s_col)
        hi = jnp.where(lane_mask, nn(sel, req_hi), 0.0)
        lo = jnp.where(lane_mask, nn(sel, req_lo), 0.0)
        col = jnp.sum(hi * 64.0 + lo, axis=1, keepdims=True)
        wcol[t] = jnp.broadcast_to(col, (FETCH, E)).astype(jnp.int32)
        row = nt(ones8, hi.astype(BF16)) * 64.0 + nt(ones8, lo.astype(BF16))
        wrow[t] = row[0:8].astype(jnp.int32)

    eye_e = onehot(iota((E, E), 0) == iota((E, E), 1))

    def step(t, carry):
        def gather(j, rows):
            at = al(j * CH, CH)
            want = wcol[t]
            lanes = iota((FETCH, E), 1) + j * CH
            r = jnp.concatenate([onehot(want == lanes), onehot(want == lanes + E)], axis=1)
            return rows + nn(r, table[pl.ds(at, CH), :].astype(BF16))

        s1[t] = lax.fori_loop(0, ROWS // CH, gather, jnp.zeros((FETCH, E), F32)).astype(BF16)

        def exchange(src, dst, n, me, peer, ssem, rsem):
            copies = []
            for k in range(1, n):
                p, d = peer(k)
                copies.append(remote(
                    src.at[t, pl.ds(al(p * SLAB, SLAB), SLAB)],
                    dst.at[t, pl.ds(al(me * SLAB, SLAB), SLAB)],
                    ssem.at[t, k], rsem.at[t, k], d,
                ))
            mine = pl.ds(al(me * SLAB, SLAB), SLAB)
            dst[t, mine] = src[t, mine]
            wait_all(copies)

        exchange(s1, r1, NZ, z, zpeer, f1s, f1r)
        s2[t] = nn(perm, r1[t]).astype(BF16)
        exchange(s2, r2, NXC, xc, xcpeer, f2s, f2r)
        fetched_t = nt(eye_e, r2[t]).astype(BF16)

        def pool(i, low):
            rows = mem[t, pl.ds(al(i * 8, 8), 8), :]
            pos = posq[...]
            cnt = []
            for b in range(2):
                n = jnp.where(pos == rows[4 * b:4 * b + 1, :], 1.0, 0.0)
                for m in range(1, BAGLEN):
                    n = n + jnp.where(pos == rows[4 * b + m:4 * b + m + 1, :], 1.0, 0.0)
                cnt.append(n.astype(BF16))
            both = jnp.concatenate(cnt, axis=1)
            counts[i] = both
            xx = nn(fetched_t, both).astype(BF16)
            xx = jnp.concatenate([xx[:, :TOK], xx[:, TOK:]], axis=0)
            at = al(i * CH, CH)
            x0s[t, pl.ds(at, CH), :] = xx
            return low + nn(down_t[:, pl.ds(at, CH)], xx)

        low = lax.fori_loop(0, NCH, pool, jnp.zeros((RANK, TOK), F32)).astype(BF16)
        lows[t] = low

        def forward(i, logit):
            at = al(i * CH, CH)
            gate = nn(up_t[pl.ds(at, CH), :], low) + bias_b[pl.ds(at, CH), :]
            gates[pl.ds(at, CH), :] = gate
            x0f = x0s[t, pl.ds(at, CH), :].astype(F32)
            x1 = (x0f * gate + x0f).astype(BF16)
            x1s[pl.ds(at, CH), :] = x1
            prod = x1.astype(F32) * out_b[pl.ds(at, CH), :]
            return logit + jnp.sum(prod.reshape(CH // 8, 8, TOK), axis=0)

        logit = lax.fori_loop(0, NCH, forward, jnp.zeros((8, TOK), F32))
        logit = jnp.sum(logit, axis=0, keepdims=True)
        dlogit = jax.nn.sigmoid(logit) - labels[pl.ds(t, 1), :].astype(F32)
        dhi = dlogit.astype(BF16).astype(F32)
        dmid = (dlogit - dhi).astype(BF16).astype(F32)
        dlo = dlogit - dhi - dmid
        sub = iota((16, TOK), 0)
        heads = jnp.where(sub == 0, dhi, jnp.where(sub == 1, dmid, jnp.where(sub == 2, dlo, 1.0)))
        heads = heads.astype(BF16)

        def backward(i, dlow):
            at = al(i * CH, CH)
            x0f = x0s[t, pl.ds(at, CH), :].astype(F32)
            dg = (dlogit * out_b[pl.ds(at, CH), :] * x0f).astype(BF16)
            dgs[t, pl.ds(at, CH), :] = dg
            bo3[0, i] = bo3[0, i] + nt(heads, dg)
            bo3[1, i] = bo3[1, i] + nt(heads, x1s[pl.ds(at, CH), :])
            return dlow + nn(up[:, pl.ds(at, CH)], dg)

        dlow = lax.fori_loop(0, NCH, backward, jnp.zeros((RANK, TOK), F32)).astype(BF16)
        dlows[t] = dlow

        def spread(i, gf):
            at = al(i * CH, CH)
            dx0 = dlogit * out_b[pl.ds(at, CH), :] * (gates[pl.ds(at, CH), :] + 1.0)
            dx0 = (dx0 + nn(down[pl.ds(at, CH), :], dlow)).astype(BF16)
            both = jnp.concatenate([dx0[:E], dx0[E:]], axis=1)
            return gf + nt(counts[i], both)

        g0[t] = lax.fori_loop(0, NCH, spread, jnp.zeros((FETCH, E), F32)).astype(BF16)
        exchange(g0, g1, NXC, xc, xcpeer, b1s, b1r)
        g2[t] = nn(perm, g1[t]).astype(BF16)
        exchange(g2, g3, NZ, z, zpeer, b2s, b2r)

        arrived = g3[t]

        def update(j, carry):
            at = al(j * CH, CH)
            want = wrow[t][0:1, :]
            rt = onehot(iota((CH, FETCH), 0) + j * CH == want)
            rg = nn(rt, arrived)
            acc = acc_b[pl.ds(at, CH), :] + jnp.mean(rg * rg, axis=1, keepdims=True)
            acc_b[pl.ds(at, CH), :] = acc
            table[pl.ds(at, CH), :] = table[pl.ds(at, CH), :] - learn_rate * rg * lax.rsqrt(acc)
            return carry

        lax.fori_loop(0, ROWS // CH, update, 0)
        return carry

    lax.fori_loop(0, STEPS, step, 0)

    def acc_rows(i, carry):
        at = al(i * E, E)
        accum_out[pl.ds(i, 1), :] = acc_b[pl.ds(at, E), :].T[0:1, :]
        return carry

    lax.fori_loop(0, ROWS // E, acc_rows, 0)

    bo[...] = jnp.zeros_like(bo)
    for i in range(NCH):
        b_row = bo3[0, i][3:4, :]
        o_rows = bo3[1, i]
        o_row = o_rows[0:1, :] + o_rows[1:2, :] + o_rows[2:3, :]
        for h in range(2):
            bo[0, 2 * i + h:2 * i + h + 1, :] = b_row[:, h * E:(h + 1) * E]
            bo[0, 32 + 2 * i + h:33 + 2 * i + h, :] = o_row[:, h * E:(h + 1) * E]
    bo_copy = remote(bo.at[0], boc, bcs, bcr, partner)

    dl_all = jnp.concatenate([dlows[t] for t in range(STEPS)], axis=1)
    lo_all = jnp.concatenate([lows[t] for t in range(STEPS)], axis=1)

    def dense(px, half):
        at = al(px * XROWS + half * HALF, 16)
        xx = jnp.concatenate([x0s[t, pl.ds(at, HALF), :] for t in range(STEPS)], axis=1)
        dd = jnp.concatenate([dgs[t, pl.ds(at, HALF), :] for t in range(STEPS)], axis=1)
        return nt(xx, dl_all), nt(dd, lo_all)

    core_copies = []
    for i in range(NX):
        px = (x + 1 + i) % NX
        gd, gu = dense(px, 1 - c)
        gs[i, :, 0:RANK] = gd.astype(BF16)
        gs[i, :, RANK:] = gu.astype(BF16)
        core_copies.append(remote(gs.at[i], rc.at[i], cs.at[i], cr.at[i], partner))

    x_copies, y_copies = [], []
    for i in range(NX):
        px = (x + 1 + i) % NX
        gd, gu = dense(px, c)
        core_copies[i].wait()
        ss[i, :, 0:RANK] = (gd + rc[i, :, 0:RANK].astype(F32)).astype(BF16)
        ss[i, :, RANK:] = (gu + rc[i, :, RANK:].astype(F32)).astype(BF16)
        if i < NX - 1:
            x_copies.append(remote(
                ss.at[i, pl.ds(0, PART)], rx1.at[i], xs.at[i], xr.at[i], xpeer(i + 1)[1]
            ))
        for k in range(1, NY):
            py, d = ypeer(k)
            y_copies.append(remote(
                ss.at[i, pl.ds(PART, PART), pl.ds(al(py * E, E), E)], ry1.at[k - 1, i],
                ys.at[i, k], yr.at[i, k], d,
            ))
    bo_copy.wait()
    bo[1] = bo[0] + boc[...]
    bx_copies = [remote(bo.at[1], box.at[k - 1], bxs.at[k], bxr.at[k], xpeer(k)[1]) for k in range(1, NX)]

    my_y = pl.ds(al(y * E, E), E)
    wait_all(x_copies)
    aa[...] = (
        ss[NX - 1, 0:PART, :].astype(F32) + rx1[0].astype(F32) + rx1[1].astype(F32) + rx1[2].astype(F32)
    ).astype(BF16)
    y2_copies = []
    for k in range(1, NY):
        py, d = ypeer(k)
        y2_copies.append(remote(
            aa.at[:, pl.ds(al(py * E, E), E)], ry2.at[k - 1], y2s.at[k], y2r.at[k], d
        ))
    wait_all(y_copies)
    for i in range(NX):
        bb[i] = (
            ss[i, PART:, my_y].astype(F32)
            + ry1[0, i].astype(F32) + ry1[1, i].astype(F32) + ry1[2, i].astype(F32)
        ).astype(BF16)
    x2_copies = []
    for k in range(1, NX):
        x2_copies.append(remote(bb.at[k - 1], rx2.at[k - 1], x2s.at[k], x2r.at[k], xpeer(k)[1]))
    wait_all(bx_copies)
    bo[2] = bo[1] + box[0] + box[1] + box[2]
    by_copies = [remote(bo.at[2], boy.at[k - 1], bys.at[k], byr.at[k], ypeer(k)[1]) for k in range(1, NY)]

    wait_all(y2_copies)
    ff[0:PART] = (
        aa[:, my_y].astype(F32) + ry2[0].astype(F32) + ry2[1].astype(F32) + ry2[2].astype(F32)
    )
    wait_all(x2_copies)
    ff[PART:] = (
        bb[NX - 1].astype(F32) + rx2[0].astype(F32) + rx2[1].astype(F32) + rx2[2].astype(F32)
    )

    def z_copy(k):
        zt = c * (NZ // NC) + k
        return pltpu.make_async_remote_copy(
            src_ref=ff.at[pl.ds(k * BLOCK, BLOCK)], dst_ref=rz.at[z],
            send_sem=zs.at[k], recv_sem=zr.at[z],
            device_id=dev(x, zt, c, y), device_id_type=pl.DeviceIdType.MESH,
        )

    for k in range(NZ // NC):
        zt = c * (NZ // NC) + k

        @pl.when(zt != z)
        def _():
            z_copy(k).start()

        @pl.when(zt == z)
        def _():
            rz[z] = ff[k * BLOCK:(k + 1) * BLOCK]

    wait_all(by_copies)
    bo[3] = bo[2] + boy[0] + boy[1] + boy[2]
    bz_copies = [remote(bo.at[3], boz.at[k - 1], bzs.at[k], bzr.at[k], zpeer(k)[1]) for k in range(1, NZ)]

    holder = z // (NZ // NC)

    @pl.when(holder == c)
    def _():
        for s in range(NZ):
            @pl.when(s != z)
            def _():
                pltpu.make_async_remote_copy(
                    src_ref=ff.at[pl.ds(0, BLOCK)], dst_ref=rz.at[s],
                    send_sem=zs.at[0], recv_sem=zr.at[s],
                    device_id=partner, device_id_type=pl.DeviceIdType.MESH,
                ).wait_recv()
        total = rz[0]
        for s in range(1, NZ):
            total = total + rz[s]
        tt[...] = total

    def window(pc, py):
        off = pc * (SHARE * NY) + py * SHARE
        first = jnp.minimum((off // 8) * 8, BLOCK - WIN)
        return al(first, 8), off - first

    def f_copy(k, h):
        py = (y + k) % NY
        pc = (c + h) % NC
        return pltpu.make_async_remote_copy(
            src_ref=tt.at[pl.ds(window(pc, py)[0], WIN)], dst_ref=fw.at[y],
            send_sem=fs.at[2 * k + h], recv_sem=fr.at[k],
            device_id=dev(x, z, pc, py), device_id_type=pl.DeviceIdType.MESH,
        )

    first, skip = window(c, y)

    @pl.when(holder == c)
    def _():
        for k in range(NY):
            for h in range(NC):
                if k or h:
                    f_copy(k, h).start()
        fw[y] = tt[pl.ds(first, WIN)]

    @pl.when(holder != c)
    def _():
        f_copy(0, 1).wait_recv()

    for k in range(1, NY):
        f_copy(k, 0).wait_recv()

    scale = 1.0 / (STEPS * TOK * NX * NY * NZ * NC)
    for py in range(NY):
        gdu_out[:, py * E:(py + 1) * E] = (
            pltpu.roll(fw[py], (WIN - skip) % WIN, 0)[0:16, :] * scale
        )

    wait_all(bz_copies)
    total = bo[3]
    for k in range(NZ - 1):
        total = total + boz[k]
    bo[4] = total * scale
    start = (owner * NY + y) * SHARE
    a = start // E
    rows = []
    for base in (0, 32):
        pair = jnp.concatenate([bo[4, pl.ds(base + a, 1), :], bo[4, pl.ds(base + a + 1, 1), :]], axis=1)
        pair = jnp.broadcast_to(pair, (8, 2 * E))
        rows.append(pltpu.roll(pair, (2 * E - start % E) % (2 * E), 1)[:, 0:E])
    bo_out[...] = jnp.where(iota((8, E), 0) == 0, rows[0], rows[1])

    for k in range(NZ // NC):
        @pl.when(c * (NZ // NC) + k != z)
        def _():
            z_copy(k).wait_send()

    @pl.when(holder == c)
    def _():
        for k in range(NY):
            for h in range(NC):
                if k or h:
                    f_copy(k, h).wait_send()


def local(table, accum, requests, members, labels, down_proj, up_proj, cross_bias, out_weight):
    reqs = jnp.transpose(requests[:, 0, 0], (0, 2, 1)).reshape(2 * STEPS, E)
    reqs = jnp.pad(reqs, ((0, 2), (0, 0)))
    mem = jnp.transpose(members, (0, 2, 3, 1)).reshape(STEPS, NB * BAGLEN, TOK)
    dma = pltpu.SemaphoreType.DMA
    vm = pltpu.VMEM
    scratch = [
        vm((NXC, NZ, 8, E), jnp.int32),
        vm((STEPS, FETCH, E), jnp.int32),
        vm((STEPS, 8, FETCH), jnp.int32),
    ]
    scratch += [vm((STEPS, FETCH, E), BF16)] * 8
    scratch += [
        vm((RANK, D_IN), BF16), vm((D_IN, RANK), BF16),
        vm((D_IN, TOK), F32), vm((D_IN, TOK), F32), vm((ROWS, E), F32), vm((FETCH, E), jnp.int32),
        vm((NCH, FETCH, 2 * TOK), BF16),
        vm((STEPS, D_IN, TOK), BF16), vm((STEPS, D_IN, TOK), BF16),
        vm((STEPS, RANK, TOK), BF16), vm((STEPS, RANK, TOK), BF16),
        vm((D_IN, TOK), F32), vm((D_IN, TOK), BF16), vm((2, NCH, 16, CH), F32),
        vm((NX, HALF, 2 * RANK), BF16), vm((NX, HALF, 2 * RANK), BF16), vm((NX, HALF, 2 * RANK), BF16),
        vm((NX - 1, PART, 2 * RANK), BF16), vm((NY - 1, NX, PART, E), BF16),
        vm((NX - 1, PART, E), BF16), vm((NY - 1, PART, E), BF16),
        vm((PART, 2 * RANK), BF16), vm((NX, PART, E), BF16), vm((HALF, E), F32),
        vm((NZ, BLOCK, E), F32), vm((BLOCK, E), F32), vm((NY, WIN, E), F32),
        vm((5, 64, E), F32), vm((64, E), F32), vm((NX - 1, 64, E), F32),
        vm((NY - 1, 64, E), F32), vm((NZ - 1, 64, E), F32),
    ]
    scratch += [dma((8,))] * 4
    scratch += [dma((STEPS, 8))] * 8
    scratch += [dma((NX,))] * 2
    scratch += [dma((NX,))] * 2
    scratch += [dma((NX, NY))] * 2
    scratch += [dma((NX,))] * 4
    scratch += [dma((NZ,))] * 2
    scratch += [dma((8,))] * 2
    scratch += [dma] * 2
    scratch += [dma((8,))] * 6
    spec = pl.BlockSpec(memory_space=pltpu.VMEM)
    table_new, accum_new, gdu, bo = pl.pallas_call(
        kernel,
        out_shape=(
            jax.ShapeDtypeStruct((ROWS, E), F32),
            jax.ShapeDtypeStruct((ROWS // E, E), F32),
            jax.ShapeDtypeStruct((16, 2 * RANK), F32),
            jax.ShapeDtypeStruct((8, E), F32),
        ),
        in_specs=[spec] * 9,
        out_specs=(spec,) * 4,
        scratch_shapes=scratch,
        compiler_params=pltpu.CompilerParams(
            collective_id=0, has_side_effects=True, vmem_limit_bytes=58 * 1024 * 1024
        ),
    )(
        table, accum.reshape(ROWS // E, E), reqs, mem, labels, down_proj, up_proj,
        cross_bias.reshape(NB, E), out_weight.astype(F32).reshape(NB, E),
    )
    return (
        table_new,
        accum_new.reshape(ROWS),
        gdu[:SHARE, :RANK],
        gdu[:SHARE, RANK:].T,
        bo[0, :SHARE],
        bo[1, :SHARE],
    )


def solution(mesh):
    both = ("owner", "group")
    in_specs = (
        P(both, None), P(both), P(None, "owner", "group", None, None),
        P(None, both, None, None), P(None, both), P(), P(), P(), P(),
    )
    out_specs = (P(both, None), P(both), P(both, None), P(None, both), P(both), P(both))
    return jax.shard_map(local, mesh=mesh, in_specs=in_specs, out_specs=out_specs, check_vma=False)
```

```python
import functools

import jax
import jax.numpy as jnp
from jax import lax
from jax.experimental import pallas as pl
from jax.experimental.pallas import tpu as pltpu
from jax.sharding import PartitionSpec as P

NX, NY, NZ, NC = 4, 4, 8, 2
OWNERS = NX * NZ * NC
NB = 26
BAGLEN = 4
STEPS = 3
E = 128
TOK = 128
RANK = 256
D_IN = NB * E
ROWS = 2048
SLOTS = 4
FETCH = OWNERS * SLOTS
CH = 256
NCH = D_IN // CH
NROW = ROWS // CH
UNROLL = 13
UNROLL_ROWS = 4
XROWS = D_IN // NX
HALF = XROWS // NC
PART = HALF // 2
BLOCK = XROWS // NZ
SHARE = 13
WIN = 24

learn_rate = 0.05
F32 = jnp.float32
BF16 = jnp.bfloat16


def nn(a, b):
    return jnp.dot(a, b, preferred_element_type=F32)


def nt(a, b):
    return lax.dot_general(a, b, (((1,), (1,)), ((), ())), preferred_element_type=F32)


def iota(shape, dim):
    return lax.broadcasted_iota(jnp.int32, shape, dim)


def onehot(mask):
    return jnp.where(mask, 1.0, 0.0).astype(BF16)


def al(value, step):
    return pl.multiple_of(value, step)


def remote(src, dst, send, recv, dev):
    copy = pltpu.make_async_remote_copy(
        src_ref=src, dst_ref=dst, send_sem=send, recv_sem=recv,
        device_id=dev, device_id_type=pl.DeviceIdType.MESH,
    )
    copy.start()
    return copy


def wait_all(copies):
    for copy in copies:
        copy.wait()


def kernel(
    table_in, accum_in, reqs, mem_in, labels, down_in, up_in, bias, outw,
    table_hbm, accum_out, gdu_out, bo_out,
    table, mem, down, up,
    rqs, rqr, wcol, wrow, s1, r1, g1, g2, rr, rt,
    down_t, up_t, bias_b, out_b, acc_b, posq,
    counts, x0s, dgs, lows, dlows, gates, x1s, bo3,
    gs, rc, ss, rx1, ry1, rx2, ry2, aa, bb, ff, rz, tt, fw,
    bo, boc, box, boy, boz,
    lsem, qs, qr, s1s, s1r, g1s, g1r,
    cs, cr, xs, xr, ys, yr, x2s, x2r, y2s, y2r, zs, zr, fs, fr,
    bcs, bcr, bxs, bxr, bys, byr, bzs, bzr,
):
    loads = [
        pltpu.make_async_copy(src, dst, lsem.at[n])
        for n, (src, dst) in enumerate(
            ((down_in, down), (up_in, up), (mem_in, mem), (table_in, table))
        )
    ]
    for load in loads:
        load.start()

    owner = lax.axis_index("owner")
    y = lax.axis_index("group")
    c = lax.rem(owner, NC)
    z = lax.rem(owner // NC, NZ)
    x = owner // (NC * NZ)
    at_x = [lax.rem(x + k, NX) for k in range(NX)]
    at_z = [lax.rem(z + k, NZ) for k in range(NZ)]
    at_y = [lax.rem(y + k, NY) for k in range(NY)]
    at_c = [c, 1 - c]

    def dev(px, pz, pc, py):
        return ((px * NZ + pz) * NC + pc, py)

    def zpeer(k):
        return at_z[k], dev(x, at_z[k], c, y)

    def xpeer(k):
        return at_x[k], dev(at_x[k], z, c, y)

    def ypeer(k):
        return at_y[k], dev(x, z, c, at_y[k])

    partner = dev(x, z, 1 - c, y)
    far = [
        (dx, dz, dc) for dx in range(NX) for dz in range(NZ) for dc in range(NC) if dx or dz or dc
    ]
    far.sort(key=lambda d: -(min(d[0], NX - d[0]) + min(d[1], NZ - d[1])))
    users = [dev(at_x[dx], at_z[dz], at_c[dc], y) for dx, dz, dc in far]

    barrier = pltpu.get_barrier_semaphore()
    greet = users + [dev(x, z, at_c[h], at_y[k]) for h in range(NC) for k in range(1, NY)]
    for peer in greet:
        pl.semaphore_signal(barrier, inc=1, device_id=peer, device_id_type=pl.DeviceIdType.MESH)

    def send_all(src, dst, ssem, rsem):
        for peer in users:
            remote(src.at[peer[0]], dst.at[owner], ssem, rsem, peer)

    def sent_all(src, dst, ssem, rsem):
        most = pl.ds(0, NX * NZ * NC - 1)
        return pltpu.make_async_remote_copy(
            src_ref=src.at[most], dst_ref=dst.at[most], send_sem=ssem, recv_sem=rsem,
            device_id=partner, device_id_type=pl.DeviceIdType.MESH,
        )

    flat = jnp.concatenate([reqs[...].astype(F32), jnp.zeros((E - 16, E), F32)], axis=0).T
    rqs[:, 0, :] = flat[0:OWNERS]

    def columns(i, carry):
        at = al(i * E, E)
        bias_b[pl.ds(at, E), :] = jnp.broadcast_to(bias[pl.ds(i, 1), :], (E, E)).T
        out_b[pl.ds(at, E), :] = jnp.broadcast_to(outw[pl.ds(i, 1), :], (E, E)).T
        return carry

    lax.fori_loop(0, NB, columns, 0, unroll=2)

    qi = iota((FETCH, E), 0)
    posq[...] = lax.rem(qi, OWNERS) * SLOTS + qi // OWNERS
    eye = onehot(iota((CH, CH), 0) == iota((CH, CH), 1))
    eye_e = onehot(iota((E, E), 0) == iota((E, E), 1))

    pl.semaphore_wait(barrier, len(greet))
    send_all(rqs, rqr, qs.at[0], qr.at[0])
    rqr[owner] = rqs[owner]

    def count(t):
        def bags(i, carry):
            rows = mem[t, pl.ds(al(i * 8, 8), 8), :]
            pos = posq[...]
            cnt = []
            for b in range(2):
                n = jnp.where(pos == rows[4 * b:4 * b + 1, :], 1.0, 0.0)
                for m in range(1, BAGLEN):
                    n = n + jnp.where(pos == rows[4 * b + m:4 * b + m + 1, :], 1.0, 0.0)
                cnt.append(n.astype(BF16))
            counts[lax.rem(t, 2), i] = jnp.concatenate(cnt, axis=1)
            return carry

        lax.fori_loop(0, NCH, bags, 0)

    loads[0].wait()
    loads[1].wait()

    def weights(i, carry):
        at = al(i * CH, CH)
        down_t[:, pl.ds(at, CH)] = nt(eye, down[pl.ds(at, CH), :]).astype(BF16)
        up_t[pl.ds(at, CH), :] = nt(eye, up[:, pl.ds(at, CH)]).astype(BF16)
        return carry

    lax.fori_loop(0, NCH, weights, 0)

    def acc_columns(i, carry):
        at = al(i * E, E)
        acc_b[pl.ds(at, E), :] = jnp.broadcast_to(accum_in[pl.ds(i, 1), :], (E, E)).T
        return carry

    lax.fori_loop(0, ROWS // E, acc_columns, 0, unroll=2)
    bo3[...] = jnp.zeros_like(bo3)
    loads[2].wait()
    count(0)

    sent_all(rqs, rqr, qs.at[0], qr.at[0]).wait_recv()
    arrived = rqr[:, 0, :]
    for t in range(STEPS):
        cols = [
            jnp.broadcast_to(arrived[:, t * SLOTS + s:t * SLOTS + s + 1], (OWNERS, E))
            for s in range(SLOTS)
        ]
        col = jnp.concatenate(cols, axis=0)
        wcol[t] = col.astype(jnp.int32)
        wrow[t] = col.T[0:8, :].astype(jnp.int32)

    def pick(t):
        def chunk(j, carry):
            lanes = iota((FETCH, E), 1) + j * CH
            want = wcol[t]
            rr[j] = jnp.concatenate([onehot(want == lanes), onehot(want == lanes + E)], axis=1)
            return carry

        lax.fori_loop(0, NROW, chunk, 0)

    def place(t):
        def chunk(j, carry):
            rt[j] = onehot(iota((CH, FETCH), 0) + j * CH == wrow[t][0:1, :])
            return carry

        lax.fori_loop(0, NROW, chunk, 0)

    def put(dst, t, rows):
        for s in range(SLOTS):
            dst[t, :, s, :] = rows[s * OWNERS:(s + 1) * OWNERS]

    def take(src, t):
        return jnp.concatenate([src[t, :, s, :] for s in range(SLOTS)], axis=0)

    pick(0)
    loads[3].wait()
    rows = jnp.zeros((FETCH, E), F32)
    for j in range(NROW):
        rows = rows + nn(rr[j], table[j * CH:(j + 1) * CH, :].astype(BF16))
    put(s1, 0, rows)

    def step(t, carry):
        send_all(s1.at[t], r1.at[t], s1s.at[t], s1r.at[t])
        r1[t, owner] = s1[t, owner]
        place(t)
        pick(jnp.minimum(t + 1, STEPS - 1))
        cur = lax.rem(t, 2)
        sent_all(s1.at[t], r1.at[t], s1s.at[t], s1r.at[t]).wait_recv()
        fetched_t = nt(eye_e, take(r1, t).astype(BF16)).astype(BF16)

        def pool(i, low):
            xx = nn(fetched_t, counts[cur, i]).astype(BF16)
            xx = jnp.concatenate([xx[:, :TOK], xx[:, TOK:]], axis=0)
            at = al(i * CH, CH)
            x0s[t, pl.ds(at, CH), :] = xx
            return low + nn(down_t[:, pl.ds(at, CH)], xx)

        low = lax.fori_loop(0, NCH, pool, jnp.zeros((RANK, TOK), F32), unroll=UNROLL).astype(BF16)
        lows[t] = low

        def forward(i, logit):
            at = al(i * CH, CH)
            gate = nn(up_t[pl.ds(at, CH), :], low) + bias_b[pl.ds(at, CH), :]
            gates[pl.ds(at, CH), :] = gate
            x0f = x0s[t, pl.ds(at, CH), :].astype(F32)
            x1 = (x0f * gate + x0f).astype(BF16)
            x1s[pl.ds(at, CH), :] = x1
            prod = x1.astype(F32) * out_b[pl.ds(at, CH), :]
            return logit + jnp.sum(prod.reshape(CH // 8, 8, TOK), axis=0)

        logit = lax.fori_loop(0, NCH, forward, jnp.zeros((8, TOK), F32), unroll=UNROLL)
        logit = jnp.sum(logit, axis=0, keepdims=True)
        dlogit = jax.nn.sigmoid(logit) - labels[pl.ds(t, 1), :].astype(F32)
        dhi = dlogit.astype(BF16).astype(F32)
        dmid = (dlogit - dhi).astype(BF16).astype(F32)
        dlo = dlogit - dhi - dmid
        sub = iota((16, TOK), 0)
        heads = jnp.where(sub == 0, dhi, jnp.where(sub == 1, dmid, jnp.where(sub == 2, dlo, 1.0)))
        heads = heads.astype(BF16)

        def backward(i, dlow):
            at = al(i * CH, CH)
            x0f = x0s[t, pl.ds(at, CH), :].astype(F32)
            dg = (dlogit * out_b[pl.ds(at, CH), :] * x0f).astype(BF16)
            dgs[t, pl.ds(at, CH), :] = dg
            bo3[0, i] = bo3[0, i] + nt(heads, dg)
            bo3[1, i] = bo3[1, i] + nt(heads, x1s[pl.ds(at, CH), :])
            return dlow + nn(up[:, pl.ds(at, CH)], dg)

        dlow = lax.fori_loop(0, NCH, backward, jnp.zeros((RANK, TOK), F32), unroll=UNROLL).astype(BF16)
        dlows[t] = dlow

        def spread(i, gf):
            at = al(i * CH, CH)
            dx0 = dlogit * out_b[pl.ds(at, CH), :] * (gates[pl.ds(at, CH), :] + 1.0)
            dx0 = (dx0 + nn(down[pl.ds(at, CH), :], dlow)).astype(BF16)
            both = jnp.concatenate([dx0[:E], dx0[E:]], axis=1)
            return gf + nt(counts[cur, i], both)

        put(g1, t, lax.fori_loop(0, NCH, spread, jnp.zeros((FETCH, E), F32), unroll=UNROLL))
        send_all(g1.at[t], g2.at[t], g1s.at[t], g1r.at[t])
        g2[t, owner] = g1[t, owner]

        @pl.when(t < STEPS - 1)
        def _():
            count(t + 1)

        sent_all(g1.at[t], g2.at[t], g1s.at[t], g1r.at[t]).wait_recv()
        back = take(g2, t)
        hi = back.astype(BF16)
        pair = jnp.concatenate([hi, (back - hi.astype(F32)).astype(BF16)], axis=1)

        def update(j, rows):
            at = al(j * CH, CH)
            rg = nn(rt[j], pair)
            rg = rg[:, :E] + rg[:, E:]
            acc = acc_b[pl.ds(at, CH), :] + jnp.mean(rg * rg, axis=1, keepdims=True)
            acc_b[pl.ds(at, CH), :] = acc
            new = table[pl.ds(at, CH), :] - learn_rate * rg * lax.rsqrt(acc)
            table[pl.ds(at, CH), :] = new
            return rows + nn(rr[j], new.astype(BF16))

        rows = lax.fori_loop(0, NROW, update, jnp.zeros((FETCH, E), F32), unroll=UNROLL_ROWS)
        put(s1, t + 1, rows)
        return carry

    lax.fori_loop(0, STEPS, step, 0)

    store = pltpu.make_async_copy(table, table_hbm, lsem.at[0])
    store.start()

    def acc_rows(i, carry):
        at = al(i * E, E)
        accum_out[pl.ds(i, 1), :] = acc_b[pl.ds(at, E), :].T[0:1, :]
        return carry

    lax.fori_loop(0, ROWS // E, acc_rows, 0)

    bo[...] = jnp.zeros_like(bo)
    for i in range(NCH):
        b_row = bo3[0, i][3:4, :]
        o_rows = bo3[1, i]
        o_row = o_rows[0:1, :] + o_rows[1:2, :] + o_rows[2:3, :]
        for h in range(2):
            bo[0, 2 * i + h:2 * i + h + 1, :] = b_row[:, h * E:(h + 1) * E]
            bo[0, 32 + 2 * i + h:33 + 2 * i + h, :] = o_row[:, h * E:(h + 1) * E]
    bo_copy = remote(bo.at[0], boc, bcs, bcr, partner)

    dl_all = jnp.concatenate([dlows[t] for t in range(STEPS)], axis=1)
    lo_all = jnp.concatenate([lows[t] for t in range(STEPS)], axis=1)

    def dense(px, half):
        at = al(px * XROWS + half * HALF, 16)
        xx = jnp.concatenate([x0s[t, pl.ds(at, HALF), :] for t in range(STEPS)], axis=1)
        dd = jnp.concatenate([dgs[t, pl.ds(at, HALF), :] for t in range(STEPS)], axis=1)
        return nt(xx, dl_all), nt(dd, lo_all)

    core_copies = []
    for i in range(NX):
        px = (x + 1 + i) % NX
        gd, gu = dense(px, 1 - c)
        gs[i, :, 0:RANK] = gd.astype(BF16)
        gs[i, :, RANK:] = gu.astype(BF16)
        core_copies.append(remote(gs.at[i], rc.at[i], cs.at[i], cr.at[i], partner))

    x_copies, y_copies = [], []
    for i in range(NX):
        px = (x + 1 + i) % NX
        gd, gu = dense(px, c)
        core_copies[i].wait()
        ss[i, :, 0:RANK] = (gd + rc[i, :, 0:RANK].astype(F32)).astype(BF16)
        ss[i, :, RANK:] = (gu + rc[i, :, RANK:].astype(F32)).astype(BF16)
        if i < NX - 1:
            x_copies.append(remote(
                ss.at[i, pl.ds(0, PART)], rx1.at[i], xs.at[i], xr.at[i], xpeer(i + 1)[1]
            ))
        for k in range(1, NY):
            py, d = ypeer(k)
            y_copies.append(remote(
                ss.at[i, pl.ds(PART, PART), pl.ds(al(py * E, E), E)], ry1.at[k - 1, i],
                ys.at[i, k], yr.at[i, k], d,
            ))
    bo_copy.wait()
    bo[1] = bo[0] + boc[...]
    bx_copies = [remote(bo.at[1], box.at[k - 1], bxs.at[k], bxr.at[k], xpeer(k)[1]) for k in range(1, NX)]

    my_y = pl.ds(al(y * E, E), E)
    wait_all(x_copies)
    aa[...] = (
        ss[NX - 1, 0:PART, :].astype(F32) + rx1[0].astype(F32) + rx1[1].astype(F32) + rx1[2].astype(F32)
    ).astype(BF16)
    y2_copies = []
    for k in range(1, NY):
        py, d = ypeer(k)
        y2_copies.append(remote(
            aa.at[:, pl.ds(al(py * E, E), E)], ry2.at[k - 1], y2s.at[k], y2r.at[k], d
        ))
    wait_all(y_copies)
    for i in range(NX):
        bb[i] = (
            ss[i, PART:, my_y].astype(F32)
            + ry1[0, i].astype(F32) + ry1[1, i].astype(F32) + ry1[2, i].astype(F32)
        ).astype(BF16)
    x2_copies = []
    for k in range(1, NX):
        x2_copies.append(remote(bb.at[k - 1], rx2.at[k - 1], x2s.at[k], x2r.at[k], xpeer(k)[1]))
    wait_all(bx_copies)
    bo[2] = bo[1] + box[0] + box[1] + box[2]
    by_copies = [remote(bo.at[2], boy.at[k - 1], bys.at[k], byr.at[k], ypeer(k)[1]) for k in range(1, NY)]

    wait_all(y2_copies)
    ff[0:PART] = (
        aa[:, my_y].astype(F32) + ry2[0].astype(F32) + ry2[1].astype(F32) + ry2[2].astype(F32)
    )
    wait_all(x2_copies)
    ff[PART:] = (
        bb[NX - 1].astype(F32) + rx2[0].astype(F32) + rx2[1].astype(F32) + rx2[2].astype(F32)
    )

    def z_copy(k):
        zt = c * (NZ // NC) + k
        return pltpu.make_async_remote_copy(
            src_ref=ff.at[pl.ds(k * BLOCK, BLOCK)], dst_ref=rz.at[z],
            send_sem=zs.at[k], recv_sem=zr.at[z],
            device_id=dev(x, zt, c, y), device_id_type=pl.DeviceIdType.MESH,
        )

    for k in range(NZ // NC):
        zt = c * (NZ // NC) + k

        @pl.when(zt != z)
        def _():
            z_copy(k).start()

        @pl.when(zt == z)
        def _():
            rz[z] = ff[k * BLOCK:(k + 1) * BLOCK]

    wait_all(by_copies)
    bo[3] = bo[2] + boy[0] + boy[1] + boy[2]
    bz_copies = [remote(bo.at[3], boz.at[k - 1], bzs.at[k], bzr.at[k], zpeer(k)[1]) for k in range(1, NZ)]

    holder = z // (NZ // NC)

    @pl.when(holder == c)
    def _():
        for s in range(NZ):
            @pl.when(s != z)
            def _():
                pltpu.make_async_remote_copy(
                    src_ref=ff.at[pl.ds(0, BLOCK)], dst_ref=rz.at[s],
                    send_sem=zs.at[0], recv_sem=zr.at[s],
                    device_id=partner, device_id_type=pl.DeviceIdType.MESH,
                ).wait_recv()
        total = rz[0]
        for s in range(1, NZ):
            total = total + rz[s]
        tt[...] = total

    def window(pc, py):
        off = pc * (SHARE * NY) + py * SHARE
        first = jnp.minimum((off // 8) * 8, BLOCK - WIN)
        return al(first, 8), off - first

    def f_copy(k, h):
        py = (y + k) % NY
        pc = (c + h) % NC
        return pltpu.make_async_remote_copy(
            src_ref=tt.at[pl.ds(window(pc, py)[0], WIN)], dst_ref=fw.at[y],
            send_sem=fs.at[2 * k + h], recv_sem=fr.at[k],
            device_id=dev(x, z, pc, py), device_id_type=pl.DeviceIdType.MESH,
        )

    first, skip = window(c, y)

    @pl.when(holder == c)
    def _():
        for k in range(NY):
            for h in range(NC):
                if k or h:
                    f_copy(k, h).start()
        fw[y] = tt[pl.ds(first, WIN)]

    @pl.when(holder != c)
    def _():
        f_copy(0, 1).wait_recv()

    for k in range(1, NY):
        f_copy(k, 0).wait_recv()

    scale = 1.0 / (STEPS * TOK * NX * NY * NZ * NC)
    for py in range(NY):
        gdu_out[:, py * E:(py + 1) * E] = (
            pltpu.roll(fw[py], (WIN - skip) % WIN, 0)[0:16, :] * scale
        )

    wait_all(bz_copies)
    total = bo[3]
    for k in range(NZ - 1):
        total = total + boz[k]
    bo[4] = total * scale
    start = (owner * NY + y) * SHARE
    a = start // E
    rows = []
    for base in (0, 32):
        pair = jnp.concatenate([bo[4, pl.ds(base + a, 1), :], bo[4, pl.ds(base + a + 1, 1), :]], axis=1)
        pair = jnp.broadcast_to(pair, (8, 2 * E))
        rows.append(pltpu.roll(pair, (2 * E - start % E) % (2 * E), 1)[:, 0:E])
    bo_out[...] = jnp.where(iota((8, E), 0) == 0, rows[0], rows[1])

    for k in range(NZ // NC):
        @pl.when(c * (NZ // NC) + k != z)
        def _():
            z_copy(k).wait_send()

    @pl.when(holder == c)
    def _():
        for k in range(NY):
            for h in range(NC):
                if k or h:
                    f_copy(k, h).wait_send()

    sent_all(rqs, rqr, qs.at[0], qr.at[0]).wait_send()
    for t in range(STEPS):
        sent_all(s1.at[t], r1.at[t], s1s.at[t], s1r.at[t]).wait_send()
        sent_all(g1.at[t], g2.at[t], g1s.at[t], g1r.at[t]).wait_send()
    store.wait()


def local(table, accum, requests, members, labels, down_proj, up_proj, cross_bias, out_weight):
    reqs = jnp.transpose(requests[:, 0, 0], (0, 2, 1)).reshape(STEPS * SLOTS, OWNERS)
    reqs = jnp.pad(reqs, ((0, 4), (0, E - OWNERS)))
    mem = jnp.transpose(members, (0, 2, 3, 1)).reshape(STEPS, NB * BAGLEN, TOK)
    dma = pltpu.SemaphoreType.DMA
    vm = pltpu.VMEM
    scratch = [
        vm((ROWS, E), F32), vm((STEPS, NB * BAGLEN, TOK), jnp.int32),
        vm((D_IN, RANK), BF16), vm((RANK, D_IN), BF16),
        vm((OWNERS, 1, E), F32), vm((OWNERS, 1, E), F32),
        vm((STEPS, FETCH, E), jnp.int32), vm((STEPS, 8, FETCH), jnp.int32),
        vm((STEPS + 1, OWNERS, SLOTS, E), F32),
    ]
    scratch += [vm((STEPS, OWNERS, SLOTS, E), F32)] * 3
    scratch += [
        vm((NROW, FETCH, CH), BF16), vm((NROW, CH, FETCH), BF16),
        vm((RANK, D_IN), BF16), vm((D_IN, RANK), BF16),
        vm((D_IN, TOK), F32), vm((D_IN, TOK), F32), vm((ROWS, E), F32), vm((FETCH, E), jnp.int32),
        vm((2, NCH, FETCH, 2 * TOK), BF16),
        vm((STEPS, D_IN, TOK), BF16), vm((STEPS, D_IN, TOK), BF16),
        vm((STEPS, RANK, TOK), BF16), vm((STEPS, RANK, TOK), BF16),
        vm((D_IN, TOK), F32), vm((D_IN, TOK), BF16), vm((2, NCH, 16, CH), F32),
        vm((NX, HALF, 2 * RANK), BF16), vm((NX, HALF, 2 * RANK), BF16), vm((NX, HALF, 2 * RANK), BF16),
        vm((NX - 1, PART, 2 * RANK), BF16), vm((NY - 1, NX, PART, E), BF16),
        vm((NX - 1, PART, E), BF16), vm((NY - 1, PART, E), BF16),
        vm((PART, 2 * RANK), BF16), vm((NX, PART, E), BF16), vm((HALF, E), F32),
        vm((NZ, BLOCK, E), F32), vm((BLOCK, E), F32), vm((NY, WIN, E), F32),
        vm((5, 64, E), F32), vm((64, E), F32), vm((NX - 1, 64, E), F32),
        vm((NY - 1, 64, E), F32), vm((NZ - 1, 64, E), F32),
    ]
    scratch += [dma((4,)), dma((1,)), dma((1,))]
    scratch += [dma((STEPS,))] * 4
    scratch += [dma((NX,))] * 2
    scratch += [dma((NX,))] * 2
    scratch += [dma((NX, NY))] * 2
    scratch += [dma((NX,))] * 4
    scratch += [dma((NZ,))] * 2
    scratch += [dma((8,))] * 2
    scratch += [dma] * 2
    scratch += [dma((8,))] * 6
    hbm = pl.BlockSpec(memory_space=pl.ANY)
    spec = pl.BlockSpec(memory_space=pltpu.VMEM)
    table_new, accum_new, gdu, bo = pl.pallas_call(
        kernel,
        out_shape=(
            jax.ShapeDtypeStruct((ROWS, E), F32),
            jax.ShapeDtypeStruct((ROWS // E, E), F32),
            jax.ShapeDtypeStruct((16, 2 * RANK), F32),
            jax.ShapeDtypeStruct((8, E), F32),
        ),
        in_specs=[hbm, spec, spec, hbm, spec, hbm, hbm, spec, spec],
        out_specs=(hbm, spec, spec, spec),
        scratch_shapes=scratch,
        compiler_params=pltpu.CompilerParams(
            collective_id=0, has_side_effects=True, vmem_limit_bytes=58 * 1024 * 1024
        ),
    )(
        table, accum.reshape(ROWS // E, E), reqs, mem, labels, down_proj, up_proj,
        cross_bias.reshape(NB, E), out_weight.astype(F32).reshape(NB, E),
    )
    return (
        table_new,
        accum_new.reshape(ROWS),
        gdu[:SHARE, :RANK],
        gdu[:SHARE, RANK:].T,
        bo[0, :SHARE],
        bo[1, :SHARE],
    )


def solution(mesh):
    both = ("owner", "group")
    in_specs = (
        P(both, None), P(both), P(None, "owner", "group", None, None),
        P(None, both, None, None), P(None, both), P(), P(), P(), P(),
    )
    out_specs = (P(both, None), P(both), P(both, None), P(None, both), P(both), P(both))
    return jax.shard_map(local, mesh=mesh, in_specs=in_specs, out_specs=out_specs, check_vma=False)
```

```python
import functools

import jax
import jax.numpy as jnp
from jax import lax
from jax.experimental import pallas as pl
from jax.experimental.pallas import tpu as pltpu
from jax.sharding import PartitionSpec as P

NX, NY, NZ, NC = 4, 4, 8, 2
OWNERS = NX * NZ * NC
NB = 26
BAGLEN = 4
STEPS = 3
E = 128
TOK = 128
RANK = 256
D_IN = NB * E
ROWS = 2048
SLOTS = 4
FETCH = OWNERS * SLOTS
CH = 256
NCH = D_IN // CH
NROW = ROWS // CH
UNROLL = 13
UNROLL_ROWS = 4
XROWS = D_IN // NX
BLOCK = XROWS // NZ
HALF = BLOCK // NC
GROUP = 64
CORE_ROWS = NX * NZ * GROUP
SHARE = 13

learn_rate = 0.05
F32 = jnp.float32
BF16 = jnp.bfloat16


def nn(a, b):
    return jnp.dot(a, b, preferred_element_type=F32)


def nt(a, b):
    return lax.dot_general(a, b, (((1,), (1,)), ((), ())), preferred_element_type=F32)


def iota(shape, dim):
    return lax.broadcasted_iota(jnp.int32, shape, dim)


def onehot(mask):
    return jnp.where(mask, 1.0, 0.0).astype(BF16)


def al(value, step):
    return pl.multiple_of(value, step)


def remote(src, dst, send, recv, dev):
    copy = pltpu.make_async_remote_copy(
        src_ref=src, dst_ref=dst, send_sem=send, recv_sem=recv,
        device_id=dev, device_id_type=pl.DeviceIdType.MESH,
    )
    copy.start()
    return copy


def wait_all(copies):
    for copy in copies:
        copy.wait()


def kernel(
    table_in, accum_in, reqs, mem_in, labels, down_in, up_in, bias, outw,
    table_hbm, accum_out, gdu_out, bo_out,
    table, mem, down, up,
    rqs, rqr, wcol, wrow, s1, r1, g1, g2, rr, rt,
    down_t, up_t, bias_b, out_b, acc_b, posq,
    counts, x0s, dgs, lows, dlows, gates, x1s, bo3,
    xw, xo, dw, do, lowp, dlowp, sa, ra, sb, rb, a2, ra2, b2, rb2, z3, rz,
    bo, boc, bw, bwx, bv, bvy, bvz,
    lsem, qs, qr, s1s, s1r, g1s, g1r,
    fs, fr, xs, xr, ys, yr, x2s, x2r, y2s, y2r, zs, zr,
    bcs, bcr, bxs, bxr, bys, byr, bzs, bzr,
):
    loads = [
        pltpu.make_async_copy(src, dst, lsem.at[n])
        for n, (src, dst) in enumerate(
            ((down_in, down), (up_in, up), (mem_in, mem), (table_in, table))
        )
    ]
    for load in loads:
        load.start()

    owner = lax.axis_index("owner")
    y = lax.axis_index("group")
    c = lax.rem(owner, NC)
    z = lax.rem(owner // NC, NZ)
    x = owner // (NC * NZ)
    at_x = [lax.rem(x + k, NX) for k in range(NX)]
    at_z = [lax.rem(z + k, NZ) for k in range(NZ)]
    at_y = [lax.rem(y + k, NY) for k in range(NY)]
    at_c = [c, 1 - c]

    def dev(px, pz, pc, py):
        return ((px * NZ + pz) * NC + pc, py)

    def zpeer(k):
        return at_z[k], dev(x, at_z[k], c, y)

    def xpeer(k):
        return at_x[k], dev(at_x[k], z, c, y)

    def ypeer(k):
        return at_y[k], dev(x, z, c, at_y[k])

    partner = dev(x, z, 1 - c, y)
    far = [
        (dx, dz, dc) for dx in range(NX) for dz in range(NZ) for dc in range(NC) if dx or dz or dc
    ]
    far.sort(key=lambda d: -(min(d[0], NX - d[0]) + min(d[1], NZ - d[1])))
    users = [dev(at_x[dx], at_z[dz], at_c[dc], y) for dx, dz, dc in far]

    barrier = pltpu.get_barrier_semaphore()
    greet = users + [dev(x, z, at_c[h], at_y[k]) for h in range(NC) for k in range(1, NY)]
    for peer in greet:
        pl.semaphore_signal(barrier, inc=1, device_id=peer, device_id_type=pl.DeviceIdType.MESH)

    def send_all(src, dst, ssem, rsem):
        for peer in users:
            remote(src.at[peer[0]], dst.at[owner], ssem, rsem, peer)

    def sent_all(src, dst, ssem, rsem):
        most = pl.ds(0, NX * NZ * NC - 1)
        return pltpu.make_async_remote_copy(
            src_ref=src.at[most], dst_ref=dst.at[most], send_sem=ssem, recv_sem=rsem,
            device_id=partner, device_id_type=pl.DeviceIdType.MESH,
        )

    flat = jnp.concatenate([reqs[...].astype(F32), jnp.zeros((E - 16, E), F32)], axis=0).T
    rqs[:, 0, :] = flat[0:OWNERS]

    def columns(i, carry):
        at = al(i * E, E)
        bias_b[pl.ds(at, E), :] = jnp.broadcast_to(bias[pl.ds(i, 1), :], (E, E)).T
        out_b[pl.ds(at, E), :] = jnp.broadcast_to(outw[pl.ds(i, 1), :], (E, E)).T
        return carry

    lax.fori_loop(0, NB, columns, 0, unroll=2)

    qi = iota((FETCH, E), 0)
    posq[...] = lax.rem(qi, OWNERS) * SLOTS + qi // OWNERS
    eye = onehot(iota((CH, CH), 0) == iota((CH, CH), 1))
    eye_e = onehot(iota((E, E), 0) == iota((E, E), 1))

    pl.semaphore_wait(barrier, len(greet))
    send_all(rqs, rqr, qs.at[0], qr.at[0])
    rqr[owner] = rqs[owner]

    def count(t):
        def bags(i, carry):
            rows = mem[t, pl.ds(al(i * 8, 8), 8), :]
            pos = posq[...]
            cnt = []
            for b in range(2):
                n = jnp.where(pos == rows[4 * b:4 * b + 1, :], 1.0, 0.0)
                for m in range(1, BAGLEN):
                    n = n + jnp.where(pos == rows[4 * b + m:4 * b + m + 1, :], 1.0, 0.0)
                cnt.append(n.astype(BF16))
            counts[lax.rem(t, 2), i] = jnp.concatenate(cnt, axis=1)
            return carry

        lax.fori_loop(0, NCH, bags, 0)

    loads[0].wait()
    loads[1].wait()

    def weights(i, carry):
        at = al(i * CH, CH)
        down_t[:, pl.ds(at, CH)] = nt(eye, down[pl.ds(at, CH), :]).astype(BF16)
        up_t[pl.ds(at, CH), :] = nt(eye, up[:, pl.ds(at, CH)]).astype(BF16)
        return carry

    lax.fori_loop(0, NCH, weights, 0)

    def acc_columns(i, carry):
        at = al(i * E, E)
        acc_b[pl.ds(at, E), :] = jnp.broadcast_to(accum_in[pl.ds(i, 1), :], (E, E)).T
        return carry

    lax.fori_loop(0, ROWS // E, acc_columns, 0, unroll=2)
    bo3[...] = jnp.zeros_like(bo3)
    loads[2].wait()
    count(0)

    sent_all(rqs, rqr, qs.at[0], qr.at[0]).wait_recv()
    arrived = rqr[:, 0, :]
    for t in range(STEPS):
        cols = [
            jnp.broadcast_to(arrived[:, t * SLOTS + s:t * SLOTS + s + 1], (OWNERS, E))
            for s in range(SLOTS)
        ]
        col = jnp.concatenate(cols, axis=0)
        wcol[t] = col.astype(jnp.int32)
        wrow[t] = col.T[0:8, :].astype(jnp.int32)

    def pick(t):
        def chunk(j, carry):
            lanes = iota((FETCH, E), 1) + j * CH
            want = wcol[t]
            rr[j] = jnp.concatenate([onehot(want == lanes), onehot(want == lanes + E)], axis=1)
            return carry

        lax.fori_loop(0, NROW, chunk, 0)

    def place(t):
        def chunk(j, carry):
            rt[j] = onehot(iota((CH, FETCH), 0) + j * CH == wrow[t][0:1, :])
            return carry

        lax.fori_loop(0, NROW, chunk, 0)

    def put(dst, t, rows):
        for s in range(SLOTS):
            dst[t, :, s, :] = rows[s * OWNERS:(s + 1) * OWNERS]

    def take(src, t):
        return jnp.concatenate([src[t, :, s, :] for s in range(SLOTS)], axis=0)

    pick(0)
    loads[3].wait()
    rows = jnp.zeros((FETCH, E), F32)
    for j in range(NROW):
        rows = rows + nn(rr[j], table[j * CH:(j + 1) * CH, :].astype(BF16))
    put(s1, 0, rows)

    def copy_to(src, dst, send, recv, peer):
        return pltpu.make_async_remote_copy(
            src_ref=src, dst_ref=dst, send_sem=send, recv_sem=recv,
            device_id=peer, device_id_type=pl.DeviceIdType.MESH,
        )

    def factors(t):
        pairs = ((xo.at[t], xw.at[t, 1]), (do.at[t], dw.at[t, 1]),
                 (lows.at[t], lowp.at[t]), (dlows.at[t], dlowp.at[t]))
        return [copy_to(a, b, fs.at[t, n], fr.at[t, n], partner) for n, (a, b) in enumerate(pairs)]

    def windows(t):
        def one(i, carry):
            to = pl.ds(al(i * GROUP, GROUP), GROUP)
            mine = pl.ds(al((i * BLOCK + HALF * c) // 16 * 16, 16), GROUP)
            other = pl.ds(al((i * BLOCK + HALF * (1 - c)) // 16 * 16, 16), GROUP)
            xw[t, 0, to, :] = x0s[t, mine, :]
            xo[t, to, :] = x0s[t, other, :]
            dw[t, 0, to, :] = dgs[t, mine, :]
            do[t, to, :] = dgs[t, other, :]
            return carry

        lax.fori_loop(0, NX * NZ, one, 0, unroll=4)
        for copy in factors(t):
            copy.start()

    mi = iota((CH, CH), 0)
    m_in = lax.rem(mi, 16)
    m_off = lax.rem(mi // GROUP, 2) * 8 + 4 * c
    m_col = mi // GROUP * GROUP + m_off + lax.rem(mi // 16, NY) * SHARE + m_in
    spots = onehot((m_col == iota((CH, CH), 1)) & (m_in < SHARE))

    def stage_x(k):
        return copy_to(sa.at[k - 1], ra.at[k - 1], xs.at[k], xr.at[k], xpeer(k)[1])

    def stage_y(i, k):
        py, d = ypeer(k)
        return copy_to(sb.at[py, i], rb.at[k - 1, i], ys.at[i, k], yr.at[i, k], d)

    def stage_y2(k):
        py, d = ypeer(k)
        return copy_to(a2.at[py], ra2.at[k - 1], y2s.at[k], y2r.at[k], d)

    def stage_x2(k):
        return copy_to(b2.at[k - 1], rb2.at[k - 1], x2s.at[k], x2r.at[k], xpeer(k)[1])

    def stage_z(k):
        pz, d = zpeer(k)
        return copy_to(z3.at[pl.ds(al(pz * 16, 16), 16)], rz.at[k - 1], zs.at[k], zr.at[k], d)

    def bo_core():
        return copy_to(bo.at[0], boc, bcs, bcr, partner)

    def bo_x(k):
        px, d = xpeer(k)
        return copy_to(bw.at[px], bwx.at[k - 1], bxs.at[k], bxr.at[k], d)

    def bo_y(k):
        return copy_to(bv.at[0], bvy.at[k - 1], bys.at[k], byr.at[k], ypeer(k)[1])

    def bo_z(k):
        return copy_to(bv.at[1], bvz.at[k - 1], bzs.at[k], bzr.at[k], zpeer(k)[1])

    def dense():
        windows(STEPS - 1)
        bo[...] = jnp.zeros_like(bo)
        for i in range(NCH):
            b_row = bo3[0, i][3:4, :]
            o_rows = bo3[1, i]
            o_row = o_rows[0:1, :] + o_rows[1:2, :] + o_rows[2:3, :]
            for h in range(2):
                bo[0, 2 * i + h:2 * i + h + 1, :] = b_row[:, h * E:(h + 1) * E]
                bo[0, 32 + 2 * i + h:33 + 2 * i + h, :] = o_row[:, h * E:(h + 1) * E]
        bo_core().start()
        for t in range(STEPS):
            for copy in factors(t):
                copy.wait_recv()
        dl = jnp.concatenate([r[t] for t in range(STEPS) for r in (dlows, dlowp)], axis=1)
        lo = jnp.concatenate([r[t] for t in range(STEPS) for r in (lows, lowp)], axis=1)
        for i in range(NX):
            px = at_x[(i + 1) % NX]
            for h in range(2):
                rows = pl.ds(al((px * 2 + h) * CH, CH), CH)
                xx = jnp.concatenate([xw[t, p, rows, :] for t in range(STEPS) for p in range(2)], axis=1)
                dd = jnp.concatenate([dw[t, p, rows, :] for t in range(STEPS) for p in range(2)], axis=1)
                g = jnp.concatenate([nt(xx, dl).astype(BF16), nt(dd, lo).astype(BF16)], axis=1)
                g = nn(spots, g).astype(BF16)
                for zl in range(NZ // 2):
                    to = (h * (NZ // 2) + zl) * 16
                    for py in range(NY):
                        at = (zl * NY + py) * 16
                        sa[i, py, to:to + 16, :] = g[at:at + 16, :RANK]
                        sb[py, i, to:to + 16, :] = g[at:at + 16, RANK:]
            if i < NX - 1:
                stage_x(i + 1).start()
            for k in range(1, NY):
                stage_y(i, k).start()
        bo_core().wait()
        both = bo[0] + boc[...]
        bo[1] = both
        for px in range(NX):
            first = px * XROWS // E
            bw[px, 0:8, :] = bo[1, first:first + 8, :]
            bw[px, 8:16, :] = bo[1, 32 + first:40 + first, :]
        for k in range(1, NX):
            bo_x(k).start()

    def second():
        for k in range(1, NX):
            bo_x(k).wait()
        bv[0] = bw[x] + bwx[0] + bwx[1] + bwx[2]
        for k in range(1, NY):
            bo_y(k).start()
        for k in range(1, NX):
            stage_x(k).wait()
        for py in range(NY):
            a2[py] = (
                sa[NX - 1, py].astype(F32)
                + ra[0, py].astype(F32) + ra[1, py].astype(F32) + ra[2, py].astype(F32)
            ).astype(BF16)
        for k in range(1, NY):
            stage_y2(k).start()
        for i in range(NX):
            for k in range(1, NY):
                stage_y(i, k).wait()
            b2[i] = (
                sb[y, i].astype(F32)
                + rb[0, i].astype(F32) + rb[1, i].astype(F32) + rb[2, i].astype(F32)
            ).astype(BF16)
            if i < NX - 1:
                stage_x2(i + 1).start()

    def step(t, carry):
        send_all(s1.at[t], r1.at[t], s1s.at[t], s1r.at[t])
        r1[t, owner] = s1[t, owner]
        place(t)
        pick(jnp.minimum(t + 1, STEPS - 1))
        cur = lax.rem(t, 2)
        sent_all(s1.at[t], r1.at[t], s1s.at[t], s1r.at[t]).wait_recv()
        fetched_t = nt(eye_e, take(r1, t).astype(BF16)).astype(BF16)

        def pool(i, low):
            xx = nn(fetched_t, counts[cur, i]).astype(BF16)
            xx = jnp.concatenate([xx[:, :TOK], xx[:, TOK:]], axis=0)
            at = al(i * CH, CH)
            x0s[t, pl.ds(at, CH), :] = xx
            return low + nn(down_t[:, pl.ds(at, CH)], xx)

        low = lax.fori_loop(0, NCH, pool, jnp.zeros((RANK, TOK), F32), unroll=UNROLL).astype(BF16)
        lows[t] = low

        def forward(i, logit):
            at = al(i * CH, CH)
            gate = nn(up_t[pl.ds(at, CH), :], low) + bias_b[pl.ds(at, CH), :]
            gates[pl.ds(at, CH), :] = gate
            x0f = x0s[t, pl.ds(at, CH), :].astype(F32)
            x1 = (x0f * gate + x0f).astype(BF16)
            x1s[pl.ds(at, CH), :] = x1
            prod = x1.astype(F32) * out_b[pl.ds(at, CH), :]
            return logit + jnp.sum(prod.reshape(CH // 8, 8, TOK), axis=0)

        logit = lax.fori_loop(0, NCH, forward, jnp.zeros((8, TOK), F32), unroll=UNROLL)
        logit = jnp.sum(logit, axis=0, keepdims=True)
        dlogit = jax.nn.sigmoid(logit) - labels[pl.ds(t, 1), :].astype(F32)
        dhi = dlogit.astype(BF16).astype(F32)
        dmid = (dlogit - dhi).astype(BF16).astype(F32)
        dlo = dlogit - dhi - dmid
        sub = iota((16, TOK), 0)
        heads = jnp.where(sub == 0, dhi, jnp.where(sub == 1, dmid, jnp.where(sub == 2, dlo, 1.0)))
        heads = heads.astype(BF16)

        def backward(i, dlow):
            at = al(i * CH, CH)
            x0f = x0s[t, pl.ds(at, CH), :].astype(F32)
            dg = (dlogit * out_b[pl.ds(at, CH), :] * x0f).astype(BF16)
            dgs[t, pl.ds(at, CH), :] = dg
            bo3[0, i] = bo3[0, i] + nt(heads, dg)
            bo3[1, i] = bo3[1, i] + nt(heads, x1s[pl.ds(at, CH), :])
            return dlow + nn(up[:, pl.ds(at, CH)], dg)

        dlow = lax.fori_loop(0, NCH, backward, jnp.zeros((RANK, TOK), F32), unroll=UNROLL).astype(BF16)
        dlows[t] = dlow

        @pl.when(t == STEPS - 1)
        def _():
            dense()

        def spread(i, gf):
            at = al(i * CH, CH)
            dx0 = dlogit * out_b[pl.ds(at, CH), :] * (gates[pl.ds(at, CH), :] + 1.0)
            dx0 = (dx0 + nn(down[pl.ds(at, CH), :], dlow)).astype(BF16)
            both = jnp.concatenate([dx0[:E], dx0[E:]], axis=1)
            return gf + nt(counts[cur, i], both)

        put(g1, t, lax.fori_loop(0, NCH, spread, jnp.zeros((FETCH, E), F32), unroll=UNROLL))
        send_all(g1.at[t], g2.at[t], g1s.at[t], g1r.at[t])
        g2[t, owner] = g1[t, owner]

        @pl.when(t < STEPS - 1)
        def _():
            count(t + 1)
            windows(t)

        @pl.when(t == STEPS - 1)
        def _():
            second()

        sent_all(g1.at[t], g2.at[t], g1s.at[t], g1r.at[t]).wait_recv()
        back = take(g2, t)
        hi = back.astype(BF16)
        pair = jnp.concatenate([hi, (back - hi.astype(F32)).astype(BF16)], axis=1)

        def update(j, rows):
            at = al(j * CH, CH)
            rg = nn(rt[j], pair)
            rg = rg[:, :E] + rg[:, E:]
            acc = acc_b[pl.ds(at, CH), :] + jnp.mean(rg * rg, axis=1, keepdims=True)
            acc_b[pl.ds(at, CH), :] = acc
            new = table[pl.ds(at, CH), :] - learn_rate * rg * lax.rsqrt(acc)
            table[pl.ds(at, CH), :] = new
            return rows + nn(rr[j], new.astype(BF16))

        rows = lax.fori_loop(0, NROW, update, jnp.zeros((FETCH, E), F32), unroll=UNROLL_ROWS)
        put(s1, t + 1, rows)
        return carry

    lax.fori_loop(0, STEPS, step, 0)

    store = pltpu.make_async_copy(table, table_hbm, lsem.at[0])
    store.start()

    def acc_rows(i, carry):
        at = al(i * E, E)
        accum_out[pl.ds(i, 1), :] = acc_b[pl.ds(at, E), :].T[0:1, :]
        return carry

    lax.fori_loop(0, ROWS // E, acc_rows, 0)

    for k in range(1, NY):
        bo_y(k).wait()
    bv[1] = bv[0] + bvy[0] + bvy[1] + bvy[2]
    for k in range(1, NZ):
        bo_z(k).start()
    for k in range(1, NY):
        stage_y2(k).wait()
    for k in range(1, NX):
        stage_x2(k).wait()
    z3[:, :RANK] = (
        a2[y].astype(F32) + ra2[0].astype(F32) + ra2[1].astype(F32) + ra2[2].astype(F32)
    ).astype(BF16)
    z3[:, RANK:] = (
        b2[NX - 1].astype(F32) + rb2[0].astype(F32) + rb2[1].astype(F32) + rb2[2].astype(F32)
    ).astype(BF16)
    for k in range(1, NZ):
        stage_z(k).start()

    scale = 1.0 / (STEPS * TOK * NX * NY * NZ * NC)
    for k in range(1, NZ):
        bo_z(k).wait()
    total = bv[1]
    for k in range(NZ - 1):
        total = total + bvz[k]
    bv[2] = total * scale
    start = (owner * NY + y) * SHARE - (x * XROWS // E) * E
    a = start // E
    rows = []
    for base in (0, 8):
        pair = jnp.concatenate([bv[2, pl.ds(base + a, 1), :], bv[2, pl.ds(lax.rem(base + a + 1, 16), 1), :]], axis=1)
        pair = jnp.broadcast_to(pair, (8, 2 * E))
        rows.append(pltpu.roll(pair, lax.rem(2 * E - lax.rem(start, E), 2 * E), 1)[:, 0:E])
    bo_out[...] = jnp.where(iota((8, E), 0) == 0, rows[0], rows[1])

    for k in range(1, NZ):
        stage_z(k).wait()
    total = z3[pl.ds(al(z * 16, 16), 16), :].astype(F32)
    for k in range(NZ - 1):
        total = total + rz[k].astype(F32)
    gdu_out[...] = total * scale

    for t in range(STEPS):
        for copy in factors(t):
            copy.wait_send()
    sent_all(rqs, rqr, qs.at[0], qr.at[0]).wait_send()
    for t in range(STEPS):
        sent_all(s1.at[t], r1.at[t], s1s.at[t], s1r.at[t]).wait_send()
        sent_all(g1.at[t], g2.at[t], g1s.at[t], g1r.at[t]).wait_send()
    store.wait()


def local(table, accum, requests, members, labels, down_proj, up_proj, cross_bias, out_weight):
    reqs = jnp.transpose(requests[:, 0, 0], (0, 2, 1)).reshape(STEPS * SLOTS, OWNERS)
    reqs = jnp.pad(reqs, ((0, 4), (0, E - OWNERS)))
    mem = jnp.transpose(members, (0, 2, 3, 1)).reshape(STEPS, NB * BAGLEN, TOK)
    dma = pltpu.SemaphoreType.DMA
    vm = pltpu.VMEM
    scratch = [
        vm((ROWS, E), F32), vm((STEPS, NB * BAGLEN, TOK), jnp.int32),
        vm((D_IN, RANK), BF16), vm((RANK, D_IN), BF16),
        vm((OWNERS, 1, E), F32), vm((OWNERS, 1, E), F32),
        vm((STEPS, FETCH, E), jnp.int32), vm((STEPS, 8, FETCH), jnp.int32),
        vm((STEPS + 1, OWNERS, SLOTS, E), F32),
    ]
    scratch += [vm((STEPS, OWNERS, SLOTS, E), F32)] * 3
    scratch += [
        vm((NROW, FETCH, CH), BF16), vm((NROW, CH, FETCH), BF16),
        vm((RANK, D_IN), BF16), vm((D_IN, RANK), BF16),
        vm((D_IN, TOK), F32), vm((D_IN, TOK), F32), vm((ROWS, E), F32), vm((FETCH, E), jnp.int32),
        vm((2, NCH, FETCH, 2 * TOK), BF16),
        vm((STEPS, D_IN, TOK), BF16), vm((STEPS, D_IN, TOK), BF16),
        vm((STEPS, RANK, TOK), BF16), vm((STEPS, RANK, TOK), BF16),
        vm((D_IN, TOK), F32), vm((D_IN, TOK), BF16), vm((2, NCH, 16, CH), F32),
        vm((STEPS, 2, CORE_ROWS, TOK), BF16), vm((STEPS, CORE_ROWS, TOK), BF16),
        vm((STEPS, 2, CORE_ROWS, TOK), BF16), vm((STEPS, CORE_ROWS, TOK), BF16),
        vm((STEPS, RANK, TOK), BF16), vm((STEPS, RANK, TOK), BF16),
        vm((NX, NY, NZ * 16, RANK), BF16), vm((NX - 1, NY, NZ * 16, RANK), BF16),
        vm((NY, NX, NZ * 16, RANK), BF16), vm((NY - 1, NX, NZ * 16, RANK), BF16),
        vm((NY, NZ * 16, RANK), BF16), vm((NY - 1, NZ * 16, RANK), BF16),
        vm((NX, NZ * 16, RANK), BF16), vm((NX - 1, NZ * 16, RANK), BF16),
        vm((NZ * 16, 2 * RANK), BF16), vm((NZ - 1, 16, 2 * RANK), BF16),
        vm((2, 64, E), F32), vm((64, E), F32),
        vm((NX, 16, E), F32), vm((NX - 1, 16, E), F32), vm((3, 16, E), F32),
        vm((NY - 1, 16, E), F32), vm((NZ - 1, 16, E), F32),
    ]
    scratch += [dma((4,)), dma((1,)), dma((1,))]
    scratch += [dma((STEPS,))] * 4
    scratch += [dma((STEPS, 4))] * 2
    scratch += [dma((NX,))] * 2
    scratch += [dma((NX, NY))] * 2
    scratch += [dma((NX,))] * 4
    scratch += [dma((NZ,))] * 2
    scratch += [dma] * 2
    scratch += [dma((8,))] * 6
    hbm = pl.BlockSpec(memory_space=pl.ANY)
    spec = pl.BlockSpec(memory_space=pltpu.VMEM)
    table_new, accum_new, gdu, bo = pl.pallas_call(
        kernel,
        out_shape=(
            jax.ShapeDtypeStruct((ROWS, E), F32),
            jax.ShapeDtypeStruct((ROWS // E, E), F32),
            jax.ShapeDtypeStruct((16, 2 * RANK), F32),
            jax.ShapeDtypeStruct((8, E), F32),
        ),
        in_specs=[hbm, spec, spec, hbm, spec, hbm, hbm, spec, spec],
        out_specs=(hbm, spec, spec, spec),
        scratch_shapes=scratch,
        compiler_params=pltpu.CompilerParams(
            collective_id=0, has_side_effects=True, vmem_limit_bytes=58 * 1024 * 1024
        ),
    )(
        table, accum.reshape(ROWS // E, E), reqs, mem, labels, down_proj, up_proj,
        cross_bias.reshape(NB, E), out_weight.astype(F32).reshape(NB, E),
    )
    return (
        table_new,
        accum_new.reshape(ROWS),
        gdu[:SHARE, :RANK],
        gdu[:SHARE, RANK:].T,
        bo[0, :SHARE],
        bo[1, :SHARE],
    )


def solution(mesh):
    both = ("owner", "group")
    in_specs = (
        P(both, None), P(both), P(None, "owner", "group", None, None),
        P(None, both, None, None), P(None, both), P(), P(), P(), P(),
    )
    out_specs = (P(both, None), P(both), P(both, None), P(None, both), P(both), P(both))
    return jax.shard_map(local, mesh=mesh, in_specs=in_specs, out_specs=out_specs, check_vma=False)
```

```python
import functools

import jax
import jax.numpy as jnp
from jax import lax
from jax.experimental import pallas as pl
from jax.experimental.pallas import tpu as pltpu
from jax.sharding import PartitionSpec as P

NX, NY, NZ, NC = 4, 4, 8, 2
OWNERS = NX * NZ * NC
NB = 26
BAGLEN = 4
STEPS = 3
E = 128
TOK = 128
RANK = 256
D_IN = NB * E
ROWS = 2048
SLOTS = 4
FETCH = OWNERS * SLOTS
CH = 256
NCH = D_IN // CH
NROW = ROWS // CH
UNROLL = 13
ORDER = (2, 1, 3, 0)
UNROLL_ROWS = 8
XROWS = D_IN // NX
BLOCK = XROWS // NZ
HALF = BLOCK // NC
GROUP = 64
CORE_ROWS = NX * NZ * GROUP
SHARE = 13

learn_rate = 0.05
F32 = jnp.float32
BF16 = jnp.bfloat16


def nn(a, b):
    return jnp.dot(a, b, preferred_element_type=F32)


def nt(a, b):
    return lax.dot_general(a, b, (((1,), (1,)), ((), ())), preferred_element_type=F32)


def iota(shape, dim):
    return lax.broadcasted_iota(jnp.int32, shape, dim)


def onehot(mask):
    return jnp.where(mask, 1.0, 0.0).astype(BF16)


def al(value, step):
    return pl.multiple_of(value, step)


def remote(src, dst, send, recv, dev):
    copy = pltpu.make_async_remote_copy(
        src_ref=src, dst_ref=dst, send_sem=send, recv_sem=recv,
        device_id=dev, device_id_type=pl.DeviceIdType.MESH,
    )
    copy.start()
    return copy


def wait_all(copies):
    for copy in copies:
        copy.wait()


def kernel(
    table_in, accum_in, reqs, mem_in, labels, down_in, up_in, bias, outw,
    table_hbm, accum_out, gdu_out, bo_out,
    table, mem, down, up,
    rqs, rqr, wcol, wrow, s1, r1, g1, g2, rr, rt,
    rpad, outf, both_t, up_t, bias_b, out_b, acc_b, posq,
    counts, x0s, glows, dlows, us, x1s, heads,
    xw, xo, glowp, dlowp, sa, ra, sb, rb, a2, ra2, b2, rb2, z3, rz,
    bo, boc, bw, bwx, bv, bvy, bvz,
    lsem, qs, qr, s1s, s1r, g1s, g1r,
    fs, fr, xs, xr, ys, yr, x2s, x2r, y2s, y2r, zs, zr,
    bcs, bcr, bxs, bxr, bys, byr, bzs, bzr,
):
    loads = [
        pltpu.make_async_copy(src, dst, lsem.at[n])
        for n, (src, dst) in enumerate(
            ((down_in, down), (up_in, up), (mem_in, mem), (table_in, table))
        )
    ]
    for load in loads:
        load.start()

    owner = lax.axis_index("owner")
    y = lax.axis_index("group")
    c = lax.rem(owner, NC)
    z = lax.rem(owner // NC, NZ)
    x = owner // (NC * NZ)
    at_x = [lax.rem(x + k, NX) for k in range(NX)]
    at_z = [lax.rem(z + k, NZ) for k in range(NZ)]
    at_y = [lax.rem(y + k, NY) for k in range(NY)]
    at_c = [c, 1 - c]

    def dev(px, pz, pc, py):
        return ((px * NZ + pz) * NC + pc, py)

    def zpeer(k):
        return at_z[k], dev(x, at_z[k], c, y)

    def xpeer(k):
        return at_x[k], dev(at_x[k], z, c, y)

    def ypeer(k):
        return at_y[k], dev(x, z, c, at_y[k])

    partner = dev(x, z, 1 - c, y)
    far = [
        (dx, dz, dc) for dx in range(NX) for dz in range(NZ) for dc in range(NC) if dx or dz or dc
    ]
    far.sort(key=lambda d: -(min(d[0], NX - d[0]) + min(d[1], NZ - d[1])))
    users = [dev(at_x[dx], at_z[dz], at_c[dc], y) for dx, dz, dc in far]

    barrier = pltpu.get_barrier_semaphore()
    greet = users + [dev(x, z, at_c[h], at_y[k]) for h in range(NC) for k in range(1, NY)]
    for peer in greet:
        pl.semaphore_signal(barrier, inc=1, device_id=peer, device_id_type=pl.DeviceIdType.MESH)

    def send_all(src, dst, ssem, rsem):
        for peer in users:
            remote(src.at[peer[0]], dst.at[owner], ssem, rsem, peer)

    def sent_all(src, dst, ssem, rsem):
        most = pl.ds(0, NX * NZ * NC - 1)
        return pltpu.make_async_remote_copy(
            src_ref=src.at[most], dst_ref=dst.at[most], send_sem=ssem, recv_sem=rsem,
            device_id=partner, device_id_type=pl.DeviceIdType.MESH,
        )

    rpad[...] = jnp.zeros_like(rpad)
    for t in range(STEPS):
        rpad[t * SLOTS:(t + 1) * SLOTS, 0:OWNERS] = reqs[t].astype(F32)
    flat = rpad[...].T
    rqs[:, 0, :] = flat[0:OWNERS]
    outf[...] = outw[...].astype(F32)
    out_b[D_IN:, :] = jnp.zeros((16, E), F32)

    def columns(i, carry):
        at = al(i * E, E)
        bias_b[pl.ds(at, E), :] = jnp.broadcast_to(bias[pl.ds(i, 1), :], (E, E)).T
        out_b[pl.ds(at, E), :] = jnp.broadcast_to(outf[pl.ds(i, 1), :], (E, E)).T
        return carry

    lax.fori_loop(0, NB, columns, 0, unroll=2)

    qi = iota((FETCH, E), 0)
    posq[...] = lax.rem(qi, OWNERS) * SLOTS + qi // OWNERS
    eye = onehot(iota((CH, CH), 0) == iota((CH, CH), 1))
    eye_e = onehot(iota((E, E), 0) == iota((E, E), 1))

    pl.semaphore_wait(barrier, len(greet))
    send_all(rqs, rqr, qs.at[0], qr.at[0])
    rqr[owner] = rqs[owner]

    def count(t):
        def bags(i, carry):
            rows = mem[t, pl.ds(al(i * 8, 8), 8), :]
            pos = posq[...]
            cnt = []
            for b in range(2):
                n = jnp.where(pos == rows[4 * b:4 * b + 1, :], 1.0, 0.0)
                for m in range(1, BAGLEN):
                    n = n + jnp.where(pos == rows[4 * b + m:4 * b + m + 1, :], 1.0, 0.0)
                cnt.append(n.astype(BF16))
            counts[lax.rem(t, 2), i] = jnp.concatenate(cnt, axis=1)
            return carry

        lax.fori_loop(0, NCH, bags, 0)

    loads[0].wait()
    loads[1].wait()

    def weights(i, carry):
        at = al(i * CH, CH)
        both_t[0:RANK, pl.ds(at, CH)] = nt(eye, down[pl.ds(at, CH), :]).astype(BF16)
        up_c = up[:, pl.ds(at, CH)]
        up_t[pl.ds(at, CH), :] = nt(eye, up_c).astype(BF16)
        w_row = jnp.concatenate([outf[pl.ds(2 * i, 1), :], outf[pl.ds(2 * i + 1, 1), :]], axis=1)
        both_t[RANK:, pl.ds(at, CH)] = (up_c.astype(F32) * w_row).astype(BF16)
        return carry

    lax.fori_loop(0, NCH, weights, 0)

    def acc_columns(i, carry):
        at = al(i * E, E)
        acc_b[pl.ds(at, E), :] = jnp.broadcast_to(accum_in[pl.ds(i, 1), :], (E, E)).T
        return carry

    lax.fori_loop(0, ROWS // E, acc_columns, 0, unroll=2)
    loads[2].wait()
    count(0)

    sent_all(rqs, rqr, qs.at[0], qr.at[0]).wait_recv()
    arrived = rqr[:, 0, :]
    for t in range(STEPS):
        cols = [
            jnp.broadcast_to(arrived[:, t * SLOTS + s:t * SLOTS + s + 1], (OWNERS, E))
            for s in range(SLOTS)
        ]
        col = jnp.concatenate(cols, axis=0)
        wcol[t] = col.astype(jnp.int32)
        wrow[t] = col.T[0:8, :].astype(jnp.int32)

    def pick(t):
        def chunk(j, carry):
            lanes = iota((FETCH, E), 1) + j * CH
            want = wcol[t]
            rr[j] = jnp.concatenate([onehot(want == lanes), onehot(want == lanes + E)], axis=1)
            return carry

        lax.fori_loop(0, NROW, chunk, 0)

    def place(t):
        def chunk(j, carry):
            rt[j] = onehot(iota((CH, FETCH), 0) + j * CH == wrow[t][0:1, :])
            return carry

        lax.fori_loop(0, NROW, chunk, 0)

    def put(dst, t, rows):
        for s in range(SLOTS):
            dst[t, :, s, :] = rows[s * OWNERS:(s + 1) * OWNERS]

    def take(src, t):
        return jnp.concatenate([src[t, :, s, :] for s in range(SLOTS)], axis=0)

    pick(0)
    loads[3].wait()
    rows = jnp.zeros((FETCH, E), F32)
    for j in range(NROW):
        rows = rows + nn(rr[j], table[j * CH:(j + 1) * CH, :].astype(BF16))
    put(s1, 0, rows)

    def copy_to(src, dst, send, recv, peer):
        return pltpu.make_async_remote_copy(
            src_ref=src, dst_ref=dst, send_sem=send, recv_sem=recv,
            device_id=peer, device_id_type=pl.DeviceIdType.MESH,
        )

    def rows_copy(t):
        return copy_to(xo.at[t], xw.at[t, 1], fs.at[t, 0], fr.at[t, 0], partner)

    def glow_copy(t):
        return copy_to(glows.at[t], glowp.at[t], fs.at[t, 1], fr.at[t, 1], partner)

    def dlow_copy(t):
        return copy_to(dlows.at[t], dlowp.at[t], fs.at[t, 2], fr.at[t, 2], partner)

    def factors(t):
        return [rows_copy(t), glow_copy(t), dlow_copy(t)]

    def windows(t):
        def one(i, carry):
            to = pl.ds(al(i * GROUP, GROUP), GROUP)
            mine = pl.ds(al((i * BLOCK + HALF * c) // 16 * 16, 16), GROUP)
            other = pl.ds(al((i * BLOCK + HALF * (1 - c)) // 16 * 16, 16), GROUP)
            xw[t, 0, to, :] = x0s[t, mine, :]
            xo[t, to, :] = x0s[t, other, :]
            return carry

        lax.fori_loop(0, NX * NZ, one, 0, unroll=4)
        rows_copy(t).start()

    mi = iota((CH, CH), 0)
    m_in = lax.rem(mi, 16)
    m_off = lax.rem(mi // GROUP, 2) * 8 + 4 * c
    m_col = mi // GROUP * GROUP + m_off + lax.rem(mi // 16, NY) * SHARE + m_in
    spots = onehot((m_col == iota((CH, CH), 1)) & (m_in < SHARE))

    def stage_x(k):
        return copy_to(sa.at[k], ra.at[k - 1], xs.at[k], xr.at[k], xpeer(k)[1])

    def stage_y(i, k):
        py, d = ypeer(k)
        return copy_to(sb.at[py, i], rb.at[k - 1, i], ys.at[i, k], yr.at[i, k], d)

    def stage_y2(k):
        py, d = ypeer(k)
        return copy_to(a2.at[py], ra2.at[k - 1], y2s.at[k], y2r.at[k], d)

    def stage_x2(k):
        return copy_to(b2.at[k], rb2.at[k - 1], x2s.at[k], x2r.at[k], xpeer(k)[1])

    def stage_z(k):
        pz, d = zpeer(k)
        return copy_to(z3.at[pl.ds(al(pz * 16, 16), 16)], rz.at[k - 1], zs.at[k], zr.at[k], d)

    def bo_core():
        return copy_to(bo.at[0], boc, bcs, bcr, partner)

    def bo_x(k):
        px, d = xpeer(k)
        return copy_to(bw.at[px], bwx.at[k - 1], bxs.at[k], bxr.at[k], d)

    def bo_y(k):
        return copy_to(bv.at[0], bvy.at[k - 1], bys.at[k], byr.at[k], ypeer(k)[1])

    def bo_z(k):
        return copy_to(bv.at[1], bvz.at[k - 1], bzs.at[k], bzr.at[k], zpeer(k)[1])

    def dense():
        for t in range(STEPS):
            for copy in factors(t):
                copy.wait_recv()
        right = jnp.concatenate([
            jnp.concatenate([r[t] for t in range(STEPS) for r in (dlows, dlowp)], axis=1),
            jnp.concatenate([r[t] for t in range(STEPS) for r in (glows, glowp)], axis=1),
        ], axis=0)
        for i in range(NX):
            px = at_x[ORDER[i]]
            for h in range(2):
                rows = pl.ds(al((px * 2 + h) * CH, CH), CH)
                xx = jnp.concatenate([xw[t, p, rows, :] for t in range(STEPS) for p in range(2)], axis=1)
                g = nn(spots, nt(xx, right).astype(BF16)).astype(BF16)
                for zl in range(NZ // 2):
                    to = (h * (NZ // 2) + zl) * 16
                    for py in range(NY):
                        at = (zl * NY + py) * 16
                        sa[ORDER[i], py, to:to + 16, :] = g[at:at + 16, :RANK]
                        sb[py, ORDER[i], to:to + 16, :] = g[at:at + 16, RANK:]
            if ORDER[i]:
                stage_x(ORDER[i]).start()
            for k in (2, 1, 3):
                stage_y(ORDER[i], k).start()

    def sums():
        head = jnp.concatenate([heads[t] for t in range(STEPS)], axis=1)
        bo[...] = jnp.zeros_like(bo)
        for i in range(NCH):
            at = i * CH
            b_rows = nt(head, jnp.concatenate([x0s[t, at:at + CH, :] for t in range(STEPS)], axis=1))
            o_rows = nt(head, jnp.concatenate([x1s[t, at:at + CH, :] for t in range(STEPS)], axis=1))
            b_row = b_rows[0:1, :] + b_rows[1:2, :] + b_rows[2:3, :]
            o_row = o_rows[0:1, :] + o_rows[1:2, :] + o_rows[2:3, :]
            for h in range(2):
                k = 2 * i + h
                bo[0, k:k + 1, :] = b_row[:, h * E:(h + 1) * E] * outf[k:k + 1, :]
                bo[0, 32 + k:33 + k, :] = o_row[:, h * E:(h + 1) * E]
        bo_core().start()
        bo_core().wait()
        both = bo[0] + boc[...]
        bo[1] = both
        for px in range(NX):
            first = px * XROWS // E
            bw[px, 0:8, :] = bo[1, first:first + 8, :]
            bw[px, 8:16, :] = bo[1, 32 + first:40 + first, :]
        for k in range(1, NX):
            bo_x(k).start()

    def second():
        for k in range(1, NX):
            bo_x(k).wait()
        bv[0] = bw[x] + bwx[0] + bwx[1] + bwx[2]
        for k in range(1, NY):
            bo_y(k).start()
        for k in range(1, NX):
            stage_x(k).wait()
        for py in range(NY):
            a2[py] = (
                sa[0, py].astype(F32)
                + ra[0, py].astype(F32) + ra[1, py].astype(F32) + ra[2, py].astype(F32)
            ).astype(BF16)
        for k in range(1, NY):
            stage_y2(k).start()
        for i in ORDER:
            for k in range(1, NY):
                stage_y(i, k).wait()
            b2[i] = (
                sb[y, i].astype(F32)
                + rb[0, i].astype(F32) + rb[1, i].astype(F32) + rb[2, i].astype(F32)
            ).astype(BF16)
            if i:
                stage_x2(i).start()

    def step(t, carry):
        send_all(s1.at[t], r1.at[t], s1s.at[t], s1r.at[t])
        r1[t, owner] = s1[t, owner]
        place(t)
        pick(jnp.minimum(t + 1, STEPS - 1))
        cur = lax.rem(t, 2)
        sent_all(s1.at[t], r1.at[t], s1s.at[t], s1r.at[t]).wait_recv()
        fetched_t = nt(eye_e, take(r1, t).astype(BF16)).astype(BF16)

        def pool(i, carry):
            xx = nn(fetched_t, counts[cur, i]).astype(BF16)
            at = al(i * CH, CH)
            x0s[t, pl.ds(at, E), :] = xx[:, :TOK]
            x0s[t, pl.ds(al(at + E, E), E), :] = xx[:, TOK:]
            return carry

        def project(i, total):
            at = al(i * CH, CH)
            return total + nn(both_t[:, pl.ds(at, CH)], x0s[t, pl.ds(at, CH), :])

        lax.fori_loop(0, NCH, pool, 0, unroll=UNROLL)
        total = lax.fori_loop(0, NCH, project, jnp.zeros((2 * RANK, TOK), F32), unroll=UNROLL)
        low = total[:RANK].astype(BF16)
        v = total[RANK:]
        vb = v.astype(BF16)

        @pl.when(t == STEPS - 1)
        def _():
            windows(t)

        def forward(i, logit):
            at = al(i * CH, CH)
            gate = nn(up_t[pl.ds(at, CH), :], low) + bias_b[pl.ds(at, CH), :]
            x0f = x0s[t, pl.ds(at, CH), :].astype(F32)
            w = out_b[pl.ds(at, CH), :]
            us[pl.ds(at, CH), :] = w * (gate + 1.0) + nn(down[pl.ds(at, CH), :], vb)
            x1 = (x0f * gate + x0f).astype(BF16)
            x1s[t, pl.ds(at, CH), :] = x1
            return logit + jnp.sum((x1.astype(F32) * w).reshape(CH // 8, 8, TOK), axis=0)

        logit = lax.fori_loop(0, NCH, forward, jnp.zeros((8, TOK), F32), unroll=UNROLL)
        logit = jnp.sum(logit, axis=0, keepdims=True)
        dlogit = jax.nn.sigmoid(logit) - labels[pl.ds(t, 1), :].astype(F32)
        dhi = dlogit.astype(BF16).astype(F32)
        dmid = (dlogit - dhi).astype(BF16).astype(F32)
        dlo = dlogit - dhi - dmid
        sub = iota((16, TOK), 0)
        split = jnp.where(sub == 0, dhi, jnp.where(sub == 1, dmid, jnp.where(sub == 2, dlo, 0.0)))
        heads[t] = split.astype(BF16)
        dlows[t] = (dlogit * v).astype(BF16)
        glows[t] = (dlogit * low.astype(F32)).astype(BF16)
        dlow_copy(t).start()
        glow_copy(t).start()

        @pl.when(t == STEPS - 1)
        def _():
            dense()

        def spread(i, gf):
            at = al(i * CH, CH)
            dx0 = (dlogit * us[pl.ds(at, CH), :]).astype(BF16)
            both = jnp.concatenate([dx0[:E], dx0[E:]], axis=1)
            return gf + nt(counts[cur, i], both)

        put(g1, t, lax.fori_loop(0, NCH, spread, jnp.zeros((FETCH, E), F32), unroll=UNROLL))
        send_all(g1.at[t], g2.at[t], g1s.at[t], g1r.at[t])
        g2[t, owner] = g1[t, owner]

        @pl.when(t < STEPS - 1)
        def _():
            count(t + 1)
            windows(t)

        @pl.when(t == STEPS - 1)
        def _():
            sums()
            second()

        sent_all(g1.at[t], g2.at[t], g1s.at[t], g1r.at[t]).wait_recv()
        back = take(g2, t)
        hi = back.astype(BF16)
        pair = jnp.concatenate([hi, (back - hi.astype(F32)).astype(BF16)], axis=1)

        def update(j, carry):
            at = al(j * CH, CH)
            rg = nn(rt[j], pair)
            rg = rg[:, :E] + rg[:, E:]
            acc = acc_b[pl.ds(at, CH), :] + jnp.mean(rg * rg, axis=1, keepdims=True)
            acc_b[pl.ds(at, CH), :] = acc
            table[pl.ds(at, CH), :] = table[pl.ds(at, CH), :] - learn_rate * rg * lax.rsqrt(acc)
            return carry

        def gather(j, rows):
            return rows + nn(rr[j], table[pl.ds(al(j * CH, CH), CH), :].astype(BF16))

        lax.fori_loop(0, NROW, update, 0, unroll=UNROLL_ROWS)
        rows = lax.fori_loop(0, NROW, gather, jnp.zeros((FETCH, E), F32), unroll=NROW)
        put(s1, t + 1, rows)
        return carry

    lax.fori_loop(0, STEPS, step, 0)

    store = pltpu.make_async_copy(table, table_hbm, lsem.at[0])
    store.start()

    def acc_rows(i, carry):
        at = al(i * E, E)
        accum_out[pl.ds(i, 1), :] = acc_b[pl.ds(at, E), :].T[0:1, :]
        return carry

    lax.fori_loop(0, ROWS // E, acc_rows, 0)

    for k in range(1, NY):
        bo_y(k).wait()
    bv[1] = bv[0] + bvy[0] + bvy[1] + bvy[2]
    for k in range(1, NZ):
        bo_z(k).start()
    for k in range(1, NY):
        stage_y2(k).wait()
    for k in range(1, NX):
        stage_x2(k).wait()
    z3[:, :RANK] = (
        a2[y].astype(F32) + ra2[0].astype(F32) + ra2[1].astype(F32) + ra2[2].astype(F32)
    ).astype(BF16)
    z3[:, RANK:] = (
        b2[0].astype(F32) + rb2[0].astype(F32) + rb2[1].astype(F32) + rb2[2].astype(F32)
    ).astype(BF16)
    for k in range(1, NZ):
        stage_z(k).start()

    scale = 1.0 / (STEPS * TOK * NX * NY * NZ * NC)
    for k in range(1, NZ):
        bo_z(k).wait()
    total = bv[1]
    for k in range(NZ - 1):
        total = total + bvz[k]
    bv[2] = total * scale
    start = (owner * NY + y) * SHARE - (x * XROWS // E) * E
    a = start // E
    rows = []
    for base in (0, 8):
        pair = jnp.concatenate([bv[2, pl.ds(base + a, 1), :], bv[2, pl.ds(lax.rem(base + a + 1, 16), 1), :]], axis=1)
        pair = jnp.broadcast_to(pair, (8, 2 * E))
        rows.append(pltpu.roll(pair, lax.rem(2 * E - lax.rem(start, E), 2 * E), 1)[:, 0:E])
    bo_out[...] = jnp.where(iota((8, E), 0) == 0, rows[0], rows[1])

    for k in range(1, NZ):
        stage_z(k).wait()
    total = z3[pl.ds(al(z * 16, 16), 16), :].astype(F32)
    for k in range(NZ - 1):
        total = total + rz[k].astype(F32)
    own = owner * NY + y
    w = out_b[pl.ds(own * SHARE, 16), :]
    gdu_out[:, :RANK] = total[:, :RANK] * scale
    gdu_out[:, RANK:] = total[:, RANK:] * scale * jnp.concatenate([w, w], axis=1)

    for t in range(STEPS):
        for copy in factors(t):
            copy.wait_send()
    sent_all(rqs, rqr, qs.at[0], qr.at[0]).wait_send()
    for t in range(STEPS):
        sent_all(s1.at[t], r1.at[t], s1s.at[t], s1r.at[t]).wait_send()
        sent_all(g1.at[t], g2.at[t], g1s.at[t], g1r.at[t]).wait_send()
    store.wait()


def finish(table_in, accum_in, gdu, bo, table, accum, down, up, bias, outw, sem):
    rows = ROWS // 8
    copies = [
        pltpu.make_async_copy(table_in.at[pl.ds(n * rows, rows)], table.at[pl.ds(n * rows, rows)], sem.at[n])
        for n in range(8)
    ]
    for copy in copies:
        copy.start()
    accum[...] = accum_in[...]
    down[...] = gdu[0:SHARE, :RANK]
    up[...] = gdu[0:SHARE, RANK:]
    bias[...] = bo[0:1, 0:SHARE]
    outw[...] = bo[1:2, 0:SHARE]
    for copy in copies:
        copy.wait()


def local(table, accum, requests, members, labels, down_proj, up_proj, cross_bias, out_weight):
    reqs = jnp.transpose(requests[:, 0, 0], (0, 2, 1))
    mem = jnp.transpose(members, (0, 2, 3, 1)).reshape(STEPS, NB * BAGLEN, TOK)
    dma = pltpu.SemaphoreType.DMA
    vm = pltpu.VMEM
    scratch = [
        vm((ROWS, E), F32), vm((STEPS, NB * BAGLEN, TOK), jnp.int32),
        vm((D_IN, RANK), BF16), vm((RANK, D_IN), BF16),
        vm((OWNERS, 1, E), F32), vm((OWNERS, 1, E), F32),
        vm((STEPS, FETCH, E), jnp.int32), vm((STEPS, 8, FETCH), jnp.int32),
        vm((STEPS + 1, OWNERS, SLOTS, E), F32),
    ]
    scratch += [vm((STEPS, OWNERS, SLOTS, E), F32)] * 3
    scratch += [
        vm((NROW, FETCH, CH), BF16), vm((NROW, CH, FETCH), BF16),
        vm((E, E), F32), vm((NB, E), F32), vm((2 * RANK, D_IN), BF16), vm((D_IN, RANK), BF16),
        vm((D_IN, TOK), F32), vm((D_IN + 16, TOK), F32), vm((ROWS, E), F32), vm((FETCH, E), jnp.int32),
        vm((2, NCH, FETCH, 2 * TOK), BF16),
        vm((STEPS, D_IN, TOK), BF16),
        vm((STEPS, RANK, TOK), BF16), vm((STEPS, RANK, TOK), BF16),
        vm((D_IN, TOK), F32), vm((STEPS, D_IN, TOK), BF16), vm((STEPS, 16, TOK), BF16),
        vm((STEPS, 2, CORE_ROWS, TOK), BF16), vm((STEPS, CORE_ROWS, TOK), BF16),
        vm((STEPS, RANK, TOK), BF16), vm((STEPS, RANK, TOK), BF16),
        vm((NX, NY, NZ * 16, RANK), BF16), vm((NX - 1, NY, NZ * 16, RANK), BF16),
        vm((NY, NX, NZ * 16, RANK), BF16), vm((NY - 1, NX, NZ * 16, RANK), BF16),
        vm((NY, NZ * 16, RANK), BF16), vm((NY - 1, NZ * 16, RANK), BF16),
        vm((NX, NZ * 16, RANK), BF16), vm((NX - 1, NZ * 16, RANK), BF16),
        vm((NZ * 16, 2 * RANK), BF16), vm((NZ - 1, 16, 2 * RANK), BF16),
        vm((2, 64, E), F32), vm((64, E), F32),
        vm((NX, 16, E), F32), vm((NX - 1, 16, E), F32), vm((3, 16, E), F32),
        vm((NY - 1, 16, E), F32), vm((NZ - 1, 16, E), F32),
    ]
    scratch += [dma((4,)), dma((1,)), dma((1,))]
    scratch += [dma((STEPS,))] * 4
    scratch += [dma((STEPS, 4))] * 2
    scratch += [dma((NX,))] * 2
    scratch += [dma((NX, NY))] * 2
    scratch += [dma((NX,))] * 4
    scratch += [dma((NZ,))] * 2
    scratch += [dma] * 2
    scratch += [dma((8,))] * 6
    hbm = pl.BlockSpec(memory_space=pl.ANY)
    spec = pl.BlockSpec(memory_space=pltpu.VMEM)
    table_new, accum_new, gdu, bo = pl.pallas_call(
        kernel,
        out_shape=(
            jax.ShapeDtypeStruct((ROWS, E), F32),
            jax.ShapeDtypeStruct((ROWS // E, E), F32),
            jax.ShapeDtypeStruct((16, 2 * RANK), F32),
            jax.ShapeDtypeStruct((8, E), F32),
        ),
        in_specs=[hbm, spec, spec, hbm, spec, hbm, hbm, spec, spec],
        out_specs=(hbm, spec, spec, spec),
        scratch_shapes=scratch,
        compiler_params=pltpu.CompilerParams(
            collective_id=0, has_side_effects=True, vmem_limit_bytes=58 * 1024 * 1024
        ),
    )(
        table, accum.reshape(ROWS // E, E), reqs, mem, labels, down_proj, up_proj,
        cross_bias.reshape(NB, E), out_weight.reshape(NB, E),
    )
    table_out, accum_out, down, up, bias, outw = pl.pallas_call(
        finish,
        out_shape=(
            jax.ShapeDtypeStruct((ROWS, E), F32),
            jax.ShapeDtypeStruct((ROWS // E, E), F32),
            jax.ShapeDtypeStruct((SHARE, RANK), F32),
            jax.ShapeDtypeStruct((SHARE, RANK), F32),
            jax.ShapeDtypeStruct((1, SHARE), F32),
            jax.ShapeDtypeStruct((1, SHARE), F32),
        ),
        in_specs=[hbm, spec, spec, spec],
        out_specs=(spec, spec, spec, spec, spec, spec),
        scratch_shapes=[dma((8,))],
    )(table_new, accum_new, gdu, bo)
    return (table_out, accum_out.reshape(ROWS), down, up.T, bias[0], outw[0])


def solution(mesh):
    both = ("owner", "group")
    in_specs = (
        P(both, None), P(both), P(None, "owner", "group", None, None),
        P(None, both, None, None), P(None, both), P(), P(), P(), P(),
    )
    out_specs = (P(both, None), P(both), P(both, None), P(None, both), P(both), P(both))
    return jax.shard_map(local, mesh=mesh, in_specs=in_specs, out_specs=out_specs, check_vma=False)
```

```python
import functools

import jax
import jax.numpy as jnp
from jax import lax
from jax.experimental import pallas as pl
from jax.experimental.pallas import tpu as pltpu
from jax.sharding import PartitionSpec as P

NX, NY, NZ, NC = 4, 4, 8, 2
OWNERS = NX * NZ * NC
NB = 26
BAGLEN = 4
STEPS = 3
E = 128
TOK = 128
RANK = 256
D_IN = NB * E
ROWS = 2048
SLOTS = 4
FETCH = OWNERS * SLOTS
CH = 256
NCH = D_IN // CH
NROW = ROWS // CH
UNROLL = 13
ORDER = (2, 1, 3, 0)
UNROLL_ROWS = 8
XROWS = D_IN // NX
BLOCK = XROWS // NZ
HALF = BLOCK // NC
GROUP = 64
CORE_ROWS = NX * NZ * GROUP
SHARE = 13

learn_rate = 0.05
F32 = jnp.float32
BF16 = jnp.bfloat16


def nn(a, b):
    return jnp.dot(a, b, preferred_element_type=F32)


def nt(a, b):
    return lax.dot_general(a, b, (((1,), (1,)), ((), ())), preferred_element_type=F32)


def iota(shape, dim):
    return lax.broadcasted_iota(jnp.int32, shape, dim)


def onehot(mask):
    return jnp.where(mask, 1.0, 0.0).astype(BF16)


def al(value, step):
    return pl.multiple_of(value, step)


def remote(src, dst, send, recv, dev):
    copy = pltpu.make_async_remote_copy(
        src_ref=src, dst_ref=dst, send_sem=send, recv_sem=recv,
        device_id=dev, device_id_type=pl.DeviceIdType.MESH,
    )
    copy.start()
    return copy


def wait_all(copies):
    for copy in copies:
        copy.wait()


def kernel(
    table_in, accum_in, reqs, mem_in, labels, down_in, up_in, bias, outw,
    table_hbm, accum_out, gdu_out, bo_out,
    table, mem, down, up,
    rqs, rqr, wcol, wrow, s1, r1, g1, g2, rr, rt,
    rpad, outf, both_t, up_t, bias_b, out_b, acc_b, posq,
    counts, x0s, glows, dlows, us, x1s, heads,
    xw, xo, glowp, dlowp, sa, ra, sb, rb, a2, ra2, b2, rb2, z3, rz,
    bo, boc, bw, bwx, bv, bvy, bvz,
    lsem, qs, qr, s1s, s1r, g1s, g1r,
    fs, fr, xs, xr, ys, yr, x2s, x2r, y2s, y2r, zs, zr,
    bcs, bcr, bxs, bxr, bys, byr, bzs, bzr,
):
    loads = [
        pltpu.make_async_copy(src, dst, lsem.at[n])
        for n, (src, dst) in enumerate(
            ((down_in, down), (up_in, up), (mem_in, mem), (table_in, table))
        )
    ]
    for load in loads:
        load.start()

    owner = lax.axis_index("owner")
    y = lax.axis_index("group")
    c = lax.rem(owner, NC)
    z = lax.rem(owner // NC, NZ)
    x = owner // (NC * NZ)
    at_x = [lax.rem(x + k, NX) for k in range(NX)]
    at_z = [lax.rem(z + k, NZ) for k in range(NZ)]
    at_y = [lax.rem(y + k, NY) for k in range(NY)]
    at_c = [c, 1 - c]

    def dev(px, pz, pc, py):
        return ((px * NZ + pz) * NC + pc, py)

    def zpeer(k):
        return at_z[k], dev(x, at_z[k], c, y)

    def xpeer(k):
        return at_x[k], dev(at_x[k], z, c, y)

    def ypeer(k):
        return at_y[k], dev(x, z, c, at_y[k])

    partner = dev(x, z, 1 - c, y)
    far = [
        (dx, dz, dc) for dx in range(NX) for dz in range(NZ) for dc in range(NC) if dx or dz or dc
    ]
    far.sort(key=lambda d: -(min(d[0], NX - d[0]) + min(d[1], NZ - d[1])))
    users = [dev(at_x[dx], at_z[dz], at_c[dc], y) for dx, dz, dc in far]

    barrier = pltpu.get_barrier_semaphore()
    greet = users + [dev(x, z, at_c[h], at_y[k]) for h in range(NC) for k in range(1, NY)]
    for peer in greet:
        pl.semaphore_signal(barrier, inc=1, device_id=peer, device_id_type=pl.DeviceIdType.MESH)

    def send_all(src, dst, ssem, rsem):
        for peer in users:
            remote(src.at[peer[0]], dst.at[owner], ssem, rsem, peer)

    def sent_all(src, dst, ssem, rsem):
        most = pl.ds(0, NX * NZ * NC - 1)
        return pltpu.make_async_remote_copy(
            src_ref=src.at[most], dst_ref=dst.at[most], send_sem=ssem, recv_sem=rsem,
            device_id=partner, device_id_type=pl.DeviceIdType.MESH,
        )

    rpad[...] = jnp.zeros_like(rpad)
    for t in range(STEPS):
        rpad[t * SLOTS:(t + 1) * SLOTS, 0:OWNERS] = reqs[t].astype(F32)
    flat = rpad[...].T
    rqs[:, 0, :] = flat[0:OWNERS]
    outf[...] = outw[...].astype(F32)
    out_b[D_IN:, :] = jnp.zeros((16, E), F32)

    def columns(i, carry):
        at = al(i * E, E)
        bias_b[pl.ds(at, E), :] = jnp.broadcast_to(bias[pl.ds(i, 1), :], (E, E)).T
        out_b[pl.ds(at, E), :] = jnp.broadcast_to(outf[pl.ds(i, 1), :], (E, E)).T
        return carry

    lax.fori_loop(0, NB, columns, 0, unroll=2)

    qi = iota((FETCH, E), 0)
    posq[...] = lax.rem(qi, OWNERS) * SLOTS + qi // OWNERS
    eye = onehot(iota((CH, CH), 0) == iota((CH, CH), 1))
    eye_e = onehot(iota((E, E), 0) == iota((E, E), 1))

    pl.semaphore_wait(barrier, len(greet))
    send_all(rqs, rqr, qs.at[0], qr.at[0])
    rqr[owner] = rqs[owner]

    def count(t):
        def bags(i, carry):
            rows = mem[t, pl.ds(al(i * 8, 8), 8), :]
            pos = posq[...]
            cnt = []
            for b in range(2):
                n = jnp.where(pos == rows[4 * b:4 * b + 1, :], 1.0, 0.0)
                for m in range(1, BAGLEN):
                    n = n + jnp.where(pos == rows[4 * b + m:4 * b + m + 1, :], 1.0, 0.0)
                cnt.append(n.astype(BF16))
            counts[lax.rem(t, 2), i] = jnp.concatenate(cnt, axis=1)
            return carry

        lax.fori_loop(0, NCH, bags, 0)

    loads[0].wait()
    loads[1].wait()

    def weights(i, carry):
        at = al(i * CH, CH)
        both_t[0:RANK, pl.ds(at, CH)] = nt(eye, down[pl.ds(at, CH), :]).astype(BF16)
        up_c = up[:, pl.ds(at, CH)]
        up_t[pl.ds(at, CH), :] = nt(eye, up_c).astype(BF16)
        w_row = jnp.concatenate([outf[pl.ds(2 * i, 1), :], outf[pl.ds(2 * i + 1, 1), :]], axis=1)
        both_t[RANK:, pl.ds(at, CH)] = (up_c.astype(F32) * w_row).astype(BF16)
        return carry

    lax.fori_loop(0, NCH, weights, 0)

    def acc_columns(i, carry):
        at = al(i * E, E)
        acc_b[pl.ds(at, E), :] = jnp.broadcast_to(accum_in[pl.ds(i, 1), :], (E, E)).T
        return carry

    lax.fori_loop(0, ROWS // E, acc_columns, 0, unroll=2)
    loads[2].wait()
    count(0)

    sent_all(rqs, rqr, qs.at[0], qr.at[0]).wait_recv()
    arrived = rqr[:, 0, :]
    for t in range(STEPS):
        cols = [
            jnp.broadcast_to(arrived[:, t * SLOTS + s:t * SLOTS + s + 1], (OWNERS, E))
            for s in range(SLOTS)
        ]
        col = jnp.concatenate(cols, axis=0)
        wcol[t] = col.astype(jnp.int32)
        wrow[t] = col.T[0:8, :].astype(jnp.int32)

    def pick(t):
        def chunk(j, carry):
            lanes = iota((FETCH, E), 1) + j * CH
            want = wcol[t]
            rr[j] = jnp.concatenate([onehot(want == lanes), onehot(want == lanes + E)], axis=1)
            return carry

        lax.fori_loop(0, NROW, chunk, 0)

    def place(t):
        def chunk(j, carry):
            rt[j] = onehot(iota((CH, FETCH), 0) + j * CH == wrow[t][0:1, :])
            return carry

        lax.fori_loop(0, NROW, chunk, 0)

    def put(dst, t, rows):
        for s in range(SLOTS):
            dst[t, :, s, :] = rows[s * OWNERS:(s + 1) * OWNERS]

    def take(src, t):
        return jnp.concatenate([src[t, :, s, :] for s in range(SLOTS)], axis=0)

    pick(0)
    loads[3].wait()
    rows = jnp.zeros((FETCH, E), F32)
    for j in range(NROW):
        rows = rows + nn(rr[j], table[j * CH:(j + 1) * CH, :].astype(BF16))
    put(s1, 0, rows)

    def copy_to(src, dst, send, recv, peer):
        return pltpu.make_async_remote_copy(
            src_ref=src, dst_ref=dst, send_sem=send, recv_sem=recv,
            device_id=peer, device_id_type=pl.DeviceIdType.MESH,
        )

    def rows_copy(t):
        return copy_to(xo.at[t], xw.at[t, 1], fs.at[t, 0], fr.at[t, 0], partner)

    def glow_copy(t):
        return copy_to(glows.at[t], glowp.at[t], fs.at[t, 1], fr.at[t, 1], partner)

    def dlow_copy(t):
        return copy_to(dlows.at[t], dlowp.at[t], fs.at[t, 2], fr.at[t, 2], partner)

    def factors(t):
        return [rows_copy(t), glow_copy(t), dlow_copy(t)]

    def windows(t):
        def one(i, carry):
            to = pl.ds(al(i * GROUP, GROUP), GROUP)
            mine = pl.ds(al((i * BLOCK + HALF * c) // 16 * 16, 16), GROUP)
            other = pl.ds(al((i * BLOCK + HALF * (1 - c)) // 16 * 16, 16), GROUP)
            xw[t, 0, to, :] = x0s[t, mine, :]
            xo[t, to, :] = x0s[t, other, :]
            return carry

        lax.fori_loop(0, NX * NZ, one, 0, unroll=4)
        rows_copy(t).start()

    mi = iota((CH, CH), 0)
    m_in = lax.rem(mi, 16)
    m_off = lax.rem(mi // GROUP, 2) * 8 + 4 * c
    m_col = mi // GROUP * GROUP + m_off + lax.rem(mi // 16, NY) * SHARE + m_in
    spots = onehot((m_col == iota((CH, CH), 1)) & (m_in < SHARE))

    def cut(h):
        return pl.ds(h * (NZ // 2) * 16, (NZ // 2) * 16)

    def stage_x(k, h):
        return copy_to(
            sa.at[k, :, cut(h)], ra.at[k - 1, :, cut(h)], xs.at[k, h], xr.at[k, h], xpeer(k)[1]
        )

    def stage_y(i, k, h):
        py, d = ypeer(k)
        return copy_to(
            sb.at[py, i, cut(h)], rb.at[k - 1, i, cut(h)], ys.at[i, k, h], yr.at[i, k, h], d
        )

    def stage_y2(k, h):
        py, d = ypeer(k)
        return copy_to(a2.at[py, cut(h)], ra2.at[k - 1, cut(h)], y2s.at[k, h], y2r.at[k, h], d)

    def stage_x2(k, h):
        return copy_to(
            b2.at[k, cut(h)], rb2.at[k - 1, cut(h)], x2s.at[k, h], x2r.at[k, h], xpeer(k)[1]
        )

    def z_copy(k, zt):
        return copy_to(
            z3.at[pl.ds(al(zt * 16, 16), 16)], rz.at[z], zs.at[k], zr.at[z], dev(x, zt, c, y)
        )

    def bo_core():
        return copy_to(bo.at[0], boc, bcs, bcr, partner)

    def bo_x(k):
        px, d = xpeer(k)
        return copy_to(bw.at[px], bwx.at[k - 1], bxs.at[k], bxr.at[k], d)

    def bo_y(k):
        return copy_to(bv.at[0], bvy.at[k - 1], bys.at[k], byr.at[k], ypeer(k)[1])

    def bo_z(k):
        return copy_to(bv.at[1], bvz.at[k - 1], bzs.at[k], bzr.at[k], zpeer(k)[1])

    def dense():
        for t in range(STEPS):
            for copy in factors(t):
                copy.wait_recv()
        right = jnp.concatenate([
            jnp.concatenate([r[t] for t in range(STEPS) for r in (dlows, dlowp)], axis=1),
            jnp.concatenate([r[t] for t in range(STEPS) for r in (glows, glowp)], axis=1),
        ], axis=0)
        for h in range(2):
            for i in range(NX):
                px = at_x[ORDER[i]]
                rows = pl.ds(al((px * 2 + h) * CH, CH), CH)
                xx = jnp.concatenate([xw[t, p, rows, :] for t in range(STEPS) for p in range(2)], axis=1)
                g = nn(spots, nt(xx, right).astype(BF16)).astype(BF16)
                for zl in range(NZ // 2):
                    to = (h * (NZ // 2) + zl) * 16
                    for py in range(NY):
                        at = (zl * NY + py) * 16
                        sa[ORDER[i], py, to:to + 16, :] = g[at:at + 16, :RANK]
                        sb[py, ORDER[i], to:to + 16, :] = g[at:at + 16, RANK:]
                if ORDER[i]:
                    stage_x(ORDER[i], h).start()
                for k in (2, 1, 3):
                    stage_y(ORDER[i], k, h).start()

    def sums():
        head = jnp.concatenate([heads[t] for t in range(STEPS)], axis=1)
        bo[...] = jnp.zeros_like(bo)
        for i in range(NCH):
            at = i * CH
            b_rows = nt(head, jnp.concatenate([x0s[t, at:at + CH, :] for t in range(STEPS)], axis=1))
            o_rows = nt(head, jnp.concatenate([x1s[t, at:at + CH, :] for t in range(STEPS)], axis=1))
            b_row = b_rows[0:1, :] + b_rows[1:2, :] + b_rows[2:3, :]
            o_row = o_rows[0:1, :] + o_rows[1:2, :] + o_rows[2:3, :]
            for h in range(2):
                k = 2 * i + h
                bo[0, k:k + 1, :] = b_row[:, h * E:(h + 1) * E] * outf[k:k + 1, :]
                bo[0, 32 + k:33 + k, :] = o_row[:, h * E:(h + 1) * E]
        bo_core().start()
        bo_core().wait()
        both = bo[0] + boc[...]
        bo[1] = both
        for px in range(NX):
            first = px * XROWS // E
            bw[px, 0:8, :] = bo[1, first:first + 8, :]
            bw[px, 8:16, :] = bo[1, 32 + first:40 + first, :]
        for k in range(1, NX):
            bo_x(k).start()

    def second():
        for k in range(1, NX):
            bo_x(k).wait()
        bv[0] = bw[x] + bwx[0] + bwx[1] + bwx[2]
        for k in range(1, NY):
            bo_y(k).start()
        first(0)
        first(1)

    def first(h):
        for k in range(1, NX):
            stage_x(k, h).wait()
        for py in range(NY):
            a2[py, cut(h)] = (
                sa[0, py, cut(h)].astype(F32)
                + ra[0, py, cut(h)].astype(F32) + ra[1, py, cut(h)].astype(F32)
                + ra[2, py, cut(h)].astype(F32)
            ).astype(BF16)
        for k in (2, 1, 3):
            stage_y2(k, h).start()
        for i in ORDER:
            for k in range(1, NY):
                stage_y(i, k, h).wait()
            b2[i, cut(h)] = (
                sb[y, i, cut(h)].astype(F32)
                + rb[0, i, cut(h)].astype(F32) + rb[1, i, cut(h)].astype(F32)
                + rb[2, i, cut(h)].astype(F32)
            ).astype(BF16)
            if i:
                stage_x2(i, h).start()

    def third(h):
        for k in range(1, NY):
            stage_y2(k, h).wait()
        for k in range(1, NX):
            stage_x2(k, h).wait()
        z3[cut(h), :RANK] = (
            a2[y, cut(h)].astype(F32) + ra2[0, cut(h)].astype(F32) + ra2[1, cut(h)].astype(F32)
            + ra2[2, cut(h)].astype(F32)
        ).astype(BF16)
        z3[cut(h), RANK:] = (
            b2[0, cut(h)].astype(F32) + rb2[0, cut(h)].astype(F32) + rb2[1, cut(h)].astype(F32)
            + rb2[2, cut(h)].astype(F32)
        ).astype(BF16)
        for k in range(NZ // 2):
            zt = h * (NZ // 2) + k

            @pl.when(zt != z)
            def _():
                z_copy(zt, zt).start()

            @pl.when(zt == z)
            def _():
                rz[z] = z3[zt * 16:zt * 16 + 16, :]

    def step(t, carry):
        send_all(s1.at[t], r1.at[t], s1s.at[t], s1r.at[t])
        r1[t, owner] = s1[t, owner]
        place(t)
        pick(jnp.minimum(t + 1, STEPS - 1))
        cur = lax.rem(t, 2)
        sent_all(s1.at[t], r1.at[t], s1s.at[t], s1r.at[t]).wait_recv()
        fetched_t = nt(eye_e, take(r1, t).astype(BF16)).astype(BF16)

        def pool(i, carry):
            xx = nn(fetched_t, counts[cur, i]).astype(BF16)
            at = al(i * CH, CH)
            x0s[t, pl.ds(at, E), :] = xx[:, :TOK]
            x0s[t, pl.ds(al(at + E, E), E), :] = xx[:, TOK:]
            return carry

        def project(i, total):
            at = al(i * CH, CH)
            return total + nn(both_t[:, pl.ds(at, CH)], x0s[t, pl.ds(at, CH), :])

        lax.fori_loop(0, NCH, pool, 0, unroll=UNROLL)
        total = lax.fori_loop(0, NCH, project, jnp.zeros((2 * RANK, TOK), F32), unroll=UNROLL)
        low = total[:RANK].astype(BF16)
        v = total[RANK:]
        vb = v.astype(BF16)

        @pl.when(t == STEPS - 1)
        def _():
            windows(t)

        def forward(i, logit):
            at = al(i * CH, CH)
            gate = nn(up_t[pl.ds(at, CH), :], low) + bias_b[pl.ds(at, CH), :]
            x0f = x0s[t, pl.ds(at, CH), :].astype(F32)
            w = out_b[pl.ds(at, CH), :]
            us[pl.ds(at, CH), :] = w * (gate + 1.0) + nn(down[pl.ds(at, CH), :], vb)
            x1 = (x0f * gate + x0f).astype(BF16)
            x1s[t, pl.ds(at, CH), :] = x1
            return logit + jnp.sum((x1.astype(F32) * w).reshape(CH // 8, 8, TOK), axis=0)

        logit = lax.fori_loop(0, NCH, forward, jnp.zeros((8, TOK), F32), unroll=UNROLL)
        logit = jnp.sum(logit, axis=0, keepdims=True)
        dlogit = jax.nn.sigmoid(logit) - labels[pl.ds(t, 1), :].astype(F32)
        dhi = dlogit.astype(BF16).astype(F32)
        dmid = (dlogit - dhi).astype(BF16).astype(F32)
        dlo = dlogit - dhi - dmid
        sub = iota((16, TOK), 0)
        split = jnp.where(sub == 0, dhi, jnp.where(sub == 1, dmid, jnp.where(sub == 2, dlo, 0.0)))
        heads[t] = split.astype(BF16)
        dlows[t] = (dlogit * v).astype(BF16)
        glows[t] = (dlogit * low.astype(F32)).astype(BF16)
        dlow_copy(t).start()
        glow_copy(t).start()

        def spread(i, gf):
            at = al(i * CH, CH)
            dx0 = (dlogit * us[pl.ds(at, CH), :]).astype(BF16)
            both = jnp.concatenate([dx0[:E], dx0[E:]], axis=1)
            return gf + nt(counts[cur, i], both)

        put(g1, t, lax.fori_loop(0, NCH, spread, jnp.zeros((FETCH, E), F32), unroll=UNROLL))
        send_all(g1.at[t], g2.at[t], g1s.at[t], g1r.at[t])
        g2[t, owner] = g1[t, owner]

        @pl.when(t < STEPS - 1)
        def _():
            count(t + 1)
            windows(t)

        @pl.when(t == STEPS - 1)
        def _():
            dense()
            sums()

        sent_all(g1.at[t], g2.at[t], g1s.at[t], g1r.at[t]).wait_recv()
        back = take(g2, t)
        hi = back.astype(BF16)
        pair = jnp.concatenate([hi, (back - hi.astype(F32)).astype(BF16)], axis=1)

        def update(j, carry):
            at = al(j * CH, CH)
            rg = nn(rt[j], pair)
            rg = rg[:, :E] + rg[:, E:]
            acc = acc_b[pl.ds(at, CH), :] + jnp.mean(rg * rg, axis=1, keepdims=True)
            acc_b[pl.ds(at, CH), :] = acc
            table[pl.ds(at, CH), :] = table[pl.ds(at, CH), :] - learn_rate * rg * lax.rsqrt(acc)
            return carry

        def gather(j, rows):
            return rows + nn(rr[j], table[pl.ds(al(j * CH, CH), CH), :].astype(BF16))

        lax.fori_loop(0, NROW, update, 0, unroll=UNROLL_ROWS)
        rows = lax.fori_loop(0, NROW, gather, jnp.zeros((FETCH, E), F32), unroll=NROW)
        put(s1, t + 1, rows)
        return carry

    lax.fori_loop(0, STEPS, step, 0)

    store = pltpu.make_async_copy(table, table_hbm, lsem.at[0])
    store.start()

    def acc_rows(i, carry):
        at = al(i * E, E)
        accum_out[pl.ds(i, 1), :] = acc_b[pl.ds(at, E), :].T[0:1, :]
        return carry

    lax.fori_loop(0, ROWS // E, acc_rows, 0)

    second()
    for k in range(1, NY):
        bo_y(k).wait()
    bv[1] = bv[0] + bvy[0] + bvy[1] + bvy[2]
    for k in range(1, NZ):
        bo_z(k).start()
    third(0)
    third(1)

    scale = 1.0 / (STEPS * TOK * NX * NY * NZ * NC)
    for k in range(1, NZ):
        bo_z(k).wait()
    total = bv[1]
    for k in range(NZ - 1):
        total = total + bvz[k]
    bv[2] = total * scale
    start = (owner * NY + y) * SHARE - (x * XROWS // E) * E
    a = start // E
    rows = []
    for base in (0, 8):
        pair = jnp.concatenate([bv[2, pl.ds(base + a, 1), :], bv[2, pl.ds(lax.rem(base + a + 1, 16), 1), :]], axis=1)
        pair = jnp.broadcast_to(pair, (8, 2 * E))
        rows.append(pltpu.roll(pair, lax.rem(2 * E - lax.rem(start, E), 2 * E), 1)[:, 0:E])
    bo_out[...] = jnp.where(iota((8, E), 0) == 0, rows[0], rows[1])

    for k in range(NZ):
        @pl.when(k != z)
        def _():
            copy_to(z3.at[pl.ds(0, 16)], rz.at[k], zs.at[0], zr.at[k], partner).wait_recv()
            z_copy(k, k).wait_send()
    total = rz[0].astype(F32)
    for k in range(1, NZ):
        total = total + rz[k].astype(F32)
    own = owner * NY + y
    w = out_b[pl.ds(own * SHARE, 16), :]
    gdu_out[:, :RANK] = total[:, :RANK] * scale
    gdu_out[:, RANK:] = total[:, RANK:] * scale * jnp.concatenate([w, w], axis=1)

    for t in range(STEPS):
        for copy in factors(t):
            copy.wait_send()
    sent_all(rqs, rqr, qs.at[0], qr.at[0]).wait_send()
    for t in range(STEPS):
        sent_all(s1.at[t], r1.at[t], s1s.at[t], s1r.at[t]).wait_send()
        sent_all(g1.at[t], g2.at[t], g1s.at[t], g1r.at[t]).wait_send()
    store.wait()


def finish(table_in, accum_in, gdu, bo, table, accum, down, up, bias, outw, sem):
    rows = ROWS // 8
    copies = [
        pltpu.make_async_copy(table_in.at[pl.ds(n * rows, rows)], table.at[pl.ds(n * rows, rows)], sem.at[n])
        for n in range(8)
    ]
    for copy in copies:
        copy.start()
    accum[...] = accum_in[...]
    down[...] = gdu[0:SHARE, :RANK]
    up[...] = gdu[0:SHARE, RANK:]
    bias[...] = bo[0:1, 0:SHARE]
    outw[...] = bo[1:2, 0:SHARE]
    for copy in copies:
        copy.wait()


def local(table, accum, requests, members, labels, down_proj, up_proj, cross_bias, out_weight):
    reqs = jnp.transpose(requests[:, 0, 0], (0, 2, 1))
    mem = jnp.transpose(members, (0, 2, 3, 1)).reshape(STEPS, NB * BAGLEN, TOK)
    dma = pltpu.SemaphoreType.DMA
    vm = pltpu.VMEM
    scratch = [
        vm((ROWS, E), F32), vm((STEPS, NB * BAGLEN, TOK), jnp.int32),
        vm((D_IN, RANK), BF16), vm((RANK, D_IN), BF16),
        vm((OWNERS, 1, E), F32), vm((OWNERS, 1, E), F32),
        vm((STEPS, FETCH, E), jnp.int32), vm((STEPS, 8, FETCH), jnp.int32),
        vm((STEPS + 1, OWNERS, SLOTS, E), F32),
    ]
    scratch += [vm((STEPS, OWNERS, SLOTS, E), F32)] * 3
    scratch += [
        vm((NROW, FETCH, CH), BF16), vm((NROW, CH, FETCH), BF16),
        vm((E, E), F32), vm((NB, E), F32), vm((2 * RANK, D_IN), BF16), vm((D_IN, RANK), BF16),
        vm((D_IN, TOK), F32), vm((D_IN + 16, TOK), F32), vm((ROWS, E), F32), vm((FETCH, E), jnp.int32),
        vm((2, NCH, FETCH, 2 * TOK), BF16),
        vm((STEPS, D_IN, TOK), BF16),
        vm((STEPS, RANK, TOK), BF16), vm((STEPS, RANK, TOK), BF16),
        vm((D_IN, TOK), F32), vm((STEPS, D_IN, TOK), BF16), vm((STEPS, 16, TOK), BF16),
        vm((STEPS, 2, CORE_ROWS, TOK), BF16), vm((STEPS, CORE_ROWS, TOK), BF16),
        vm((STEPS, RANK, TOK), BF16), vm((STEPS, RANK, TOK), BF16),
        vm((NX, NY, NZ * 16, RANK), BF16), vm((NX - 1, NY, NZ * 16, RANK), BF16),
        vm((NY, NX, NZ * 16, RANK), BF16), vm((NY - 1, NX, NZ * 16, RANK), BF16),
        vm((NY, NZ * 16, RANK), BF16), vm((NY - 1, NZ * 16, RANK), BF16),
        vm((NX, NZ * 16, RANK), BF16), vm((NX - 1, NZ * 16, RANK), BF16),
        vm((NZ * 16, 2 * RANK), BF16), vm((NZ, 16, 2 * RANK), BF16),
        vm((2, 64, E), F32), vm((64, E), F32),
        vm((NX, 16, E), F32), vm((NX - 1, 16, E), F32), vm((3, 16, E), F32),
        vm((NY - 1, 16, E), F32), vm((NZ - 1, 16, E), F32),
    ]
    scratch += [dma((4,)), dma((1,)), dma((1,))]
    scratch += [dma((STEPS,))] * 4
    scratch += [dma((STEPS, 4))] * 2
    scratch += [dma((NX, 2))] * 2
    scratch += [dma((NX, NY, 2))] * 2
    scratch += [dma((NX, 2))] * 4
    scratch += [dma((NZ,))] * 2
    scratch += [dma] * 2
    scratch += [dma((8,))] * 6
    hbm = pl.BlockSpec(memory_space=pl.ANY)
    spec = pl.BlockSpec(memory_space=pltpu.VMEM)
    table_new, accum_new, gdu, bo = pl.pallas_call(
        kernel,
        out_shape=(
            jax.ShapeDtypeStruct((ROWS, E), F32),
            jax.ShapeDtypeStruct((ROWS // E, E), F32),
            jax.ShapeDtypeStruct((16, 2 * RANK), F32),
            jax.ShapeDtypeStruct((8, E), F32),
        ),
        in_specs=[hbm, spec, spec, hbm, spec, hbm, hbm, spec, spec],
        out_specs=(hbm, spec, spec, spec),
        scratch_shapes=scratch,
        compiler_params=pltpu.CompilerParams(
            collective_id=0, has_side_effects=True, vmem_limit_bytes=58 * 1024 * 1024
        ),
    )(
        table, accum.reshape(ROWS // E, E), reqs, mem, labels, down_proj, up_proj,
        cross_bias.reshape(NB, E), out_weight.reshape(NB, E),
    )
    table_out, accum_out, down, up, bias, outw = pl.pallas_call(
        finish,
        out_shape=(
            jax.ShapeDtypeStruct((ROWS, E), F32),
            jax.ShapeDtypeStruct((ROWS // E, E), F32),
            jax.ShapeDtypeStruct((SHARE, RANK), F32),
            jax.ShapeDtypeStruct((SHARE, RANK), F32),
            jax.ShapeDtypeStruct((1, SHARE), F32),
            jax.ShapeDtypeStruct((1, SHARE), F32),
        ),
        in_specs=[hbm, spec, spec, spec],
        out_specs=(spec, spec, spec, spec, spec, spec),
        scratch_shapes=[dma((8,))],
    )(table_new, accum_new, gdu, bo)
    return (table_out, accum_out.reshape(ROWS), down, up.T, bias[0], outw[0])


def solution(mesh):
    both = ("owner", "group")
    in_specs = (
        P(both, None), P(both), P(None, "owner", "group", None, None),
        P(None, both, None, None), P(None, both), P(), P(), P(), P(),
    )
    out_specs = (P(both, None), P(both), P(both, None), P(None, both), P(both), P(both))
    return jax.shard_map(local, mesh=mesh, in_specs=in_specs, out_specs=out_specs, check_vma=False)
```

```python
import functools

import jax
import jax.numpy as jnp
from jax import lax
from jax.experimental import pallas as pl
from jax.experimental.pallas import tpu as pltpu
from jax.sharding import PartitionSpec as P

NX, NY, NZ, NC = 4, 4, 8, 2
OWNERS = NX * NZ * NC
NB = 26
BAGLEN = 4
STEPS = 3
E = 128
TOK = 128
RANK = 256
D_IN = NB * E
ROWS = 2048
SLOTS = 4
FETCH = OWNERS * SLOTS
CH = 256
NCH = D_IN // CH
NROW = ROWS // CH
UNROLL = 13
ORDER = (2, 1, 3, 0)
UNROLL_ROWS = 8
XROWS = D_IN // NX
BLOCK = XROWS // NZ
HALF = BLOCK // NC
GROUP = 64
CORE_ROWS = NX * NZ * GROUP
SHARE = 13

learn_rate = 0.05
F32 = jnp.float32
BF16 = jnp.bfloat16


def nn(a, b):
    return jnp.dot(a, b, preferred_element_type=F32)


def nt(a, b):
    return lax.dot_general(a, b, (((1,), (1,)), ((), ())), preferred_element_type=F32)


def iota(shape, dim):
    return lax.broadcasted_iota(jnp.int32, shape, dim)


def onehot(mask):
    return jnp.where(mask, 1.0, 0.0).astype(BF16)


def al(value, step):
    return pl.multiple_of(value, step)


def remote(src, dst, send, recv, dev):
    copy = pltpu.make_async_remote_copy(
        src_ref=src, dst_ref=dst, send_sem=send, recv_sem=recv,
        device_id=dev, device_id_type=pl.DeviceIdType.MESH,
    )
    copy.start()
    return copy


def wait_all(copies):
    for copy in copies:
        copy.wait()


def kernel(
    table_in, accum_in, reqs, mem_in, labels, down_in, up_in, bias, outw,
    table_hbm, accum_out, gdu_out, bo_out,
    table, mem, down, up,
    rqs, rqr, acc_q, base_q, same, match, back, wcol, wrow, s1, r1, g1, g2, rr, rt,
    rpad, outf, both_t, up_t, bias_b, out_b, acc_b, posq,
    counts, x0s, glows, dlows, us, x1s, heads,
    xw, xo, glowp, dlowp, sa, ra, sb, rb, a2, ra2, b2, rb2, z3, rz,
    bo, boc, bw, bwx, bv, bvy, bvz,
    lsem, qs, qr, s1s, s1r, g1s, g1r,
    fs, fr, xs, xr, ys, yr, x2s, x2r, y2s, y2r, zs, zr,
    bcs, bcr, bxs, bxr, bys, byr, bzs, bzr,
):
    loads = [
        pltpu.make_async_copy(src, dst, lsem.at[n])
        for n, (src, dst) in enumerate(
            ((down_in, down), (up_in, up), (mem_in, mem), (table_in, table))
        )
    ]
    for load in loads:
        load.start()

    owner = lax.axis_index("owner")
    y = lax.axis_index("group")
    c = lax.rem(owner, NC)
    z = lax.rem(owner // NC, NZ)
    x = owner // (NC * NZ)
    at_x = [lax.rem(x + k, NX) for k in range(NX)]
    at_z = [lax.rem(z + k, NZ) for k in range(NZ)]
    at_y = [lax.rem(y + k, NY) for k in range(NY)]
    at_c = [c, 1 - c]

    def dev(px, pz, pc, py):
        return ((px * NZ + pz) * NC + pc, py)

    def zpeer(k):
        return at_z[k], dev(x, at_z[k], c, y)

    def xpeer(k):
        return at_x[k], dev(at_x[k], z, c, y)

    def ypeer(k):
        return at_y[k], dev(x, z, c, at_y[k])

    partner = dev(x, z, 1 - c, y)
    far = [
        (dx, dz, dc) for dx in range(NX) for dz in range(NZ) for dc in range(NC) if dx or dz or dc
    ]
    far.sort(key=lambda d: -(min(d[0], NX - d[0]) + min(d[1], NZ - d[1])))
    users = [dev(at_x[dx], at_z[dz], at_c[dc], y) for dx, dz, dc in far]

    barrier = pltpu.get_barrier_semaphore()
    greet = users + [dev(x, z, at_c[h], at_y[k]) for h in range(NC) for k in range(1, NY)]
    for peer in greet:
        pl.semaphore_signal(barrier, inc=1, device_id=peer, device_id_type=pl.DeviceIdType.MESH)

    def send_all(src, dst, ssem, rsem):
        for peer in users:
            remote(src.at[peer[0]], dst.at[owner], ssem, rsem, peer)

    def sent_all(src, dst, ssem, rsem):
        most = pl.ds(0, NX * NZ * NC - 1)
        return pltpu.make_async_remote_copy(
            src_ref=src.at[most], dst_ref=dst.at[most], send_sem=ssem, recv_sem=rsem,
            device_id=partner, device_id_type=pl.DeviceIdType.MESH,
        )

    rpad[...] = jnp.zeros_like(rpad)
    for t in range(STEPS):
        rpad[t * SLOTS:(t + 1) * SLOTS, 0:OWNERS] = reqs[t].astype(F32)
    flat = rpad[...].T
    rqs[:, 0, :] = flat[0:OWNERS]
    outf[...] = outw[...].astype(F32)
    out_b[D_IN:, :] = jnp.zeros((16, E), F32)

    def columns(i, carry):
        at = al(i * E, E)
        bias_b[pl.ds(at, E), :] = jnp.broadcast_to(bias[pl.ds(i, 1), :], (E, E)).T
        out_b[pl.ds(at, E), :] = jnp.broadcast_to(outf[pl.ds(i, 1), :], (E, E)).T
        return carry

    lax.fori_loop(0, NB, columns, 0, unroll=2)

    qi = iota((FETCH, E), 0)
    posq[...] = lax.rem(qi, OWNERS) * SLOTS + qi // OWNERS
    eye = onehot(iota((CH, CH), 0) == iota((CH, CH), 1))
    eye_e = onehot(iota((E, E), 0) == iota((E, E), 1))

    pl.semaphore_wait(barrier, len(greet))
    send_all(rqs, rqr, qs.at[0], qr.at[0])
    rqr[owner] = rqs[owner]

    def count(t):
        def bags(i, carry):
            rows = mem[t, pl.ds(al(i * 8, 8), 8), :]
            pos = posq[...]
            cnt = []
            for b in range(2):
                n = jnp.where(pos == rows[4 * b:4 * b + 1, :], 1.0, 0.0)
                for m in range(1, BAGLEN):
                    n = n + jnp.where(pos == rows[4 * b + m:4 * b + m + 1, :], 1.0, 0.0)
                cnt.append(n.astype(BF16))
            counts[lax.rem(t, 2), i] = jnp.concatenate(cnt, axis=1)
            return carry

        lax.fori_loop(0, NCH, bags, 0)

    loads[0].wait()
    loads[1].wait()

    def weights(i, carry):
        at = al(i * CH, CH)
        both_t[0:RANK, pl.ds(at, CH)] = nt(eye, down[pl.ds(at, CH), :]).astype(BF16)
        up_c = up[:, pl.ds(at, CH)]
        up_t[pl.ds(at, CH), :] = nt(eye, up_c).astype(BF16)
        w_row = jnp.concatenate([outf[pl.ds(2 * i, 1), :], outf[pl.ds(2 * i + 1, 1), :]], axis=1)
        both_t[RANK:, pl.ds(at, CH)] = (up_c.astype(F32) * w_row).astype(BF16)
        return carry

    lax.fori_loop(0, NCH, weights, 0)

    def acc_columns(i, carry):
        at = al(i * E, E)
        acc_b[pl.ds(at, E), :] = jnp.broadcast_to(accum_in[pl.ds(i, 1), :], (E, E)).T
        return carry

    lax.fori_loop(0, ROWS // E, acc_columns, 0, unroll=2)
    loads[2].wait()
    count(0)

    sent_all(rqs, rqr, qs.at[0], qr.at[0]).wait_recv()
    arrived = rqr[:, 0, :]
    for t in range(STEPS):
        cols = [
            jnp.broadcast_to(arrived[:, t * SLOTS + s:t * SLOTS + s + 1], (OWNERS, E))
            for s in range(SLOTS)
        ]
        col = jnp.concatenate(cols, axis=0)
        wcol[t] = col.astype(jnp.int32)
        wrow[t] = col.T[0:8, :].astype(jnp.int32)

    def pick(t):
        def chunk(j, carry):
            lanes = iota((FETCH, E), 1) + j * CH
            want = wcol[t]
            rr[j] = jnp.concatenate([onehot(want == lanes), onehot(want == lanes + E)], axis=1)
            return carry

        lax.fori_loop(0, NROW, chunk, 0)

    def place(t):
        def chunk(j, carry):
            rt[j] = onehot(iota((CH, FETCH), 0) + j * CH == wrow[t][0:1, :])
            return carry

        lax.fori_loop(0, NROW, chunk, 0)

    def put(dst, t, rows):
        for s in range(SLOTS):
            dst[t, :, s, :] = rows[s * OWNERS:(s + 1) * OWNERS]

    def take(src, t):
        return jnp.concatenate([src[t, :, s, :] for s in range(SLOTS)], axis=0)

    pick(0)
    loads[3].wait()
    rows = jnp.zeros((FETCH, E), F32)
    for j in range(NROW):
        rows = rows + nn(rr[j], table[j * CH:(j + 1) * CH, :].astype(BF16))
    put(s1, 0, rows)

    def halves(v):
        hi = v.astype(BF16)
        return jnp.concatenate([hi, (v - hi.astype(F32)).astype(BF16)], axis=1)

    def update_all():
        def chunk(j, carry):
            at = al(j * CH, CH)
            rg = nn(rt[j], back[...])
            rg = rg[:, :E] + rg[:, E:]
            acc = acc_b[pl.ds(at, CH), :] + jnp.mean(rg * rg, axis=1, keepdims=True)
            acc_b[pl.ds(at, CH), :] = acc
            table[pl.ds(at, CH), :] = table[pl.ds(at, CH), :] - learn_rate * rg * lax.rsqrt(acc)
            return carry

        lax.fori_loop(0, NROW, chunk, 0, unroll=UNROLL_ROWS)

    def exact_rows(src):
        def chunk(j, total):
            v = src[pl.ds(al(j * CH, CH), CH), :]
            hi = v.astype(BF16)
            rest = v - hi.astype(F32)
            mid = rest.astype(BF16)
            lo = (rest - mid.astype(F32)).astype(BF16)
            return total + nn(rr[j], jnp.concatenate([hi, mid, lo], axis=1))

        total = lax.fori_loop(0, NROW, chunk, jnp.zeros((FETCH, 3 * E), F32), unroll=UNROLL_ROWS)
        return total[:, :E] + total[:, E:2 * E] + total[:, 2 * E:]

    def prepare(t):
        lane = iota((CH, E), 1)

        def chunk(j, total):
            v = acc_b[pl.ds(al(j * CH, CH), CH), :]
            hi = v.astype(BF16).astype(F32)
            mid = (v - hi).astype(BF16).astype(F32)
            part = jnp.where(lane == 0, hi, jnp.where(lane == 1, mid, v - hi - mid))
            return total + nn(rr[j], part.astype(BF16))

        total = lax.fori_loop(0, NROW, chunk, jnp.zeros((FETCH, E), F32), unroll=UNROLL_ROWS)
        total = total[:, 0:1] + total[:, 1:2] + total[:, 2:3]
        acc_q[...] = jnp.broadcast_to(total, (FETCH, E))
        pick(t + 1)
        base_q[...] = exact_rows(table)

    def pair_up(t):
        row = wrow[t][0:1, :]

        def equal(col, row):
            return jnp.concatenate([onehot(col == row[:, :E]), onehot(col == row[:, E:])], axis=1)

        alike = equal(wcol[t], row)
        same[...] = alike
        earlier = onehot(iota((FETCH, FETCH), 0) < iota((FETCH, FETCH), 1))
        seen = nn(jnp.ones((16, FETCH), BF16), alike * earlier)[0:1, :]
        match[...] = equal(wcol[t + 1], jnp.where(seen > 0.5, -1, row))

    def copy_to(src, dst, send, recv, peer):
        return pltpu.make_async_remote_copy(
            src_ref=src, dst_ref=dst, send_sem=send, recv_sem=recv,
            device_id=peer, device_id_type=pl.DeviceIdType.MESH,
        )

    def rows_copy(t):
        return copy_to(xo.at[t], xw.at[t, 1], fs.at[t, 0], fr.at[t, 0], partner)

    def glow_copy(t):
        return copy_to(glows.at[t], glowp.at[t], fs.at[t, 1], fr.at[t, 1], partner)

    def dlow_copy(t):
        return copy_to(dlows.at[t], dlowp.at[t], fs.at[t, 2], fr.at[t, 2], partner)

    def factors(t):
        return [rows_copy(t), glow_copy(t), dlow_copy(t)]

    def windows(t):
        def one(i, carry):
            to = pl.ds(al(i * GROUP, GROUP), GROUP)
            mine = pl.ds(al((i * BLOCK + HALF * c) // 16 * 16, 16), GROUP)
            other = pl.ds(al((i * BLOCK + HALF * (1 - c)) // 16 * 16, 16), GROUP)
            xw[t, 0, to, :] = x0s[t, mine, :]
            xo[t, to, :] = x0s[t, other, :]
            return carry

        lax.fori_loop(0, NX * NZ, one, 0, unroll=4)
        rows_copy(t).start()

    mi = iota((CH, CH), 0)
    m_in = lax.rem(mi, 16)
    m_off = lax.rem(mi // GROUP, 2) * 8 + 4 * c
    m_col = mi // GROUP * GROUP + m_off + lax.rem(mi // 16, NY) * SHARE + m_in
    spots = onehot((m_col == iota((CH, CH), 1)) & (m_in < SHARE))

    def cut(h):
        return pl.ds(h * (NZ // 2) * 16, (NZ // 2) * 16)

    def stage_x(k, h):
        return copy_to(
            sa.at[k, :, cut(h)], ra.at[k - 1, :, cut(h)], xs.at[k, h], xr.at[k, h], xpeer(k)[1]
        )

    def stage_y(i, k, h):
        py, d = ypeer(k)
        return copy_to(
            sb.at[py, i, cut(h)], rb.at[k - 1, i, cut(h)], ys.at[i, k, h], yr.at[i, k, h], d
        )

    def stage_y2(k, h):
        py, d = ypeer(k)
        return copy_to(a2.at[py, cut(h)], ra2.at[k - 1, cut(h)], y2s.at[k, h], y2r.at[k, h], d)

    def stage_x2(k, h):
        return copy_to(
            b2.at[k, cut(h)], rb2.at[k - 1, cut(h)], x2s.at[k, h], x2r.at[k, h], xpeer(k)[1]
        )

    def z_copy(k, zt):
        return copy_to(
            z3.at[pl.ds(al(zt * 16, 16), 16)], rz.at[z], zs.at[k], zr.at[z], dev(x, zt, c, y)
        )

    def bo_core():
        return copy_to(bo.at[0], boc, bcs, bcr, partner)

    def bo_x(k):
        px, d = xpeer(k)
        return copy_to(bw.at[px], bwx.at[k - 1], bxs.at[k], bxr.at[k], d)

    def bo_y(k):
        return copy_to(bv.at[0], bvy.at[k - 1], bys.at[k], byr.at[k], ypeer(k)[1])

    def bo_z(k):
        return copy_to(bv.at[1], bvz.at[k - 1], bzs.at[k], bzr.at[k], zpeer(k)[1])

    def dense():
        for t in range(STEPS):
            for copy in factors(t):
                copy.wait_recv()
        right = jnp.concatenate([
            jnp.concatenate([r[t] for t in range(STEPS) for r in (dlows, dlowp)], axis=1),
            jnp.concatenate([r[t] for t in range(STEPS) for r in (glows, glowp)], axis=1),
        ], axis=0)
        for h in range(2):
            for i in range(NX):
                px = at_x[ORDER[i]]
                rows = pl.ds(al((px * 2 + h) * CH, CH), CH)
                xx = jnp.concatenate([xw[t, p, rows, :] for t in range(STEPS) for p in range(2)], axis=1)
                g = nn(spots, nt(xx, right).astype(BF16)).astype(BF16)
                for zl in range(NZ // 2):
                    to = (h * (NZ // 2) + zl) * 16
                    for py in range(NY):
                        at = (zl * NY + py) * 16
                        sa[ORDER[i], py, to:to + 16, :] = g[at:at + 16, :RANK]
                        sb[py, ORDER[i], to:to + 16, :] = g[at:at + 16, RANK:]
                if ORDER[i]:
                    stage_x(ORDER[i], h).start()
                for k in (2, 1, 3):
                    stage_y(ORDER[i], k, h).start()

    def sums():
        head = jnp.concatenate([heads[t] for t in range(STEPS)], axis=1)
        bo[...] = jnp.zeros_like(bo)
        for i in range(NCH):
            at = i * CH
            b_rows = nt(head, jnp.concatenate([x0s[t, at:at + CH, :] for t in range(STEPS)], axis=1))
            o_rows = nt(head, jnp.concatenate([x1s[t, at:at + CH, :] for t in range(STEPS)], axis=1))
            b_row = b_rows[0:1, :] + b_rows[1:2, :] + b_rows[2:3, :]
            o_row = o_rows[0:1, :] + o_rows[1:2, :] + o_rows[2:3, :]
            for h in range(2):
                k = 2 * i + h
                bo[0, k:k + 1, :] = b_row[:, h * E:(h + 1) * E] * outf[k:k + 1, :]
                bo[0, 32 + k:33 + k, :] = o_row[:, h * E:(h + 1) * E]
        bo_core().start()
        bo_core().wait()
        both = bo[0] + boc[...]
        bo[1] = both
        for px in range(NX):
            first = px * XROWS // E
            bw[px, 0:8, :] = bo[1, first:first + 8, :]
            bw[px, 8:16, :] = bo[1, 32 + first:40 + first, :]
        for k in range(1, NX):
            bo_x(k).start()

    def second():
        for k in range(1, NX):
            bo_x(k).wait()
        bv[0] = bw[x] + bwx[0] + bwx[1] + bwx[2]
        for k in range(1, NY):
            bo_y(k).start()
        first(0)

    def first(h):
        for k in range(1, NX):
            stage_x(k, h).wait()
        for py in range(NY):
            a2[py, cut(h)] = (
                sa[0, py, cut(h)].astype(F32)
                + ra[0, py, cut(h)].astype(F32) + ra[1, py, cut(h)].astype(F32)
                + ra[2, py, cut(h)].astype(F32)
            ).astype(BF16)
        for k in (2, 1, 3):
            stage_y2(k, h).start()
        for i in ORDER:
            for k in range(1, NY):
                stage_y(i, k, h).wait()
            b2[i, cut(h)] = (
                sb[y, i, cut(h)].astype(F32)
                + rb[0, i, cut(h)].astype(F32) + rb[1, i, cut(h)].astype(F32)
                + rb[2, i, cut(h)].astype(F32)
            ).astype(BF16)
            if i:
                stage_x2(i, h).start()

    def third(h):
        for k in range(1, NY):
            stage_y2(k, h).wait()
        for k in range(1, NX):
            stage_x2(k, h).wait()
        z3[cut(h), :RANK] = (
            a2[y, cut(h)].astype(F32) + ra2[0, cut(h)].astype(F32) + ra2[1, cut(h)].astype(F32)
            + ra2[2, cut(h)].astype(F32)
        ).astype(BF16)
        z3[cut(h), RANK:] = (
            b2[0, cut(h)].astype(F32) + rb2[0, cut(h)].astype(F32) + rb2[1, cut(h)].astype(F32)
            + rb2[2, cut(h)].astype(F32)
        ).astype(BF16)
        for k in range(NZ // 2):
            zt = h * (NZ // 2) + k

            @pl.when(zt != z)
            def _():
                z_copy(zt, zt).start()

            @pl.when(zt == z)
            def _():
                rz[z] = z3[zt * 16:zt * 16 + 16, :]

    def step(t, carry):
        send_all(s1.at[t], r1.at[t], s1s.at[t], s1r.at[t])
        r1[t, owner] = s1[t, owner]

        @pl.when(t > 0)
        def _():
            update_all()

        place(t)

        @pl.when(t < STEPS - 1)
        def _():
            prepare(t)

        cur = lax.rem(t, 2)
        sent_all(s1.at[t], r1.at[t], s1s.at[t], s1r.at[t]).wait_recv()
        fetched_t = nt(eye_e, take(r1, t).astype(BF16)).astype(BF16)

        def pool(i, carry):
            xx = nn(fetched_t, counts[cur, i]).astype(BF16)
            at = al(i * CH, CH)
            x0s[t, pl.ds(at, E), :] = xx[:, :TOK]
            x0s[t, pl.ds(al(at + E, E), E), :] = xx[:, TOK:]
            return carry

        def project(i, total):
            at = al(i * CH, CH)
            return total + nn(both_t[:, pl.ds(at, CH)], x0s[t, pl.ds(at, CH), :])

        lax.fori_loop(0, NCH, pool, 0, unroll=UNROLL)
        total = lax.fori_loop(0, NCH, project, jnp.zeros((2 * RANK, TOK), F32), unroll=UNROLL)
        low = total[:RANK].astype(BF16)
        v = total[RANK:]
        vb = v.astype(BF16)

        @pl.when(t == STEPS - 1)
        def _():
            windows(t)

        def forward(i, logit):
            at = al(i * CH, CH)
            gate = nn(up_t[pl.ds(at, CH), :], low) + bias_b[pl.ds(at, CH), :]
            x0f = x0s[t, pl.ds(at, CH), :].astype(F32)
            w = out_b[pl.ds(at, CH), :]
            us[pl.ds(at, CH), :] = w * (gate + 1.0) + nn(down[pl.ds(at, CH), :], vb)
            x1 = (x0f * gate + x0f).astype(BF16)
            x1s[t, pl.ds(at, CH), :] = x1
            return logit + jnp.sum((x1.astype(F32) * w).reshape(CH // 8, 8, TOK), axis=0)

        logit = lax.fori_loop(0, NCH, forward, jnp.zeros((8, TOK), F32), unroll=UNROLL)
        logit = jnp.sum(logit, axis=0, keepdims=True)
        dlogit = jax.nn.sigmoid(logit) - labels[pl.ds(t, 1), :].astype(F32)
        dhi = dlogit.astype(BF16).astype(F32)
        dmid = (dlogit - dhi).astype(BF16).astype(F32)
        dlo = dlogit - dhi - dmid
        sub = iota((16, TOK), 0)
        split = jnp.where(sub == 0, dhi, jnp.where(sub == 1, dmid, jnp.where(sub == 2, dlo, 0.0)))
        heads[t] = split.astype(BF16)
        dlows[t] = (dlogit * v).astype(BF16)
        glows[t] = (dlogit * low.astype(F32)).astype(BF16)
        dlow_copy(t).start()
        glow_copy(t).start()

        def spread(i, gf):
            at = al(i * CH, CH)
            dx0 = (dlogit * us[pl.ds(at, CH), :]).astype(BF16)
            both = jnp.concatenate([dx0[:E], dx0[E:]], axis=1)
            return gf + nt(counts[cur, i], both)

        put(g1, t, lax.fori_loop(0, NCH, spread, jnp.zeros((FETCH, E), F32), unroll=UNROLL))
        send_all(g1.at[t], g2.at[t], g1s.at[t], g1r.at[t])
        g2[t, owner] = g1[t, owner]

        @pl.when(t < STEPS - 1)
        def _():
            pair_up(t)
            count(t + 1)
            windows(t)

        @pl.when(t == STEPS - 1)
        def _():
            dense()
            sums()

        sent_all(g1.at[t], g2.at[t], g1s.at[t], g1r.at[t]).wait_recv()
        pair = halves(take(g2, t))
        back[...] = pair

        @pl.when(t < STEPS - 1)
        def _():
            rg = nn(same[...], pair)
            rg = rg[:, :E] + rg[:, E:]
            acc = acc_q[...] + jnp.mean(rg * rg, axis=1, keepdims=True)
            moved = nn(match[...], halves(learn_rate * rg * lax.rsqrt(acc)))
            put(s1, t + 1, base_q[...] - (moved[:, :E] + moved[:, E:]))

        return carry

    lax.fori_loop(0, STEPS, step, 0)
    second()
    update_all()

    store = pltpu.make_async_copy(table, table_hbm, lsem.at[0])
    store.start()

    def acc_rows(i, carry):
        at = al(i * E, E)
        accum_out[pl.ds(i, 1), :] = acc_b[pl.ds(at, E), :].T[0:1, :]
        return carry

    lax.fori_loop(0, ROWS // E, acc_rows, 0)

    first(1)
    for k in range(1, NY):
        bo_y(k).wait()
    bv[1] = bv[0] + bvy[0] + bvy[1] + bvy[2]
    for k in range(1, NZ):
        bo_z(k).start()
    third(0)
    third(1)

    scale = 1.0 / (STEPS * TOK * NX * NY * NZ * NC)
    for k in range(1, NZ):
        bo_z(k).wait()
    total = bv[1]
    for k in range(NZ - 1):
        total = total + bvz[k]
    bv[2] = total * scale
    start = (owner * NY + y) * SHARE - (x * XROWS // E) * E
    a = start // E
    rows = []
    for base in (0, 8):
        pair = jnp.concatenate([bv[2, pl.ds(base + a, 1), :], bv[2, pl.ds(lax.rem(base + a + 1, 16), 1), :]], axis=1)
        pair = jnp.broadcast_to(pair, (8, 2 * E))
        rows.append(pltpu.roll(pair, lax.rem(2 * E - lax.rem(start, E), 2 * E), 1)[:, 0:E])
    bo_out[...] = jnp.where(iota((8, E), 0) == 0, rows[0], rows[1])

    for k in range(NZ):
        @pl.when(k != z)
        def _():
            copy_to(z3.at[pl.ds(0, 16)], rz.at[k], zs.at[0], zr.at[k], partner).wait_recv()
            z_copy(k, k).wait_send()
    total = rz[0].astype(F32)
    for k in range(1, NZ):
        total = total + rz[k].astype(F32)
    own = owner * NY + y
    w = out_b[pl.ds(own * SHARE, 16), :]
    gdu_out[:, :RANK] = total[:, :RANK] * scale
    gdu_out[:, RANK:] = total[:, RANK:] * scale * jnp.concatenate([w, w], axis=1)

    for t in range(STEPS):
        for copy in factors(t):
            copy.wait_send()
    sent_all(rqs, rqr, qs.at[0], qr.at[0]).wait_send()
    for t in range(STEPS):
        sent_all(s1.at[t], r1.at[t], s1s.at[t], s1r.at[t]).wait_send()
        sent_all(g1.at[t], g2.at[t], g1s.at[t], g1r.at[t]).wait_send()
    store.wait()


def finish(table_in, accum_in, gdu, bo, table, accum, down, up, bias, outw, sem):
    rows = ROWS // 8
    copies = [
        pltpu.make_async_copy(table_in.at[pl.ds(n * rows, rows)], table.at[pl.ds(n * rows, rows)], sem.at[n])
        for n in range(8)
    ]
    for copy in copies:
        copy.start()
    accum[...] = accum_in[...]
    down[...] = gdu[0:SHARE, :RANK]
    up[...] = gdu[0:SHARE, RANK:]
    bias[...] = bo[0:1, 0:SHARE]
    outw[...] = bo[1:2, 0:SHARE]
    for copy in copies:
        copy.wait()


def local(table, accum, requests, members, labels, down_proj, up_proj, cross_bias, out_weight):
    reqs = jnp.transpose(requests[:, 0, 0], (0, 2, 1))
    mem = jnp.transpose(members, (0, 2, 3, 1)).reshape(STEPS, NB * BAGLEN, TOK)
    dma = pltpu.SemaphoreType.DMA
    vm = pltpu.VMEM
    scratch = [
        vm((ROWS, E), F32), vm((STEPS, NB * BAGLEN, TOK), jnp.int32),
        vm((D_IN, RANK), BF16), vm((RANK, D_IN), BF16),
        vm((OWNERS, 1, E), F32), vm((OWNERS, 1, E), F32),
        vm((FETCH, E), F32), vm((FETCH, E), F32),
        vm((FETCH, FETCH), BF16), vm((FETCH, FETCH), BF16), vm((FETCH, 2 * E), BF16),
        vm((STEPS, FETCH, E), jnp.int32), vm((STEPS, 8, FETCH), jnp.int32),
        vm((STEPS + 1, OWNERS, SLOTS, E), F32),
    ]
    scratch += [vm((STEPS, OWNERS, SLOTS, E), F32)] * 3
    scratch += [
        vm((NROW, FETCH, CH), BF16), vm((NROW, CH, FETCH), BF16),
        vm((E, E), F32), vm((NB, E), F32), vm((2 * RANK, D_IN), BF16), vm((D_IN, RANK), BF16),
        vm((D_IN, TOK), F32), vm((D_IN + 16, TOK), F32), vm((ROWS, E), F32), vm((FETCH, E), jnp.int32),
        vm((2, NCH, FETCH, 2 * TOK), BF16),
        vm((STEPS, D_IN, TOK), BF16),
        vm((STEPS, RANK, TOK), BF16), vm((STEPS, RANK, TOK), BF16),
        vm((D_IN, TOK), F32), vm((STEPS, D_IN, TOK), BF16), vm((STEPS, 16, TOK), BF16),
        vm((STEPS, 2, CORE_ROWS, TOK), BF16), vm((STEPS, CORE_ROWS, TOK), BF16),
        vm((STEPS, RANK, TOK), BF16), vm((STEPS, RANK, TOK), BF16),
        vm((NX, NY, NZ * 16, RANK), BF16), vm((NX - 1, NY, NZ * 16, RANK), BF16),
        vm((NY, NX, NZ * 16, RANK), BF16), vm((NY - 1, NX, NZ * 16, RANK), BF16),
        vm((NY, NZ * 16, RANK), BF16), vm((NY - 1, NZ * 16, RANK), BF16),
        vm((NX, NZ * 16, RANK), BF16), vm((NX - 1, NZ * 16, RANK), BF16),
        vm((NZ * 16, 2 * RANK), BF16), vm((NZ, 16, 2 * RANK), BF16),
        vm((2, 64, E), F32), vm((64, E), F32),
        vm((NX, 16, E), F32), vm((NX - 1, 16, E), F32), vm((3, 16, E), F32),
        vm((NY - 1, 16, E), F32), vm((NZ - 1, 16, E), F32),
    ]
    scratch += [dma((4,)), dma((1,)), dma((1,))]
    scratch += [dma((STEPS,))] * 4
    scratch += [dma((STEPS, 4))] * 2
    scratch += [dma((NX, 2))] * 2
    scratch += [dma((NX, NY, 2))] * 2
    scratch += [dma((NX, 2))] * 4
    scratch += [dma((NZ,))] * 2
    scratch += [dma] * 2
    scratch += [dma((8,))] * 6
    hbm = pl.BlockSpec(memory_space=pl.ANY)
    spec = pl.BlockSpec(memory_space=pltpu.VMEM)
    table_new, accum_new, gdu, bo = pl.pallas_call(
        kernel,
        out_shape=(
            jax.ShapeDtypeStruct((ROWS, E), F32),
            jax.ShapeDtypeStruct((ROWS // E, E), F32),
            jax.ShapeDtypeStruct((16, 2 * RANK), F32),
            jax.ShapeDtypeStruct((8, E), F32),
        ),
        in_specs=[hbm, spec, spec, hbm, spec, hbm, hbm, spec, spec],
        out_specs=(hbm, spec, spec, spec),
        scratch_shapes=scratch,
        compiler_params=pltpu.CompilerParams(
            collective_id=0, has_side_effects=True, vmem_limit_bytes=58 * 1024 * 1024
        ),
    )(
        table, accum.reshape(ROWS // E, E), reqs, mem, labels, down_proj, up_proj,
        cross_bias.reshape(NB, E), out_weight.reshape(NB, E),
    )
    table_out, accum_out, down, up, bias, outw = pl.pallas_call(
        finish,
        out_shape=(
            jax.ShapeDtypeStruct((ROWS, E), F32),
            jax.ShapeDtypeStruct((ROWS // E, E), F32),
            jax.ShapeDtypeStruct((SHARE, RANK), F32),
            jax.ShapeDtypeStruct((SHARE, RANK), F32),
            jax.ShapeDtypeStruct((1, SHARE), F32),
            jax.ShapeDtypeStruct((1, SHARE), F32),
        ),
        in_specs=[hbm, spec, spec, spec],
        out_specs=(spec, spec, spec, spec, spec, spec),
        scratch_shapes=[dma((8,))],
    )(table_new, accum_new, gdu, bo)
    return (table_out, accum_out.reshape(ROWS), down, up.T, bias[0], outw[0])


def solution(mesh):
    both = ("owner", "group")
    in_specs = (
        P(both, None), P(both), P(None, "owner", "group", None, None),
        P(None, both, None, None), P(None, both), P(), P(), P(), P(),
    )
    out_specs = (P(both, None), P(both), P(both, None), P(None, both), P(both), P(both))
    return jax.shard_map(local, mesh=mesh, in_specs=in_specs, out_specs=out_specs, check_vma=False)
```

```python
import functools

import jax
import jax.numpy as jnp
from jax import lax
from jax.experimental import pallas as pl
from jax.experimental.pallas import tpu as pltpu
from jax.sharding import PartitionSpec as P

NX, NY, NZ, NC = 4, 4, 8, 2
OWNERS = NX * NZ * NC
NB = 26
BAGLEN = 4
STEPS = 3
E = 128
TOK = 128
RANK = 256
D_IN = NB * E
ROWS = 2048
SLOTS = 4
FETCH = OWNERS * SLOTS
CH = 256
NCH = D_IN // CH
NROW = ROWS // CH
UNROLL = 13
ORDER = (2, 1, 3, 0)
UNROLL_ROWS = 8
XROWS = D_IN // NX
BLOCK = XROWS // NZ
HALF = BLOCK // NC
GROUP = 64
CORE_ROWS = NX * NZ * GROUP
SHARE = 13

learn_rate = 0.05
F32 = jnp.float32
BF16 = jnp.bfloat16


def nn(a, b):
    return jnp.dot(a, b, preferred_element_type=F32)


def nt(a, b):
    return lax.dot_general(a, b, (((1,), (1,)), ((), ())), preferred_element_type=F32)


def iota(shape, dim):
    return lax.broadcasted_iota(jnp.int32, shape, dim)


def onehot(mask):
    return jnp.where(mask, 1.0, 0.0).astype(BF16)


def al(value, step):
    return pl.multiple_of(value, step)


def remote(src, dst, send, recv, dev):
    copy = pltpu.make_async_remote_copy(
        src_ref=src, dst_ref=dst, send_sem=send, recv_sem=recv,
        device_id=dev, device_id_type=pl.DeviceIdType.MESH,
    )
    copy.start()
    return copy


def wait_all(copies):
    for copy in copies:
        copy.wait()


def kernel(
    table_in, accum_in, reqs, mem_in, labels, down_in, up_in, bias, outw,
    table_hbm, accum_out, gdu_out, bo_out,
    table, mem, down, up,
    rqs, rqr, acc_q, base_q, same, match, back, wcol, wrow, s1, r1, g1, g2, rr, rt,
    rpad, outf, both_t, up_t, bias_b, out_b, acc_b, posq,
    counts, x0s, glows, dlows, us, x1s, heads,
    xw, xo, glowp, dlowp, sa, ra, sb, rb, a2, ra2, b2, rb2, z3, rz,
    bo, boc, bw, bwx, bv, bvy, bvz,
    lsem, qs, qr, s1s, s1r, g1s, g1r,
    fs, fr, xs, xr, ys, yr, x2s, x2r, y2s, y2r, zs, zr,
    bcs, bcr, bxs, bxr, bys, byr, bzs, bzr,
):
    loads = [
        pltpu.make_async_copy(src, dst, lsem.at[n])
        for n, (src, dst) in enumerate(
            ((down_in, down), (up_in, up), (mem_in, mem), (table_in, table))
        )
    ]
    for load in loads:
        load.start()

    owner = lax.axis_index("owner")
    y = lax.axis_index("group")
    c = lax.rem(owner, NC)
    z = lax.rem(owner // NC, NZ)
    x = owner // (NC * NZ)
    at_x = [lax.rem(x + k, NX) for k in range(NX)]
    at_z = [lax.rem(z + k, NZ) for k in range(NZ)]
    at_y = [lax.rem(y + k, NY) for k in range(NY)]
    at_c = [c, 1 - c]

    def dev(px, pz, pc, py):
        return ((px * NZ + pz) * NC + pc, py)

    def zpeer(k):
        return at_z[k], dev(x, at_z[k], c, y)

    def xpeer(k):
        return at_x[k], dev(at_x[k], z, c, y)

    def ypeer(k):
        return at_y[k], dev(x, z, c, at_y[k])

    partner = dev(x, z, 1 - c, y)
    far = [
        (dx, dz, dc) for dx in range(NX) for dz in range(NZ) for dc in range(NC) if dx or dz or dc
    ]
    far.sort(key=lambda d: -(min(d[0], NX - d[0]) + min(d[1], NZ - d[1])))
    users = [dev(at_x[dx], at_z[dz], at_c[dc], y) for dx, dz, dc in far]

    barrier = pltpu.get_barrier_semaphore()
    greet = users + [dev(x, z, at_c[h], at_y[k]) for h in range(NC) for k in range(1, NY)]
    for peer in greet:
        pl.semaphore_signal(barrier, inc=1, device_id=peer, device_id_type=pl.DeviceIdType.MESH)

    def send_all(src, dst, ssem, rsem):
        for peer in users:
            remote(src.at[peer[0]], dst.at[owner], ssem, rsem, peer)

    def sent_all(src, dst, ssem, rsem):
        most = pl.ds(0, NX * NZ * NC - 1)
        return pltpu.make_async_remote_copy(
            src_ref=src.at[most], dst_ref=dst.at[most], send_sem=ssem, recv_sem=rsem,
            device_id=partner, device_id_type=pl.DeviceIdType.MESH,
        )

    rpad[...] = jnp.zeros_like(rpad)
    for t in range(STEPS):
        rpad[t * SLOTS:(t + 1) * SLOTS, 0:OWNERS] = reqs[t].astype(F32)
    flat = rpad[...].T
    rqs[:, 0, :] = flat[0:OWNERS]
    outf[...] = outw[...].astype(F32)
    out_b[D_IN:, :] = jnp.zeros((16, E), F32)

    def columns(i, carry):
        at = al(i * E, E)
        bias_b[pl.ds(at, E), :] = jnp.broadcast_to(bias[pl.ds(i, 1), :], (E, E)).T
        out_b[pl.ds(at, E), :] = jnp.broadcast_to(outf[pl.ds(i, 1), :], (E, E)).T
        return carry

    lax.fori_loop(0, NB, columns, 0, unroll=2)

    qi = iota((FETCH, E), 0)
    posq[...] = lax.rem(qi, OWNERS) * SLOTS + qi // OWNERS
    eye = onehot(iota((CH, CH), 0) == iota((CH, CH), 1))
    eye_e = onehot(iota((E, E), 0) == iota((E, E), 1))

    pl.semaphore_wait(barrier, len(greet))
    send_all(rqs, rqr, qs.at[0], qr.at[0])
    rqr[owner] = rqs[owner]

    def count(t):
        def bags(i, carry):
            rows = mem[t, pl.ds(al(i * 8, 8), 8), :]
            pos = posq[...]
            cnt = []
            for b in range(2):
                n = jnp.where(pos == rows[4 * b:4 * b + 1, :], 1.0, 0.0)
                for m in range(1, BAGLEN):
                    n = n + jnp.where(pos == rows[4 * b + m:4 * b + m + 1, :], 1.0, 0.0)
                cnt.append(n.astype(BF16))
            counts[lax.rem(t, 2), i] = jnp.concatenate(cnt, axis=1)
            return carry

        lax.fori_loop(0, NCH, bags, 0, unroll=UNROLL)

    loads[0].wait()
    loads[1].wait()

    def weights(i, carry):
        at = al(i * CH, CH)
        both_t[0:RANK, pl.ds(at, CH)] = nt(eye, down[pl.ds(at, CH), :]).astype(BF16)
        up_c = up[:, pl.ds(at, CH)]
        up_t[pl.ds(at, CH), :] = nt(eye, up_c).astype(BF16)
        w_row = jnp.concatenate([outf[pl.ds(2 * i, 1), :], outf[pl.ds(2 * i + 1, 1), :]], axis=1)
        both_t[RANK:, pl.ds(at, CH)] = (up_c.astype(F32) * w_row).astype(BF16)
        return carry

    lax.fori_loop(0, NCH, weights, 0, unroll=UNROLL)

    def acc_columns(i, carry):
        at = al(i * E, E)
        acc_b[pl.ds(at, E), :] = jnp.broadcast_to(accum_in[pl.ds(i, 1), :], (E, E)).T
        return carry

    lax.fori_loop(0, ROWS // E, acc_columns, 0, unroll=2)
    loads[2].wait()
    count(0)

    sent_all(rqs, rqr, qs.at[0], qr.at[0]).wait_recv()
    arrived = rqr[:, 0, :]
    for t in range(STEPS):
        cols = [
            jnp.broadcast_to(arrived[:, t * SLOTS + s:t * SLOTS + s + 1], (OWNERS, E))
            for s in range(SLOTS)
        ]
        col = jnp.concatenate(cols, axis=0)
        wcol[t] = col.astype(jnp.int32)
        wrow[t] = col.T[0:8, :].astype(jnp.int32)

    def pick(t):
        def chunk(j, carry):
            lanes = iota((FETCH, E), 1) + j * CH
            want = wcol[t]
            rr[j] = jnp.concatenate([onehot(want == lanes), onehot(want == lanes + E)], axis=1)
            return carry

        lax.fori_loop(0, NROW, chunk, 0, unroll=NROW)

    def place(t):
        def chunk(j, carry):
            rt[j] = onehot(iota((CH, FETCH), 0) + j * CH == wrow[t][0:1, :])
            return carry

        lax.fori_loop(0, NROW, chunk, 0, unroll=NROW)

    def put(dst, t, rows):
        for s in range(SLOTS):
            dst[t, :, s, :] = rows[s * OWNERS:(s + 1) * OWNERS]

    def take(src, t):
        return jnp.concatenate([src[t, :, s, :] for s in range(SLOTS)], axis=0)

    pick(0)
    loads[3].wait()
    rows = jnp.zeros((FETCH, E), F32)
    for j in range(NROW):
        rows = rows + nn(rr[j], table[j * CH:(j + 1) * CH, :].astype(BF16))
    put(s1, 0, rows)

    def halves(v):
        hi = v.astype(BF16)
        return jnp.concatenate([hi, (v - hi.astype(F32)).astype(BF16)], axis=1)

    def update_all():
        def chunk(j, carry):
            at = al(j * CH, CH)
            rg = nn(rt[j], back[...])
            rg = rg[:, :E] + rg[:, E:]
            acc = acc_b[pl.ds(at, CH), :] + jnp.mean(rg * rg, axis=1, keepdims=True)
            acc_b[pl.ds(at, CH), :] = acc
            table[pl.ds(at, CH), :] = table[pl.ds(at, CH), :] - learn_rate * rg * lax.rsqrt(acc)
            return carry

        lax.fori_loop(0, NROW, chunk, 0, unroll=UNROLL_ROWS)

    def exact_rows(src):
        def chunk(j, total):
            v = src[pl.ds(al(j * CH, CH), CH), :]
            hi = v.astype(BF16)
            rest = v - hi.astype(F32)
            mid = rest.astype(BF16)
            lo = (rest - mid.astype(F32)).astype(BF16)
            return total + nn(rr[j], jnp.concatenate([hi, mid, lo], axis=1))

        total = lax.fori_loop(0, NROW, chunk, jnp.zeros((FETCH, 3 * E), F32), unroll=UNROLL_ROWS)
        return total[:, :E] + total[:, E:2 * E] + total[:, 2 * E:]

    def prepare(t):
        lane = iota((CH, E), 1)

        def chunk(j, total):
            v = acc_b[pl.ds(al(j * CH, CH), CH), :]
            hi = v.astype(BF16).astype(F32)
            mid = (v - hi).astype(BF16).astype(F32)
            part = jnp.where(lane == 0, hi, jnp.where(lane == 1, mid, v - hi - mid))
            return total + nn(rr[j], part.astype(BF16))

        total = lax.fori_loop(0, NROW, chunk, jnp.zeros((FETCH, E), F32), unroll=UNROLL_ROWS)
        total = total[:, 0:1] + total[:, 1:2] + total[:, 2:3]
        acc_q[...] = jnp.broadcast_to(total, (FETCH, E))
        pick(t + 1)
        base_q[...] = exact_rows(table)

    def pair_up(t):
        row = wrow[t][0:1, :]

        def equal(col, row):
            return jnp.concatenate([onehot(col == row[:, :E]), onehot(col == row[:, E:])], axis=1)

        alike = equal(wcol[t], row)
        same[...] = alike
        earlier = onehot(iota((FETCH, FETCH), 0) < iota((FETCH, FETCH), 1))
        seen = nn(jnp.ones((16, FETCH), BF16), alike * earlier)[0:1, :]
        match[...] = equal(wcol[t + 1], jnp.where(seen > 0.5, -1, row))

    def copy_to(src, dst, send, recv, peer):
        return pltpu.make_async_remote_copy(
            src_ref=src, dst_ref=dst, send_sem=send, recv_sem=recv,
            device_id=peer, device_id_type=pl.DeviceIdType.MESH,
        )

    def rows_copy(t):
        return copy_to(xo.at[t], xw.at[t, 1], fs.at[t, 0], fr.at[t, 0], partner)

    def glow_copy(t):
        return copy_to(glows.at[t], glowp.at[t], fs.at[t, 1], fr.at[t, 1], partner)

    def dlow_copy(t):
        return copy_to(dlows.at[t], dlowp.at[t], fs.at[t, 2], fr.at[t, 2], partner)

    def factors(t):
        return [rows_copy(t), glow_copy(t), dlow_copy(t)]

    def windows(t):
        def one(i, carry):
            to = pl.ds(al(i * GROUP, GROUP), GROUP)
            mine = pl.ds(al((i * BLOCK + HALF * c) // 16 * 16, 16), GROUP)
            other = pl.ds(al((i * BLOCK + HALF * (1 - c)) // 16 * 16, 16), GROUP)
            xw[t, 0, to, :] = x0s[t, mine, :]
            xo[t, to, :] = x0s[t, other, :]
            return carry

        lax.fori_loop(0, NX * NZ, one, 0, unroll=4)
        rows_copy(t).start()

    mi = iota((CH, CH), 0)
    m_in = lax.rem(mi, 16)
    m_off = lax.rem(mi // GROUP, 2) * 8 + 4 * c
    m_col = mi // GROUP * GROUP + m_off + lax.rem(mi // 16, NY) * SHARE + m_in
    spots = onehot((m_col == iota((CH, CH), 1)) & (m_in < SHARE))

    def cut(h):
        return pl.ds(h * (NZ // 2) * 16, (NZ // 2) * 16)

    def stage_x(k, h):
        return copy_to(
            sa.at[k, :, cut(h)], ra.at[k - 1, :, cut(h)], xs.at[k, h], xr.at[k, h], xpeer(k)[1]
        )

    def stage_y(i, k, h):
        py, d = ypeer(k)
        return copy_to(
            sb.at[py, i, cut(h)], rb.at[k - 1, i, cut(h)], ys.at[i, k, h], yr.at[i, k, h], d
        )

    def stage_y2(k, h):
        py, d = ypeer(k)
        return copy_to(a2.at[py, cut(h)], ra2.at[k - 1, cut(h)], y2s.at[k, h], y2r.at[k, h], d)

    def stage_x2(k, h):
        return copy_to(
            b2.at[k, cut(h)], rb2.at[k - 1, cut(h)], x2s.at[k, h], x2r.at[k, h], xpeer(k)[1]
        )

    def z_copy(k, zt):
        return copy_to(
            z3.at[pl.ds(al(zt * 16, 16), 16)], rz.at[z], zs.at[k], zr.at[z], dev(x, zt, c, y)
        )

    def bo_core():
        return copy_to(bo.at[0], boc, bcs, bcr, partner)

    def bo_x(k):
        px, d = xpeer(k)
        return copy_to(bw.at[px], bwx.at[k - 1], bxs.at[k], bxr.at[k], d)

    def bo_y(k):
        return copy_to(bv.at[0], bvy.at[k - 1], bys.at[k], byr.at[k], ypeer(k)[1])

    def bo_z(k):
        return copy_to(bv.at[1], bvz.at[k - 1], bzs.at[k], bzr.at[k], zpeer(k)[1])

    def dense():
        for t in range(STEPS):
            for copy in factors(t):
                copy.wait_recv()
        right = jnp.concatenate([
            jnp.concatenate([r[t] for t in range(STEPS) for r in (dlows, dlowp)], axis=1),
            jnp.concatenate([r[t] for t in range(STEPS) for r in (glows, glowp)], axis=1),
        ], axis=0)
        for h in range(2):
            for i in range(NX):
                px = at_x[ORDER[i]]
                rows = pl.ds(al((px * 2 + h) * CH, CH), CH)
                xx = jnp.concatenate([xw[t, p, rows, :] for t in range(STEPS) for p in range(2)], axis=1)
                g = nn(spots, nt(xx, right).astype(BF16)).astype(BF16)
                for zl in range(NZ // 2):
                    to = (h * (NZ // 2) + zl) * 16
                    for py in range(NY):
                        at = (zl * NY + py) * 16
                        sa[ORDER[i], py, to:to + 16, :] = g[at:at + 16, :RANK]
                        sb[py, ORDER[i], to:to + 16, :] = g[at:at + 16, RANK:]
                if ORDER[i]:
                    stage_x(ORDER[i], h).start()
                for k in (2, 1, 3):
                    stage_y(ORDER[i], k, h).start()

    def sums():
        head = jnp.concatenate([heads[t] for t in range(STEPS)], axis=1)
        bo[...] = jnp.zeros_like(bo)
        for i in range(NCH):
            at = i * CH
            b_rows = nt(head, jnp.concatenate([x0s[t, at:at + CH, :] for t in range(STEPS)], axis=1))
            o_rows = nt(head, jnp.concatenate([x1s[t, at:at + CH, :] for t in range(STEPS)], axis=1))
            b_row = b_rows[0:1, :] + b_rows[1:2, :] + b_rows[2:3, :]
            o_row = o_rows[0:1, :] + o_rows[1:2, :] + o_rows[2:3, :]
            for h in range(2):
                k = 2 * i + h
                bo[0, k:k + 1, :] = b_row[:, h * E:(h + 1) * E] * outf[k:k + 1, :]
                bo[0, 32 + k:33 + k, :] = o_row[:, h * E:(h + 1) * E]
        bo_core().start()
        bo_core().wait()
        both = bo[0] + boc[...]
        bo[1] = both
        for px in range(NX):
            first = px * XROWS // E
            bw[px, 0:8, :] = bo[1, first:first + 8, :]
            bw[px, 8:16, :] = bo[1, 32 + first:40 + first, :]
        for k in range(1, NX):
            bo_x(k).start()

    def second():
        for k in range(1, NX):
            bo_x(k).wait()
        bv[0] = bw[x] + bwx[0] + bwx[1] + bwx[2]
        for k in range(1, NY):
            bo_y(k).start()
        first(0)

    def first(h):
        for k in range(1, NX):
            stage_x(k, h).wait()
        for py in range(NY):
            a2[py, cut(h)] = (
                sa[0, py, cut(h)].astype(F32)
                + ra[0, py, cut(h)].astype(F32) + ra[1, py, cut(h)].astype(F32)
                + ra[2, py, cut(h)].astype(F32)
            ).astype(BF16)
        for k in (2, 1, 3):
            stage_y2(k, h).start()
        for i in ORDER:
            for k in range(1, NY):
                stage_y(i, k, h).wait()
            b2[i, cut(h)] = (
                sb[y, i, cut(h)].astype(F32)
                + rb[0, i, cut(h)].astype(F32) + rb[1, i, cut(h)].astype(F32)
                + rb[2, i, cut(h)].astype(F32)
            ).astype(BF16)
            if i:
                stage_x2(i, h).start()

    def third(h):
        for k in range(1, NY):
            stage_y2(k, h).wait()
        for k in range(1, NX):
            stage_x2(k, h).wait()
        z3[cut(h), :RANK] = (
            a2[y, cut(h)].astype(F32) + ra2[0, cut(h)].astype(F32) + ra2[1, cut(h)].astype(F32)
            + ra2[2, cut(h)].astype(F32)
        ).astype(BF16)
        z3[cut(h), RANK:] = (
            b2[0, cut(h)].astype(F32) + rb2[0, cut(h)].astype(F32) + rb2[1, cut(h)].astype(F32)
            + rb2[2, cut(h)].astype(F32)
        ).astype(BF16)
        for k in range(NZ // 2):
            zt = h * (NZ // 2) + k

            @pl.when(zt != z)
            def _():
                z_copy(zt, zt).start()

            @pl.when(zt == z)
            def _():
                rz[z] = z3[zt * 16:zt * 16 + 16, :]

    def step(t, carry):
        send_all(s1.at[t], r1.at[t], s1s.at[t], s1r.at[t])
        r1[t, owner] = s1[t, owner]

        @pl.when(t > 0)
        def _():
            update_all()

        place(t)

        @pl.when(t < STEPS - 1)
        def _():
            prepare(t)

        cur = lax.rem(t, 2)
        sent_all(s1.at[t], r1.at[t], s1s.at[t], s1r.at[t]).wait_recv()
        fetched_t = nt(eye_e, take(r1, t).astype(BF16)).astype(BF16)

        def pool(i, carry):
            xx = nn(fetched_t, counts[cur, i]).astype(BF16)
            at = al(i * CH, CH)
            x0s[t, pl.ds(at, E), :] = xx[:, :TOK]
            x0s[t, pl.ds(al(at + E, E), E), :] = xx[:, TOK:]
            return carry

        def project(i, total):
            at = al(i * CH, CH)
            return total + nn(both_t[:, pl.ds(at, CH)], x0s[t, pl.ds(at, CH), :])

        lax.fori_loop(0, NCH, pool, 0, unroll=UNROLL)
        total = lax.fori_loop(0, NCH, project, jnp.zeros((2 * RANK, TOK), F32), unroll=UNROLL)
        low = total[:RANK].astype(BF16)
        v = total[RANK:]
        vb = v.astype(BF16)

        def forward(i, logit):
            at = al(i * CH, CH)
            gate = nn(up_t[pl.ds(at, CH), :], low) + bias_b[pl.ds(at, CH), :]
            x0f = x0s[t, pl.ds(at, CH), :].astype(F32)
            w = out_b[pl.ds(at, CH), :]
            us[pl.ds(at, CH), :] = w * (gate + 1.0) + nn(down[pl.ds(at, CH), :], vb)
            x1 = (x0f * gate + x0f).astype(BF16)
            x1s[t, pl.ds(at, CH), :] = x1
            return logit + jnp.sum((x1.astype(F32) * w).reshape(CH // 8, 8, TOK), axis=0)

        logit = lax.fori_loop(0, NCH, forward, jnp.zeros((8, TOK), F32), unroll=UNROLL)
        logit = jnp.sum(logit, axis=0, keepdims=True)
        dlogit = jax.nn.sigmoid(logit) - labels[pl.ds(t, 1), :].astype(F32)
        dhi = dlogit.astype(BF16).astype(F32)
        dmid = (dlogit - dhi).astype(BF16).astype(F32)
        dlo = dlogit - dhi - dmid
        sub = iota((16, TOK), 0)
        split = jnp.where(sub == 0, dhi, jnp.where(sub == 1, dmid, jnp.where(sub == 2, dlo, 0.0)))
        heads[t] = split.astype(BF16)
        dlows[t] = (dlogit * v).astype(BF16)
        glows[t] = (dlogit * low.astype(F32)).astype(BF16)
        dlow_copy(t).start()
        glow_copy(t).start()

        @pl.when(t == STEPS - 1)
        def _():
            windows(t)


        def spread(i, gf):
            at = al(i * CH, CH)
            dx0 = (dlogit * us[pl.ds(at, CH), :]).astype(BF16)
            both = jnp.concatenate([dx0[:E], dx0[E:]], axis=1)
            return gf + nt(counts[cur, i], both)

        put(g1, t, lax.fori_loop(0, NCH, spread, jnp.zeros((FETCH, E), F32), unroll=UNROLL))
        send_all(g1.at[t], g2.at[t], g1s.at[t], g1r.at[t])
        g2[t, owner] = g1[t, owner]

        @pl.when(t < STEPS - 1)
        def _():
            pair_up(t)
            count(t + 1)
            windows(t)

        @pl.when(t == STEPS - 1)
        def _():
            dense()
            sums()

        sent_all(g1.at[t], g2.at[t], g1s.at[t], g1r.at[t]).wait_recv()
        pair = halves(take(g2, t))
        back[...] = pair

        @pl.when(t < STEPS - 1)
        def _():
            rg = nn(same[...], pair)
            rg = rg[:, :E] + rg[:, E:]
            acc = acc_q[...] + jnp.mean(rg * rg, axis=1, keepdims=True)
            moved = nn(match[...], halves(learn_rate * rg * lax.rsqrt(acc)))
            put(s1, t + 1, base_q[...] - (moved[:, :E] + moved[:, E:]))

        return carry

    lax.fori_loop(0, STEPS, step, 0)
    second()
    update_all()

    store = pltpu.make_async_copy(table, table_hbm, lsem.at[0])
    store.start()

    def acc_rows(i, carry):
        at = al(i * E, E)
        accum_out[pl.ds(i, 1), :] = acc_b[pl.ds(at, E), :].T[0:1, :]
        return carry

    lax.fori_loop(0, ROWS // E, acc_rows, 0)

    first(1)
    for k in range(1, NY):
        bo_y(k).wait()
    bv[1] = bv[0] + bvy[0] + bvy[1] + bvy[2]
    for k in range(1, NZ):
        bo_z(k).start()
    third(0)
    third(1)

    scale = 1.0 / (STEPS * TOK * NX * NY * NZ * NC)
    for k in range(1, NZ):
        bo_z(k).wait()
    total = bv[1]
    for k in range(NZ - 1):
        total = total + bvz[k]
    bv[2] = total * scale
    start = (owner * NY + y) * SHARE - (x * XROWS // E) * E
    a = start // E
    rows = []
    for base in (0, 8):
        pair = jnp.concatenate([bv[2, pl.ds(base + a, 1), :], bv[2, pl.ds(lax.rem(base + a + 1, 16), 1), :]], axis=1)
        pair = jnp.broadcast_to(pair, (8, 2 * E))
        rows.append(pltpu.roll(pair, lax.rem(2 * E - lax.rem(start, E), 2 * E), 1)[:, 0:E])
    bo_out[...] = jnp.where(iota((8, E), 0) == 0, rows[0], rows[1])

    for k in range(NZ):
        @pl.when(k != z)
        def _():
            copy_to(z3.at[pl.ds(0, 16)], rz.at[k], zs.at[0], zr.at[k], partner).wait_recv()
            z_copy(k, k).wait_send()
    total = rz[0].astype(F32)
    for k in range(1, NZ):
        total = total + rz[k].astype(F32)
    own = owner * NY + y
    w = out_b[pl.ds(own * SHARE, 16), :]
    gdu_out[:, :RANK] = total[:, :RANK] * scale
    gdu_out[:, RANK:] = total[:, RANK:] * scale * jnp.concatenate([w, w], axis=1)

    for t in range(STEPS):
        for copy in factors(t):
            copy.wait_send()
    sent_all(rqs, rqr, qs.at[0], qr.at[0]).wait_send()
    for t in range(STEPS):
        sent_all(s1.at[t], r1.at[t], s1s.at[t], s1r.at[t]).wait_send()
        sent_all(g1.at[t], g2.at[t], g1s.at[t], g1r.at[t]).wait_send()
    store.wait()


def finish(table_in, accum_in, gdu, bo, table, accum, down, up, bias, outw, sem):
    rows = ROWS // 8
    copies = [
        pltpu.make_async_copy(table_in.at[pl.ds(n * rows, rows)], table.at[pl.ds(n * rows, rows)], sem.at[n])
        for n in range(8)
    ]
    for copy in copies:
        copy.start()
    accum[...] = accum_in[...]
    down[...] = gdu[0:SHARE, :RANK]
    up[...] = gdu[0:SHARE, RANK:]
    bias[...] = bo[0:1, 0:SHARE]
    outw[...] = bo[1:2, 0:SHARE]
    for copy in copies:
        copy.wait()


def local(table, accum, requests, members, labels, down_proj, up_proj, cross_bias, out_weight):
    reqs = jnp.transpose(requests[:, 0, 0], (0, 2, 1))
    mem = jnp.transpose(members, (0, 2, 3, 1)).reshape(STEPS, NB * BAGLEN, TOK)
    dma = pltpu.SemaphoreType.DMA
    vm = pltpu.VMEM
    scratch = [
        vm((ROWS, E), F32), vm((STEPS, NB * BAGLEN, TOK), jnp.int32),
        vm((D_IN, RANK), BF16), vm((RANK, D_IN), BF16),
        vm((OWNERS, 1, E), F32), vm((OWNERS, 1, E), F32),
        vm((FETCH, E), F32), vm((FETCH, E), F32),
        vm((FETCH, FETCH), BF16), vm((FETCH, FETCH), BF16), vm((FETCH, 2 * E), BF16),
        vm((STEPS, FETCH, E), jnp.int32), vm((STEPS, 8, FETCH), jnp.int32),
        vm((STEPS + 1, OWNERS, SLOTS, E), F32),
    ]
    scratch += [vm((STEPS, OWNERS, SLOTS, E), F32)] * 3
    scratch += [
        vm((NROW, FETCH, CH), BF16), vm((NROW, CH, FETCH), BF16),
        vm((E, E), F32), vm((NB, E), F32), vm((2 * RANK, D_IN), BF16), vm((D_IN, RANK), BF16),
        vm((D_IN, TOK), F32), vm((D_IN + 16, TOK), F32), vm((ROWS, E), F32), vm((FETCH, E), jnp.int32),
        vm((2, NCH, FETCH, 2 * TOK), BF16),
        vm((STEPS, D_IN, TOK), BF16),
        vm((STEPS, RANK, TOK), BF16), vm((STEPS, RANK, TOK), BF16),
        vm((D_IN, TOK), F32), vm((STEPS, D_IN, TOK), BF16), vm((STEPS, 16, TOK), BF16),
        vm((STEPS, 2, CORE_ROWS, TOK), BF16), vm((STEPS, CORE_ROWS, TOK), BF16),
        vm((STEPS, RANK, TOK), BF16), vm((STEPS, RANK, TOK), BF16),
        vm((NX, NY, NZ * 16, RANK), BF16), vm((NX - 1, NY, NZ * 16, RANK), BF16),
        vm((NY, NX, NZ * 16, RANK), BF16), vm((NY - 1, NX, NZ * 16, RANK), BF16),
        vm((NY, NZ * 16, RANK), BF16), vm((NY - 1, NZ * 16, RANK), BF16),
        vm((NX, NZ * 16, RANK), BF16), vm((NX - 1, NZ * 16, RANK), BF16),
        vm((NZ * 16, 2 * RANK), BF16), vm((NZ, 16, 2 * RANK), BF16),
        vm((2, 64, E), F32), vm((64, E), F32),
        vm((NX, 16, E), F32), vm((NX - 1, 16, E), F32), vm((3, 16, E), F32),
        vm((NY - 1, 16, E), F32), vm((NZ - 1, 16, E), F32),
    ]
    scratch += [dma((4,)), dma((1,)), dma((1,))]
    scratch += [dma((STEPS,))] * 4
    scratch += [dma((STEPS, 4))] * 2
    scratch += [dma((NX, 2))] * 2
    scratch += [dma((NX, NY, 2))] * 2
    scratch += [dma((NX, 2))] * 4
    scratch += [dma((NZ,))] * 2
    scratch += [dma] * 2
    scratch += [dma((8,))] * 6
    hbm = pl.BlockSpec(memory_space=pl.ANY)
    spec = pl.BlockSpec(memory_space=pltpu.VMEM)
    table_new, accum_new, gdu, bo = pl.pallas_call(
        kernel,
        out_shape=(
            jax.ShapeDtypeStruct((ROWS, E), F32),
            jax.ShapeDtypeStruct((ROWS // E, E), F32),
            jax.ShapeDtypeStruct((16, 2 * RANK), F32),
            jax.ShapeDtypeStruct((8, E), F32),
        ),
        in_specs=[hbm, spec, spec, hbm, spec, hbm, hbm, spec, spec],
        out_specs=(hbm, spec, spec, spec),
        scratch_shapes=scratch,
        compiler_params=pltpu.CompilerParams(
            collective_id=0, has_side_effects=True, vmem_limit_bytes=58 * 1024 * 1024
        ),
    )(
        table, accum.reshape(ROWS // E, E), reqs, mem, labels, down_proj, up_proj,
        cross_bias.reshape(NB, E), out_weight.reshape(NB, E),
    )
    table_out, accum_out, down, up, bias, outw = pl.pallas_call(
        finish,
        out_shape=(
            jax.ShapeDtypeStruct((ROWS, E), F32),
            jax.ShapeDtypeStruct((ROWS // E, E), F32),
            jax.ShapeDtypeStruct((SHARE, RANK), F32),
            jax.ShapeDtypeStruct((SHARE, RANK), F32),
            jax.ShapeDtypeStruct((1, SHARE), F32),
            jax.ShapeDtypeStruct((1, SHARE), F32),
        ),
        in_specs=[hbm, spec, spec, spec],
        out_specs=(spec, spec, spec, spec, spec, spec),
        scratch_shapes=[dma((8,))],
    )(table_new, accum_new, gdu, bo)
    return (table_out, accum_out.reshape(ROWS), down, up.T, bias[0], outw[0])


def solution(mesh):
    both = ("owner", "group")
    in_specs = (
        P(both, None), P(both), P(None, "owner", "group", None, None),
        P(None, both, None, None), P(None, both), P(), P(), P(), P(),
    )
    out_specs = (P(both, None), P(both), P(both, None), P(None, both), P(both), P(both))
    return jax.shard_map(local, mesh=mesh, in_specs=in_specs, out_specs=out_specs, check_vma=False)
```
